512 devices in a mesh: tm: 32 (over y, x), gy: 16 (over z, core).
Axes of the slice: x: 4, y: 8, z: 8, core: 2. Of those that a mesh axis runs over, the one named last changes fastest.
Arguments:
- initial_state: float32 [3, 256, 1024], P(None, 'gy'), may hold values from -4 to 4
- guessed_ends: float32 [32, 3, 256, 1024], P('tm', None, 'gy'), may hold values from -4 to 4
- velocity: float32 [32, 2, 256, 1024], P('tm', None, 'gy'), may hold values from -1 to 1
Outputs:
- corrected: float32 [32, 3, 256, 1024], P('tm', None, 'gy')
- relaxed: float32 [32, 3, 256, 1024], P('tm', None, 'gy')
The draws below stay inside these ranges and needn't reach their ends.
All inputs are finite; a program needn't handle non-finite values.
Results may differ from the reference program's by a relative error of at most 0.00002.
Values sent between devices are 32-bit elements; how exact they have to be, the bound alone decides.
No kernel may reach another device: no remote copies, remote signals or barrier semaphores. Data moves between devices by JAX's collectives and lax.ppermute only.
A program may use at most 64 MiB of HBM per device.

```python
import jax
import jax.numpy as jnp

NX = 1024
FINE = 4
GROUP = 4
NY = 256
INTERVALS = 32
N_TM = 32


def shard_levels(key, dims, shards, smallest, top_value):
    loudness, own = 1.0, jax.random.fold_in(key, 6)
    for position, shards_of in shards:
        heights = jnp.exp(jax.random.uniform(jax.random.fold_in(own, position), (shards_of,), jnp.float32, smallest / len(shards), top_value / len(shards)))
        loudness = loudness * jnp.repeat(heights, dims[position] // shards_of).reshape([-1 if axis == position else 1 for axis in range(len(dims))])
    return loudness


def normal_values(own_key, dims, scale, bound, split=(), held_as=jnp.bfloat16):
    loudness = shard_levels(own_key, dims, split, -0.22, 0.18) if split else 1.0
    entries = jax.random.normal(own_key, dims, jnp.float32) * scale * loudness
    return jnp.minimum(jnp.maximum(entries, -bound), bound).astype(held_as)


def setup_inputs(seed: int = 0) -> dict:
    keys = jax.random.split(jax.random.key(seed), 4)
    initial_state = normal_values(keys[0], (3, NY, NX), 1.0, 4.0, ((1, 16),), jnp.float32)
    guessed_ends = normal_values(keys[1], (INTERVALS, 3, NY, NX), 1.0, 4.0, ((0, 32), (2, 16)), jnp.float32)
    velocity = jnp.clip(jax.random.uniform(keys[2], (INTERVALS, 2, NY, NX), jnp.float32, -1.0, 1.0) * shard_levels(keys[2], (INTERVALS, 2, NY, NX), ((0, 32), (2, 16)), -0.4, 0.0), -1.0, 1.0)
    return {"initial_state": initial_state, "guessed_ends": guessed_ends, "velocity": velocity}


diffusion = (0.05, 0.15, 0.4)
kappa_coupling = 0.1
time_step = 0.0125


def advance(extended, velocity, factor):
    center = extended[:, 1:-1]
    northern = extended[:, 2:]
    southern = extended[:, :-2]
    eastern = jnp.roll(center, -1, axis=2)
    western = jnp.roll(center, 1, axis=2)
    speed_across = velocity[0] + kappa_coupling * center[0]
    speed_along = velocity[1] + kappa_coupling * center[1]
    transport = jnp.maximum(speed_across, 0.0) * (center - western) + jnp.minimum(speed_across, 0.0) * (eastern - center)
    transport = transport + jnp.maximum(speed_along, 0.0) * (center - southern) + jnp.minimum(speed_along, 0.0) * (northern - center)
    spread = northern + southern + eastern + western - 4.0 * center
    viscous = jnp.array(diffusion, jnp.float32)[:, None, None]
    return center + factor * (viscous * spread - transport)


def one_step(state, velocity, factor):
    extended = jnp.pad(state, ((0, 0), (1, 1), (0, 0)))
    return advance(extended, velocity, factor)


def interval(state, velocity):
    for section in range(FINE):
        state = one_step(state, velocity, time_step)
    return state


def reference(initial_state, guessed_ends, velocity):
    level_one = FINE * time_step
    coarsest = FINE * GROUP * time_step
    stepper = jax.vmap(one_step, in_axes=(0, 0, None))
    begins = jnp.concatenate([initial_state[None], guessed_ends[:-1]], axis=0)
    fine_ends = jax.vmap(interval)(begins, velocity)
    coarse_begin = stepper(begins, velocity, level_one)
    sources = fine_ends - coarse_begin
    current = coarse_begin[0::GROUP] + sources[0::GROUP]
    for k in range(1, GROUP):
        current = stepper(current, velocity[k::GROUP], level_one) + sources[k::GROUP]
    forcing = current - stepper(begins[0::GROUP], velocity[GROUP - 1::GROUP], coarsest)
    chain = []
    state = initial_state
    for j in range(N_TM // GROUP):
        state = one_step(state, velocity[GROUP * j + GROUP - 1], coarsest) + forcing[j]
        chain.append(state)
    settled = jnp.stack(chain)
    current = jnp.concatenate([initial_state[None], settled[:-1]], axis=0)
    columns = []
    for k in range(GROUP - 1):
        current = stepper(current, velocity[k::GROUP], level_one) + sources[k::GROUP]
        columns.append(current)
    columns.append(settled)
    corrected = jnp.stack(columns, axis=1).reshape(guessed_ends.shape)
    final_begins = jnp.concatenate([initial_state[None], corrected[:-1]], axis=0)
    relaxed = jax.vmap(interval)(final_begins, velocity)
    return corrected, relaxed
```

```python
import functools

import jax
import jax.numpy as jnp
from jax import lax
from jax.experimental import pallas as pl
from jax.experimental.pallas import tpu as pltpu
from jax.sharding import PartitionSpec as P

FINE = 4
GROUP = 4
GROUPS = 8
HALO = 16
TILE = 32
ROWS = 16
HALF = 64
BAND = 24

diffusion = (0.05, 0.15, 0.4)
kappa_coupling = 0.1
time_step = 0.0125
level_one = FINE * time_step
coarsest = FINE * GROUP * time_step

VMEM = pl.BlockSpec(memory_space=pltpu.VMEM)
SMEM = pl.BlockSpec(memory_space=pltpu.SMEM)


def lanes():
    return lax.broadcasted_iota(jnp.int32, (8, 128), 1)


def sublanes():
    return lax.broadcasted_iota(jnp.int32, (8, 128), 0)


def update(u, north, south, east, west, v0, v1, h):
    across = h * v0 + (h * kappa_coupling) * u[0]
    along = h * v1 + (h * kappa_coupling) * u[1]
    a, b = jnp.maximum(across, 0.0), jnp.minimum(across, 0.0)
    e, d = jnp.maximum(along, 0.0), jnp.minimum(along, 0.0)
    new = []
    for c in range(3):
        k = h * diffusion[c]
        x = (k - b) * (east[c] - u[c]) - (k + a) * (u[c] - west[c])
        y = (k - d) * (north[c] - u[c]) - (k + e) * (u[c] - south[c])
        new.append(u[c] + (x + y))
    return new


def cut_kernel(meta, init, ends, vel, out):
    last = meta[0] == GROUP * GROUPS - 1
    low = lanes() < HALF
    for a in range(5):
        if a < 3:
            top = jnp.where(last, init[a, 0:8, :], ends[a, 0:8, :])
            bottom = jnp.where(last, init[a, 8:16, :], ends[a, 8:16, :])
        else:
            top, bottom = vel[a - 3, 0:8, :], vel[a - 3, 8:16, :]
        for q in range(4):
            upper = pltpu.roll(top, (HALO - TILE * q) % 1024, 1)
            lower = pltpu.roll(bottom, (HALO + HALF - TILE * q) % 1024, 1)
            for b in range(8):
                at = slice(128 * b, 128 * b + 128)
                out[(4 * b + q) * 5 + a] = jnp.where(low, upper[:, at], lower[:, at])


def cycle_kernel(meta, prv, cur, nxt, out, ua, ub, vv, src, gg, ff, init, xa, xb, yy, cc):
    lane, sub = lanes(), sublanes()
    low = lane < HALF
    at_bottom = jnp.logical_and(low, meta[0] == 0)
    at_top = jnp.logical_and(jnp.logical_not(low), meta[0] == meta[1] - 1)

    def finish(buf, base):
        for c in range(3):
            buf[base + c, HALO] = jnp.where(at_bottom, 0.0, buf[base + c, HALO])
            buf[base + c, 9] = jnp.where(at_top, 0.0, buf[base + c, 9])
            buf[base + c, 0] = pltpu.roll(buf[base + c, BAND], HALF, 1)
            buf[base + c, BAND + 1] = pltpu.roll(buf[base + c, 1], HALF, 1)

    def step(buf, base, k, h, emit):
        def row(r, carry):
            u = [buf[base + c, r + 1] for c in range(3)]
            north = [buf[base + c, r + 2] for c in range(3)]
            south = [buf[base + c, r] for c in range(3)]
            east = [pltpu.roll(x, 127, 1) for x in u]
            west = [pltpu.roll(x, 1, 1) for x in u]
            emit(r, update(u, north, south, east, west, vv[2 * k, r], vv[2 * k + 1, r], h))
            return carry

        lax.fori_loop(0, BAND, row, 0, unroll=8)

    for k in range(GROUP):
        for a in range(5):
            for y in range(8):
                at = pl.ds(k * 40 + a * 8 + y, 8, stride=160)
                p, m, n = prv[at, :], cur[at, :], nxt[at, :]
                rows = (
                    (y, jnp.where(low, p, m)),
                    (y + 8, pltpu.roll(jnp.where(low, n, p), HALF, 1)),
                    (y + 16, jnp.where(low, m, n)),
                )
                for r, value in rows:
                    if a >= 3:
                        vv[2 * k + a - 3, r] = value
                    elif k == GROUP - 1:
                        value = pltpu.roll(value, 1, 0)
                        ua[a, r + 1] = value
                        init[a, r + 1] = value
                        xa[a, r + 1] = value
                    else:
                        ua[3 * (k + 1) + a, r + 1] = value

    finish(xa, 0)

    def first(k, carry):
        finish(ua, 3 * k)

        def coarse(r, new):
            for c in range(3):
                src[3 * k + c, r] = new[c]

        step(ua, 3 * k, k, level_one, coarse)
        return carry

    lax.fori_loop(0, GROUP, first, 0)

    def keep_g(r, new):
        for c in range(3):
            gg[c, r] = new[c]

    step(ua, 0, GROUP - 1, coarsest, keep_g)

    def into(buf, base):
        def emit(r, new):
            for c in range(3):
                buf[base + c, r + 1] = new[c]

        return emit

    def fine(k, carry):
        base = 3 * k

        def last(r, new):
            for c in range(3):
                ua[base + c, r + 1] = new[c]
                src[base + c, r] = new[c] - src[base + c, r]

        step(ua, base, k, time_step, into(ub, base))
        finish(ub, base)
        step(ub, base, k, time_step, into(ua, base))
        finish(ua, base)
        step(ua, base, k, time_step, into(ub, base))
        finish(ub, base)
        step(ub, base, k, time_step, last)
        finish(ua, base)
        return carry

    lax.fori_loop(0, GROUP, fine, 0)

    def plus(buf, k, base):
        def emit(r, new):
            for c in range(3):
                buf[base + c, r + 1] = new[c] + src[3 * k + c, r]

        return emit

    step(ua, 0, 1, level_one, plus(ub, 1, 0))
    finish(ub, 0)
    step(ub, 0, 2, level_one, plus(ua, 2, 0))
    finish(ua, 0)

    def forcing(r, new):
        for c in range(3):
            ff[c, r] = new[c] + src[3 * (GROUP - 1) + c, r] - gg[c, r]

    step(ua, 0, GROUP - 1, level_one, forcing)

    def settle(buf, to):
        def emit(r, new):
            for c in range(3):
                y = new[c] + ff[c, r]
                yy[c, r] = y
                to[c, r + 1] = jnp.where(sub == 0, init[c, r + 1], pltpu.roll(y, 1, 0))

        step(buf, 0, GROUP - 1, coarsest, emit)
        finish(to, 0)

    def two(i, carry):
        settle(xa, xb)
        settle(xb, xa)
        return carry

    lax.fori_loop(0, GROUPS // 2, two, 0)

    step(xa, 0, 0, level_one, plus(cc, 0, 0))
    finish(cc, 0)
    step(cc, 0, 1, level_one, plus(cc, 1, 3))
    finish(cc, 3)
    step(cc, 3, 2, level_one, plus(cc, 2, 6))

    def compact(read, c, y):
        m = jnp.where(low, read(c, y + 16), read(c, y))
        return jnp.where(lane < TILE, pltpu.roll(m, 128 - HALO, 1), pltpu.roll(m, 128 - HALO - TILE, 1))

    reads = [
        lambda c, r: xa[c, r + 1],
        lambda c, r: cc[c, r + 1],
        lambda c, r: cc[3 + c, r + 1],
        lambda c, r: cc[6 + c, r + 1],
        lambda c, r: yy[c, r],
    ]
    for c in range(3):
        for y in range(8):
            before = compact(reads[0], c, y)
            for k in range(GROUP):
                own = compact(reads[k + 1], c, y)
                value = jnp.where(low, own, pltpu.roll(before, HALF, 1))
                out[pl.ds(k * 24 + c * 8 + y, 8, stride=96), :] = value
                before = own


def join_kernel(tiles, vel, own, begin, up, down):
    lane = lanes()
    group = lane // TILE

    def rows_out(a, y0, b, value):
        begin[pl.ds((a * ROWS + y0) * 8 + b, 8, stride=8), :] = value
        if y0 == 0:
            down[pl.ds(a * FINE * 8 + b, FINE, stride=8), :] = value[0:FINE]
        else:
            up[pl.ds(a * FINE * 8 + b, FINE, stride=8), :] = value[8 - FINE : 8]

    for c in range(3):
        for b in range(8):
            t = [tiles[(4 * b + q) * 3 + c] for q in range(4)]
            for part in range(4):
                value = None
                for q in range(4):
                    shift = (TILE * (q - part)) % 128
                    x = pltpu.roll(t[q], shift, 1) if shift else t[q]
                    value = x if value is None else jnp.where(group == q, x, value)
                y0 = 8 * (part % 2)
                if part < 2:
                    own[c, y0 : y0 + 8, 128 * b : 128 * b + 128] = value
                else:
                    rows_out(c, y0, b, value)
    for c in range(2):
        for b in range(8):
            for y0 in (0, 8):
                rows_out(3 + c, y0, b, vel[c, y0 : y0 + 8, 128 * b : 128 * b + 128])


def relax_kernel(meta, mid, below, above, out, wa, wb, vv, flat):
    lane = lanes()
    tall = ROWS + 2 * FINE
    for a in range(5):
        buf, at = (wa, a * tall) if a < 3 else (vv, (a - 3) * tall)
        for r in range(FINE):
            buf[at + r] = below[a * FINE + r]
            buf[at + FINE + ROWS + r] = above[a * FINE + r]
        for r in range(ROWS):
            buf[at + FINE + r] = mid[a * ROWS + r]

    bottom, top = meta[0] == 0, meta[0] == meta[1] - 1
    buf, to = wa, wb
    for section in range(FINE):
        for r in range(section + 1, tall - section - 1):
            u = [buf[c * tall + r] for c in range(3)]
            north = [buf[c * tall + r + 1] for c in range(3)]
            south = [buf[c * tall + r - 1] for c in range(3)]
            east, west = [], []
            for x in u:
                x1 = pltpu.roll(x, 127, 1)
                east.append(jnp.where(lane == 127, pltpu.roll(x1, 7, 0), x1))
                x2 = pltpu.roll(x, 1, 1)
                west.append(jnp.where(lane == 0, pltpu.roll(x2, 1, 0), x2))
            new = update(u, north, south, east, west, vv[r], vv[tall + r], time_step)
            for c in range(3):
                if section == FINE - 1:
                    flat[(c * ROWS + r - FINE) * 8 : (c * ROWS + r - FINE) * 8 + 8, :] = new[c]
                elif r == FINE - 1:
                    to[c * tall + r] = jnp.where(bottom, 0.0, new[c])
                elif r == FINE + ROWS:
                    to[c * tall + r] = jnp.where(top, 0.0, new[c])
                else:
                    to[c * tall + r] = new[c]
        buf, to = to, buf
    for c in range(3):
        for b in range(8):
            for y0 in (0, 8):
                out[c, y0 : y0 + 8, 128 * b : 128 * b + 128] = flat[pl.ds((c * ROWS + y0) * 8 + b, 8, stride=8), :]


def f32(*shape):
    return jax.ShapeDtypeStruct(shape, jnp.float32)


def buffer(*shape):
    return pltpu.VMEM(shape, jnp.float32)


def call(kernel, n_scalars, n_arrays, outs, scratch=()):
    many = isinstance(outs, tuple)
    return pl.pallas_call(
        kernel,
        out_shape=outs,
        in_specs=[SMEM] * n_scalars + [VMEM] * n_arrays,
        out_specs=(VMEM,) * len(outs) if many else VMEM,
        scratch_shapes=list(scratch),
        compiler_params=pltpu.CompilerParams(vmem_limit_bytes=24 * 1024 * 1024),
    )


def cut(meta, init, ends, vel):
    return call(cut_kernel, 1, 3, f32(160, 8, 128))(meta, init, ends, vel)


def cycle(meta, prv, cur, nxt):
    tall = BAND + 2
    scratch = [
        buffer(12, tall, 8, 128),
        buffer(12, tall, 8, 128),
        buffer(8, BAND, 8, 128),
        buffer(12, BAND, 8, 128),
        buffer(3, BAND, 8, 128),
        buffer(3, BAND, 8, 128),
        buffer(3, tall, 8, 128),
        buffer(3, tall, 8, 128),
        buffer(3, tall, 8, 128),
        buffer(3, BAND, 8, 128),
        buffer(9, tall, 8, 128),
    ]
    return call(cycle_kernel, 1, 3, f32(768, 128), scratch)(meta, prv, cur, nxt)


def join(tiles, vel):
    halo = 5 * FINE * 8
    outs = (f32(3, ROWS, 1024), f32(5 * ROWS * 8, 128), f32(halo, 128), f32(halo, 128))
    return call(join_kernel, 0, 2, outs)(tiles, vel)


def relax(meta, mid, below, above):
    tall = ROWS + 2 * FINE
    scratch = [
        buffer(3 * tall, 8, 128),
        buffer(3 * tall, 8, 128),
        buffer(2 * tall, 8, 128),
        buffer(3 * ROWS * 8, 128),
    ]
    return call(relax_kernel, 1, 3, f32(3, ROWS, 1024), scratch)(meta, mid, below, above)


def per_device(initial_state, guessed_ends, velocity):
    slabs = lax.axis_size("gy")
    forward = [(i, i + 1) for i in range(slabs - 1)]
    backward = [(i + 1, i) for i in range(slabs - 1)]
    intervals = lax.axis_size("tm")
    here = lax.axis_index("tm").astype(jnp.int32).reshape(1)
    slab = jnp.stack([lax.axis_index("gy").astype(jnp.int32), jnp.int32(slabs)])
    flow = velocity[0]

    windows = cut(here, initial_state, guessed_ends[0], flow)
    cur = lax.all_to_all(windows.reshape(intervals, 40, 128), "tm", 0, 0)
    cur = cur.reshape(intervals * 40, 128)
    prv = lax.ppermute(cur, "gy", forward)
    nxt = lax.ppermute(cur, "gy", backward)
    tiles = cycle(slab, prv, cur, nxt)
    tiles = lax.all_to_all(tiles.reshape(intervals, 24, 128), "tm", 0, 0)
    own, mid, up, down = join(tiles.reshape(intervals * 3, 8, 128), flow)
    below = lax.ppermute(up, "gy", forward)
    above = lax.ppermute(down, "gy", backward)
    relaxed = relax(
        slab,
        mid.reshape(5 * ROWS, 8, 128),
        below.reshape(5 * FINE, 8, 128),
        above.reshape(5 * FINE, 8, 128),
    )
    return own[None], relaxed[None]


def solution(mesh):
    placed = (P(None, "gy", None), P("tm", None, "gy", None), P("tm", None, "gy", None))
    return jax.shard_map(
        per_device,
        mesh=mesh,
        in_specs=placed,
        out_specs=(P("tm", None, "gy", None), P("tm", None, "gy", None)),
        check_vma=False,
    )
```

```python
import jax
import jax.numpy as jnp
from jax import lax
from jax.experimental import pallas as pl
from jax.experimental.pallas import tpu as pltpu
from jax.sharding import PartitionSpec as P

FINE = 4
GROUP = 4
GROUPS = 8
HALO = 16
TILE = 32
ROWS = 16
HALF = 64
BAND = 24

diffusion = (0.05, 0.15, 0.4)
kappa_coupling = 0.1
time_step = 0.0125
level_one = FINE * time_step
coarsest = FINE * GROUP * time_step

VMEM = pl.BlockSpec(memory_space=pltpu.VMEM)
HBM = pl.BlockSpec(memory_space=pltpu.HBM)
SMEM = pl.BlockSpec(memory_space=pltpu.SMEM)


def lanes():
    return lax.broadcasted_iota(jnp.int32, (8, 128), 1)


def sublanes():
    return lax.broadcasted_iota(jnp.int32, (8, 128), 0)


def slope(u, plus, minus, east, west, across, along):
    a, b = jnp.maximum(across, 0.0), jnp.minimum(across, 0.0)
    e, d = jnp.maximum(along, 0.0), jnp.minimum(along, 0.0)
    out = []
    for c in range(3):
        k = diffusion[c]
        x = (k - b) * (east[c] - u[c]) - (k + a) * (u[c] - west[c])
        y = (k - d) * (plus[c] - u[c]) - (k + e) * (u[c] - minus[c])
        out.append(x + y)
    return out


def cut_kernel(meta, init_hbm, ends_hbm, vel_hbm, out, init, ends, vel, sems):
    copies = [
        pltpu.make_async_copy(far, near, sems.at[i])
        for i, (far, near) in enumerate(((init_hbm, init), (ends_hbm, ends), (vel_hbm, vel)))
    ]
    for copy in copies:
        copy.start()
    for copy in copies:
        copy.wait()
    last = meta[0] == GROUP * GROUPS - 1
    low = lanes() < HALF
    for a in range(5):
        if a < 3:
            top = jnp.where(last, init[a, 0:8, :], ends[a, 0:8, :])
            bottom = jnp.where(last, init[a, 8:16, :], ends[a, 8:16, :])
        else:
            top, bottom = vel[a - 3, 0:8, :], vel[a - 3, 8:16, :]
        for q in range(4):
            upper = pltpu.roll(top, (HALO - TILE * q) % 1024, 1)
            lower = pltpu.roll(bottom, (HALO + HALF - TILE * q) % 1024, 1)
            for b in range(8):
                at = slice(128 * b, 128 * b + 128)
                out[(4 * b + q) * 5 + a] = jnp.where(low, upper[:, at], lower[:, at])


def cycle_kernel(meta, mate, cur, other, out, ua, ub, vv, src, gg, ff, init, xa, xb, yy, cc):
    lane, sub = lanes(), sublanes()
    low = lane < HALF
    sign = jnp.where(low, 1.0, -1.0)
    swing = kappa_coupling * sign
    even = meta[0] % 2 == 0
    first = lane // HALF == meta[0] % 2
    outside = jnp.where(low, meta[0], meta[1] - 1 - meta[0]) == 0

    def step(buf, base, k, start, emit):
        rows = {}

        def row(r):
            if r not in rows:
                rows[r] = [buf[base + c, r] for c in range(3)]
            return rows[r]

        for r in range(start, BAND):
            u = row(r)
            east = [pltpu.roll(x, 127, 1) for x in u]
            west = [pltpu.roll(x, 1, 1) for x in u]
            across = vv[2 * k, r] + kappa_coupling * u[0]
            along = vv[2 * k + 1, r] + swing * u[1]
            emit(r, u, slope(u, row(r + 1), row(r - 1), east, west, across, along))

    def put(buf, at, r, value):
        if r == HALO - 1:
            value = jnp.where(outside, 0.0, value)
        buf[at, r] = value
        if r == BAND - 1:
            buf[at, BAND] = pltpu.roll(value, HALF, 1)

    for k in range(GROUP):
        for a in range(5):
            at = k * 40 + a * 8
            own = [cur[pl.ds(at + y, 8, stride=160), :] for y in range(8)]
            for y in range(8):
                up, down = jnp.where(even, y, 7 - y), jnp.where(even, 7 - y, y)
                o = other[pl.ds(at + up, 8, stride=160), :]
                m = mate[pl.ds(at + down, 8, stride=160), :]
                rows = (
                    (y, jnp.where(first, o, m)),
                    (y + 8, pltpu.roll(jnp.where(first, m, o), HALF, 1)),
                    (y + 16, jnp.where(low, own[y], own[7 - y])),
                )
                for r, value in rows:
                    if a == 3:
                        vv[2 * k, r] = value
                    elif a == 4:
                        vv[2 * k + 1, r] = sign * value
                    elif k == GROUP - 1:
                        value = pltpu.roll(value, 1, 0)
                        put(ua, a, r, value)
                        put(xa, a, r, value)
                        xb[a, r] = value
                        init[a, r] = value
                    else:
                        put(ua, 3 * (k + 1) + a, r, value)

    def keep_g(r, u, s):
        for c in range(3):
            gg[c, r] = u[c] + coarsest * s[c]

    step(ua, 0, GROUP - 1, 7, keep_g)

    def fine(k, carry):
        base = 3 * k

        def opening(r, u, s):
            for c in range(3):
                put(ub, base + c, r, u[c] + time_step * s[c])
                src[base + c, r] = u[c] + level_one * s[c]

        def onward(buf):
            def emit(r, u, s):
                for c in range(3):
                    put(buf, base + c, r, u[c] + time_step * s[c])

            return emit

        def closing(r, u, s):
            for c in range(3):
                end = u[c] + time_step * s[c]
                put(ua, base + c, r, end)
                src[base + c, r] = end - src[base + c, r]

        step(ua, base, k, 1, opening)
        step(ub, base, k, 2, onward(ua))
        step(ua, base, k, 3, onward(ub))
        step(ub, base, k, 4, closing)
        return carry

    lax.fori_loop(0, GROUP, fine, 0)

    def plus(buf, k, base):
        def emit(r, u, s):
            for c in range(3):
                put(buf, base + c, r, u[c] + level_one * s[c] + src[3 * k + c, r])

        return emit

    step(ua, 0, 1, 5, plus(ub, 1, 0))
    step(ub, 0, 2, 6, plus(ua, 2, 0))

    def forcing(r, u, s):
        for c in range(3):
            ff[c, r] = u[c] + level_one * s[c] + src[3 * (GROUP - 1) + c, r] - gg[c, r]

    step(ua, 0, GROUP - 1, 7, forcing)

    for t in range(GROUPS):
        buf, to = (xa, xb) if t % 2 == 0 else (xb, xa)

        def settle(r, u, s):
            for c in range(3):
                y = u[c] + coarsest * s[c] + ff[c, r]
                if t == GROUPS - 1 and r >= HALO:
                    yy[c, r] = y
                put(to, c, r, jnp.where(sub == 0, init[c, r], pltpu.roll(y, 1, 0)))

        step(buf, 0, GROUP - 1, max(7, 6 + t), settle)

    step(xa, 0, 0, 14, plus(cc, 0, 0))
    step(cc, 0, 1, 15, plus(cc, 1, 3))
    step(cc, 3, 2, 16, plus(cc, 2, 6))

    def compact(buf, base, c, y):
        m = jnp.where(low, buf[base + c, y + 16], buf[base + c, 23 - y])
        return jnp.where(lane < TILE, pltpu.roll(m, 128 - HALO, 1), pltpu.roll(m, 128 - HALO - TILE, 1))

    reads = [(xa, 0), (cc, 0), (cc, 3), (cc, 6), (yy, 0)]
    for c in range(3):
        for y in range(8):
            before = compact(*reads[0], c, y)
            for k in range(GROUP):
                own = compact(*reads[k + 1], c, y)
                value = jnp.where(low, own, pltpu.roll(before, HALF, 1))
                out[pl.ds(k * 24 + c * 8 + y, 8, stride=96), :] = value
                before = own


def join_kernel(meta, tiles, vel, own, begin, mate, other):
    group = lanes() // TILE
    even = meta[0] % 2 == 0

    def rows_out(a, b, top, bottom):
        begin[pl.ds(a * ROWS * 8 + b, 8, stride=8), :] = top
        begin[pl.ds((a * ROWS + 8) * 8 + b, 8, stride=8), :] = bottom
        down, up = top[0:FINE], bottom[8 - FINE : 8]
        at = pl.ds(a * FINE * 8 + b, FINE, stride=8)
        mate[at, :] = jnp.where(even, up, down)
        other[at, :] = jnp.where(even, down, up)

    for c in range(3):
        for b in range(8):
            t = [tiles[(4 * b + q) * 3 + c] for q in range(4)]
            parts = []
            for part in range(4):
                value = None
                for q in range(4):
                    shift = (TILE * (q - part)) % 128
                    x = pltpu.roll(t[q], shift, 1) if shift else t[q]
                    value = x if value is None else jnp.where(group == q, x, value)
                parts.append(value)
            at = slice(128 * b, 128 * b + 128)
            own[c, 0:8, at], own[c, 8:16, at] = parts[0], parts[1]
            rows_out(c, b, parts[2], parts[3])
    for c in range(2):
        for b in range(8):
            at = slice(128 * b, 128 * b + 128)
            rows_out(3 + c, b, vel[c, 0:8, at], vel[c, 8:16, at])


def relax_kernel(meta, mid, mate, other, out, wa, wb, vv, flat):
    lane = lanes()
    tall = ROWS + 2 * FINE
    even = meta[0] % 2 == 0
    for a in range(5):
        buf, at = (wa, a * tall) if a < 3 else (vv, (a - 3) * tall)
        for r in range(FINE):
            m, o = mate[a * FINE + r], other[a * FINE + r]
            buf[at + r] = jnp.where(even, o, m)
            buf[at + FINE + ROWS + r] = jnp.where(even, m, o)
        for r in range(ROWS):
            buf[at + FINE + r] = mid[a * ROWS + r]

    bottom, top = meta[0] == 0, meta[0] == meta[1] - 1
    buf, to = wa, wb
    for section in range(FINE):
        for r in range(section + 1, tall - section - 1):
            u = [buf[c * tall + r] for c in range(3)]
            north = [buf[c * tall + r + 1] for c in range(3)]
            south = [buf[c * tall + r - 1] for c in range(3)]
            east, west = [], []
            for x in u:
                x1 = pltpu.roll(x, 127, 1)
                east.append(jnp.where(lane == 127, pltpu.roll(x1, 7, 0), x1))
                x2 = pltpu.roll(x, 1, 1)
                west.append(jnp.where(lane == 0, pltpu.roll(x2, 1, 0), x2))
            across = vv[r] + kappa_coupling * u[0]
            along = vv[tall + r] + kappa_coupling * u[1]
            s = slope(u, north, south, east, west, across, along)
            for c in range(3):
                new = u[c] + time_step * s[c]
                if section == FINE - 1:
                    flat[(c * ROWS + r - FINE) * 8 : (c * ROWS + r - FINE) * 8 + 8, :] = new
                elif r == FINE - 1:
                    to[c * tall + r] = jnp.where(bottom, 0.0, new)
                elif r == FINE + ROWS:
                    to[c * tall + r] = jnp.where(top, 0.0, new)
                else:
                    to[c * tall + r] = new
        buf, to = to, buf
    for c in range(3):
        for b in range(8):
            for y0 in (0, 8):
                out[c, y0 : y0 + 8, 128 * b : 128 * b + 128] = flat[pl.ds((c * ROWS + y0) * 8 + b, 8, stride=8), :]


def f32(*shape):
    return jax.ShapeDtypeStruct(shape, jnp.float32)


def buffer(*shape):
    return pltpu.VMEM(shape, jnp.float32)


def call(kernel, n_scalars, n_arrays, outs, scratch=(), space=VMEM, mib=24):
    many = isinstance(outs, tuple)
    return pl.pallas_call(
        kernel,
        out_shape=outs,
        in_specs=[SMEM] * n_scalars + [space] * n_arrays,
        out_specs=(VMEM,) * len(outs) if many else VMEM,
        scratch_shapes=list(scratch),
        compiler_params=pltpu.CompilerParams(vmem_limit_bytes=mib * 1024 * 1024),
    )


def cut(meta, init, ends, vel):
    state, flow = buffer(3, ROWS, 1024), buffer(2, ROWS, 1024)
    scratch = [state, state, flow, pltpu.SemaphoreType.DMA((3,))]
    return call(cut_kernel, 1, 3, f32(160, 8, 128), scratch, HBM, 60)(meta, init, ends, vel)


def cycle(meta, mate, cur, other):
    tall = BAND + 1
    scratch = [
        buffer(12, tall, 8, 128),
        buffer(12, tall, 8, 128),
        buffer(8, BAND, 8, 128),
        buffer(12, BAND, 8, 128),
        buffer(3, BAND, 8, 128),
        buffer(3, BAND, 8, 128),
        buffer(3, tall, 8, 128),
        buffer(3, tall, 8, 128),
        buffer(3, tall, 8, 128),
        buffer(3, BAND, 8, 128),
        buffer(9, tall, 8, 128),
    ]
    return call(cycle_kernel, 1, 3, f32(768, 128), scratch)(meta, mate, cur, other)


def join(meta, tiles, vel):
    halo = 5 * FINE * 8
    outs = (f32(3, ROWS, 1024), f32(5 * ROWS * 8, 128), f32(halo, 128), f32(halo, 128))
    return call(join_kernel, 1, 2, outs)(meta, tiles, vel)


def relax(meta, mid, mate, other):
    tall = ROWS + 2 * FINE
    scratch = [
        buffer(3 * tall, 8, 128),
        buffer(3 * tall, 8, 128),
        buffer(2 * tall, 8, 128),
        buffer(3 * ROWS * 8, 128),
    ]
    return call(relax_kernel, 1, 3, f32(3, ROWS, 1024), scratch)(meta, mid, mate, other)


def per_device(initial_state, guessed_ends, velocity):
    slabs = lax.axis_size("gy")
    mates = [(i, i ^ 1) for i in range(slabs)]
    others = [(i, i + 1 if i % 2 else i - 1) for i in range(1, slabs - 1)]
    intervals = lax.axis_size("tm")
    here = lax.axis_index("tm").astype(jnp.int32).reshape(1)
    slab = jnp.stack([lax.axis_index("gy").astype(jnp.int32), jnp.int32(slabs)])
    flow = velocity[0]

    windows = cut(here, initial_state, guessed_ends[0], flow)
    cur = lax.all_to_all(windows.reshape(intervals, 40, 128), "tm", 0, 0)
    cur = cur.reshape(intervals * 40, 128)
    mate = lax.ppermute(cur, "gy", mates)
    other = lax.ppermute(cur, "gy", others)
    tiles = cycle(slab, mate, cur, other)
    tiles = lax.all_to_all(tiles.reshape(intervals, 24, 128), "tm", 0, 0)
    own, mid, mate, other = join(slab, tiles.reshape(intervals * 3, 8, 128), flow)
    mate = lax.ppermute(mate, "gy", mates)
    other = lax.ppermute(other, "gy", others)
    relaxed = relax(
        slab,
        mid.reshape(5 * ROWS, 8, 128),
        mate.reshape(5 * FINE, 8, 128),
        other.reshape(5 * FINE, 8, 128),
    )
    return own[None], relaxed[None]


def solution(mesh):
    placed = (P(None, "gy", None), P("tm", None, "gy", None), P("tm", None, "gy", None))
    return jax.shard_map(
        per_device,
        mesh=mesh,
        in_specs=placed,
        out_specs=(P("tm", None, "gy", None), P("tm", None, "gy", None)),
        check_vma=False,
    )
```

```python
import jax
import jax.numpy as jnp
from jax import lax
from jax.experimental import pallas as pl
from jax.experimental.pallas import tpu as pltpu
from jax.sharding import PartitionSpec as P

FINE = 4
GROUP = 4
GROUPS = 8
HALO = 16
TILE = 32
ROWS = 16
HALF = 64
BAND = 24

diffusion = (0.05, 0.15, 0.4)
kappa_coupling = 0.1
time_step = 0.0125
coarsest = FINE * GROUP * time_step

VMEM = pl.BlockSpec(memory_space=pltpu.VMEM)
HBM = pl.BlockSpec(memory_space=pltpu.HBM)
SMEM = pl.BlockSpec(memory_space=pltpu.SMEM)


def lanes():
    return lax.broadcasted_iota(jnp.int32, (8, 128), 1)


def sublanes():
    return lax.broadcasted_iota(jnp.int32, (8, 128), 0)


def swap8(values):
    sub = sublanes()
    for s in (4, 2, 1):
        keep = sub % (2 * s) < s
        new = list(values)
        for p in range(8):
            if p % (2 * s) < s:
                a, b = values[p], values[p + s]
                new[p] = jnp.where(keep, a, pltpu.roll(b, s, 0))
                new[p + s] = jnp.where(keep, pltpu.roll(a, 8 - s, 0), b)
        values = new
    return values


def slope(west, east, below, above, across, along, scale=1.0):
    right, upward = across > 0.0, along > 0.0
    out = []
    for c in range(3):
        spread = (east[c] - west[c]) + (above[c] - below[c])
        transport = across * jnp.where(right, west[c], east[c]) + along * jnp.where(upward, below[c], above[c])
        out.append((scale * time_step * diffusion[c]) * spread - transport)
    return out


def cut_kernel(meta, init_hbm, ends_hbm, vel_hbm, out, flow, init, ends, vel, sems):
    copies = [
        pltpu.make_async_copy(far, near, sems.at[i])
        for i, (far, near) in enumerate(((init_hbm, init), (ends_hbm, ends), (vel_hbm, vel)))
    ]
    for copy in copies:
        copy.start()
    for copy in copies:
        copy.wait()
    last = meta[0] == GROUP * GROUPS - 1
    low = lanes() < HALF
    for a in range(5):
        if a < 3:
            top = jnp.where(last, init[a, 0:8, :], ends[a, 0:8, :])
            bottom = jnp.where(last, init[a, 8:16, :], ends[a, 8:16, :])
        else:
            top, bottom = vel[a - 3, 0:8, :], vel[a - 3, 8:16, :]
        for q in range(4):
            upper = pltpu.roll(top, (HALO - TILE * q) % 1024, 1)
            lower = pltpu.roll(bottom, (HALO + HALF - TILE * q) % 1024, 1)
            for b in range(8):
                at = slice(128 * b, 128 * b + 128)
                out[(4 * b + q) * 5 + a] = jnp.where(low, upper[:, at], lower[:, at])
    for c in range(2):
        for y0 in (0, 8):
            blocks = [vel[c, y0 : y0 + 8, 128 * b : 128 * b + 128] for b in range(8)]
            for y, value in enumerate(swap8(blocks)):
                flow[c * ROWS + y0 + y] = value


def cycle_kernel(meta, mate, cur, other, out, ua, ub, vv, src, gg, ff, init, xa, xb, yy, cc):
    lane, sub = lanes(), sublanes()
    low = lane < HALF
    sign = jnp.where(low, 1.0, -1.0)
    kappa = time_step * kappa_coupling
    swing = kappa * sign
    even = meta[0] % 2 == 0
    outside = jnp.where(low, meta[0], meta[1] - 1 - meta[0]) == 0

    def step(buf, base, k, start, emit, scale=1.0):
        pl.when(meta[1] > 0)(lambda: sweep(buf, base, k, start, emit, scale))

    def sweep(buf, base, k, start, emit, scale):
        rows, climbs = {}, {}

        def row(r):
            if r not in rows:
                rows[r] = [buf[base + c, r] for c in range(3)]
            return rows[r]

        def climb(r):
            if r not in climbs:
                climbs[r] = [x - y for x, y in zip(row(r + 1), row(r))]
            return climbs[r]

        for r in range(start, BAND):
            u = row(r)
            west = [x - pltpu.roll(x, 1, 1) for x in u]
            east = [pltpu.roll(x, 127, 1) - x for x in u]
            across = vv[2 * k, r] + (scale * kappa) * u[0]
            along = vv[2 * k + 1, r] + (scale * swing) * u[1]
            emit(r, u, slope(west, east, climb(r - 1), climb(r), across, along, scale))

    def put(buf, at, r, value):
        if r == HALO - 1:
            value = jnp.where(outside, 0.0, value)
        buf[at, r] = value
        if r == BAND - 1:
            buf[at, BAND] = pltpu.roll(value, HALF, 1)

    for k in range(GROUP):
        for a in range(5):
            at = [(4 * j + k) * 5 + a for j in range(8)]
            own = swap8([cur[i] for i in at])
            before = swap8([jnp.where(even, other[i], mate[i]) for i in at])
            after = swap8([jnp.where(even, mate[i], other[i]) for i in at])
            for y in range(8):
                rows = (
                    (y, jnp.where(low, before[y], after[7 - y])),
                    (y + 8, pltpu.roll(jnp.where(low, after[7 - y], before[y]), HALF, 1)),
                    (y + 16, jnp.where(low, own[y], own[7 - y])),
                )
                for r, value in rows:
                    if a == 3:
                        vv[2 * k, r] = time_step * value
                        if k == GROUP - 1:
                            vv[2 * GROUP, r] = coarsest * value
                    elif a == 4:
                        vv[2 * k + 1, r] = (time_step * sign) * value
                        if k == GROUP - 1:
                            vv[2 * GROUP + 1, r] = (coarsest * sign) * value
                    elif k == GROUP - 1:
                        value = pltpu.roll(value, 1, 0)
                        put(ua, a, r, value)
                        put(xa, a, r, value)
                        xb[a, r] = value
                        init[a, r] = value
                    else:
                        put(ua, 3 * (k + 1) + a, r, value)

    def keep_g(r, u, s):
        for c in range(3):
            gg[c, r] = u[c] + s[c]

    step(ua, 0, GROUP, 7, keep_g, float(FINE * GROUP))

    def fine(k, carry):
        base = 3 * k

        def opening(r, u, s):
            for c in range(3):
                put(ub, base + c, r, u[c] + s[c])
                src[base + c, r] = u[c] + float(FINE) * s[c]

        def onward(buf):
            def emit(r, u, s):
                for c in range(3):
                    put(buf, base + c, r, u[c] + s[c])

            return emit

        def closing(r, u, s):
            for c in range(3):
                end = u[c] + s[c]
                put(ua, base + c, r, end)
                src[base + c, r] = end - src[base + c, r]

        step(ua, base, k, 1, opening)
        step(ub, base, k, 2, onward(ua))
        step(ua, base, k, 3, onward(ub))
        step(ub, base, k, 4, closing)
        return carry

    lax.fori_loop(0, GROUP, fine, 0)

    def plus(buf, k, base):
        def emit(r, u, s):
            for c in range(3):
                put(buf, base + c, r, u[c] + float(FINE) * s[c] + src[3 * k + c, r])

        return emit

    step(ua, 0, 1, 5, plus(ub, 1, 0))
    step(ub, 0, 2, 6, plus(ua, 2, 0))

    def forcing(r, u, s):
        for c in range(3):
            ff[c, r] = u[c] + float(FINE) * s[c] + src[3 * (GROUP - 1) + c, r] - gg[c, r]

    step(ua, 0, GROUP - 1, 7, forcing)

    for t in range(GROUPS):
        buf, to = (xa, xb) if t % 2 == 0 else (xb, xa)

        def settle(r, u, s):
            for c in range(3):
                y = u[c] + s[c] + ff[c, r]
                if t == GROUPS - 1 and r >= HALO:
                    yy[c, r] = y
                put(to, c, r, jnp.where(sub == 0, init[c, r], pltpu.roll(y, 1, 0)))

        step(buf, 0, GROUP, max(7, 6 + t), settle, float(FINE * GROUP))

    step(xa, 0, 0, 14, plus(cc, 0, 0))
    step(cc, 0, 1, 15, plus(cc, 1, 3))
    step(cc, 3, 2, 16, plus(cc, 2, 6))

    def compact(buf, base, c, y):
        m = jnp.where(low, buf[base + c, y + 16], buf[base + c, 23 - y])
        return jnp.where(lane < TILE, pltpu.roll(m, 128 - HALO, 1), pltpu.roll(m, 128 - HALO - TILE, 1))

    reads = [(xa, 0), (cc, 0), (cc, 3), (cc, 6), (yy, 0)]
    for c in range(3):
        before = [compact(*reads[0], c, y) for y in range(8)]
        for k in range(GROUP):
            own = [compact(*reads[k + 1], c, y) for y in range(8)]
            values = [jnp.where(low, x, pltpu.roll(y, HALF, 1)) for x, y in zip(own, before)]
            for j, value in enumerate(swap8(values)):
                out[(4 * j + k) * 3 + c] = value
            before = own


def gathered(tiles, c, b, part):
    group = lanes() // TILE
    value = None
    for q in range(4):
        shift = (TILE * (q - part)) % 128
        x = tiles[(4 * b + q) * 3 + c]
        x = pltpu.roll(x, shift, 1) if shift else x
        value = x if value is None else jnp.where(group == q, x, value)
    return value


def begin_kernel(meta, tiles, flow, begin, mate, other):
    even = meta[0] % 2 == 0
    for c in range(5):
        if c < 3:
            rows = []
            for part in (2, 3):
                rows += swap8([gathered(tiles, c, b, part) for b in range(8)])
            for y in range(ROWS):
                begin[c * ROWS + y] = rows[y]
        else:
            rows = [flow[(c - 3) * ROWS + y] for y in range(ROWS)]
        for y in range(FINE):
            down, up = rows[y], rows[ROWS - FINE + y]
            mate[c * FINE + y] = jnp.where(even, up, down)
            other[c * FINE + y] = jnp.where(even, down, up)


def own_kernel(tiles, own):
    for c in range(3):
        for b in range(8):
            at = slice(128 * b, 128 * b + 128)
            own[c, 0:8, at] = gathered(tiles, c, b, 0)
            own[c, 8:16, at] = gathered(tiles, c, b, 1)


def relax_kernel(meta, mid, flow, mate, other, out, wa, wb, vv):
    lane = lanes()
    tall = ROWS + 2 * FINE
    kappa = time_step * kappa_coupling
    even = meta[0] % 2 == 0
    for a in range(5):
        src, buf, at = (mid, wa, a) if a < 3 else (flow, vv, a - 3)
        scale = 1.0 if a < 3 else time_step
        for r in range(FINE):
            m, o = mate[a * FINE + r], other[a * FINE + r]
            buf[at * tall + r] = scale * jnp.where(even, o, m)
            buf[at * tall + FINE + ROWS + r] = scale * jnp.where(even, m, o)
        for r in range(ROWS):
            buf[at * tall + FINE + r] = scale * src[at * ROWS + r]

    bottom, top = meta[0] == 0, meta[0] == meta[1] - 1
    def sweep(section, buf, to):
        rows = {r: [buf[c * tall + r] for c in range(3)] for r in range(section, tall - section)}
        climbs = {r: [x - y for x, y in zip(rows[r + 1], rows[r])] for r in range(section, tall - section - 1)}
        ends = []
        for r in range(section + 1, tall - section - 1):
            u = rows[r]
            west, east = [], []
            for x in u:
                y = pltpu.roll(x, 1, 1)
                west.append(x - jnp.where(lane == 0, pltpu.roll(y, 1, 0), y))
                y = pltpu.roll(x, 127, 1)
                east.append(jnp.where(lane == 127, pltpu.roll(y, 7, 0), y) - x)
            across = vv[r] + kappa * u[0]
            along = vv[tall + r] + kappa * u[1]
            s = slope(west, east, climbs[r - 1], climbs[r], across, along)
            new = [x + y for x, y in zip(u, s)]
            ends.append(new)
            for c in range(3):
                if r == FINE - 1:
                    new[c] = jnp.where(bottom, 0.0, new[c])
                elif r == FINE + ROWS:
                    new[c] = jnp.where(top, 0.0, new[c])
                if section < FINE - 1:
                    to[c * tall + r] = new[c]
        if section == FINE - 1:
            for y0 in (0, 8):
                for c in range(3):
                    for b, value in enumerate(swap8([ends[y0 + y][c] for y in range(8)])):
                        out[c, y0 : y0 + 8, 128 * b : 128 * b + 128] = value

    for section in range(FINE):
        buf, to = (wa, wb) if section % 2 == 0 else (wb, wa)
        sweep(section, buf, to)


def f32(*shape):
    return jax.ShapeDtypeStruct(shape, jnp.float32)


def buffer(*shape):
    return pltpu.VMEM(shape, jnp.float32)


def call(kernel, n_scalars, n_arrays, outs, scratch=(), space=VMEM, mib=24):
    many = isinstance(outs, tuple)
    return pl.pallas_call(
        kernel,
        out_shape=outs,
        in_specs=[SMEM] * n_scalars + [space] * n_arrays,
        out_specs=(VMEM,) * len(outs) if many else VMEM,
        scratch_shapes=list(scratch),
        compiler_params=pltpu.CompilerParams(vmem_limit_bytes=mib * 1024 * 1024),
    )


def cut(meta, init, ends, vel):
    state, flow = buffer(3, ROWS, 1024), buffer(2, ROWS, 1024)
    scratch = [state, state, flow, pltpu.SemaphoreType.DMA((3,))]
    outs = (f32(160, 8, 128), f32(2 * ROWS, 8, 128))
    return call(cut_kernel, 1, 3, outs, scratch, HBM, 60)(meta, init, ends, vel)


def cycle(meta, mate, cur, other):
    tall = BAND + 1
    scratch = [
        buffer(12, tall, 8, 128),
        buffer(12, tall, 8, 128),
        buffer(10, BAND, 8, 128),
        buffer(12, BAND, 8, 128),
        buffer(3, BAND, 8, 128),
        buffer(3, BAND, 8, 128),
        buffer(3, tall, 8, 128),
        buffer(3, tall, 8, 128),
        buffer(3, tall, 8, 128),
        buffer(3, BAND, 8, 128),
        buffer(9, tall, 8, 128),
    ]
    return call(cycle_kernel, 1, 3, f32(96, 8, 128), scratch)(meta, mate, cur, other)


def begins(meta, tiles, flow):
    halo = f32(5 * FINE, 8, 128)
    return call(begin_kernel, 1, 2, (f32(3 * ROWS, 8, 128), halo, halo))(meta, tiles, flow)


def owns(tiles):
    return call(own_kernel, 0, 1, f32(3, ROWS, 1024))(tiles)


def relax(meta, mid, flow, mate, other):
    tall = ROWS + 2 * FINE
    scratch = [buffer(3 * tall, 8, 128), buffer(3 * tall, 8, 128), buffer(2 * tall, 8, 128)]
    return call(relax_kernel, 1, 4, f32(3, ROWS, 1024), scratch)(meta, mid, flow, mate, other)


def per_device(initial_state, guessed_ends, velocity):
    slabs = lax.axis_size("gy")
    mates = [(i, i ^ 1) for i in range(slabs)]
    others = [(i, i + 1 if i % 2 else i - 1) for i in range(1, slabs - 1)]
    intervals = lax.axis_size("tm")
    here = lax.axis_index("tm").astype(jnp.int32).reshape(1)
    slab = jnp.stack([lax.axis_index("gy").astype(jnp.int32), jnp.int32(slabs)])

    windows, flow = cut(here, initial_state, guessed_ends[0], velocity[0])
    cur = lax.all_to_all(windows.reshape(intervals, 40, 128), "tm", 0, 0)
    cur = cur.reshape(intervals * 5, 8, 128)
    mate = lax.ppermute(cur, "gy", mates)
    other = lax.ppermute(cur, "gy", others)
    tiles = cycle(slab, mate, cur, other)
    tiles = lax.all_to_all(tiles.reshape(intervals, 24, 128), "tm", 0, 0)
    tiles = tiles.reshape(intervals * 3, 8, 128)
    mid, mate, other = begins(slab, tiles, flow)
    mate = lax.ppermute(mate, "gy", mates)
    other = lax.ppermute(other, "gy", others)
    own = owns(tiles)
    relaxed = relax(slab, mid, flow, mate, other)
    return own[None], relaxed[None]


def solution(mesh):
    placed = (P(None, "gy", None), P("tm", None, "gy", None), P("tm", None, "gy", None))
    return jax.shard_map(
        per_device,
        mesh=mesh,
        in_specs=placed,
        out_specs=(P("tm", None, "gy", None), P("tm", None, "gy", None)),
        check_vma=False,
    )
```

```python
import functools

import jax
import jax.numpy as jnp
from jax import lax
from jax.experimental import pallas as pl
from jax.experimental.pallas import tpu as pltpu
from jax.sharding import PartitionSpec as P

FINE = 4
GROUP = 4
GROUPS = 8
HALO = 16
TILE = 32
ROWS = 16
HALF = 64
BAND = 24

diffusion = (0.05, 0.15, 0.4)
kappa_coupling = 0.1
time_step = 0.0125
coarsest = FINE * GROUP * time_step

VMEM = pl.BlockSpec(memory_space=pltpu.VMEM)
HBM = pl.BlockSpec(memory_space=pltpu.HBM)
SMEM = pl.BlockSpec(memory_space=pltpu.SMEM)


def lanes():
    return lax.broadcasted_iota(jnp.int32, (8, 128), 1)


def sublanes():
    return lax.broadcasted_iota(jnp.int32, (8, 128), 0)


def swap8(values):
    sub = sublanes()
    for s in (4, 2, 1):
        keep = sub % (2 * s) < s
        new = list(values)
        for p in range(8):
            if p % (2 * s) < s:
                a, b = values[p], values[p + s]
                new[p] = jnp.where(keep, a, pltpu.roll(b, s, 0))
                new[p + s] = jnp.where(keep, pltpu.roll(a, 8 - s, 0), b)
        values = new
    return values


def slope(west, east, below, above, across, along, scale=1.0):
    right, upward = across > 0.0, along > 0.0
    out = []
    for c in range(3):
        spread = (east[c] - west[c]) + (above[c] - below[c])
        transport = across * jnp.where(right, west[c], east[c]) + along * jnp.where(upward, below[c], above[c])
        out.append((scale * time_step * diffusion[c]) * spread - transport)
    return out


def cut_kernel(meta, init_hbm, ends_hbm, vel_hbm, out, flow, init, ends, vel, sems):
    copies = [
        pltpu.make_async_copy(far, near, sems.at[i])
        for i, (far, near) in enumerate(((init_hbm, init), (ends_hbm, ends), (vel_hbm, vel)))
    ]
    for copy in copies:
        copy.start()
    for copy in copies:
        copy.wait()
    last = meta[0] == GROUP * GROUPS - 1
    low = lanes() < HALF
    for a in range(5):
        if a < 3:
            top = jnp.where(last, init[a, 0:8, :], ends[a, 0:8, :])
            bottom = jnp.where(last, init[a, 8:16, :], ends[a, 8:16, :])
        else:
            top, bottom = vel[a - 3, 0:8, :], vel[a - 3, 8:16, :]
        for q in range(4):
            upper = pltpu.roll(top, (HALO - TILE * q) % 1024, 1)
            lower = pltpu.roll(bottom, (HALO + HALF - TILE * q) % 1024, 1)
            for b in range(8):
                at = slice(128 * b, 128 * b + 128)
                out[(4 * b + q) * 5 + a] = jnp.where(low, upper[:, at], lower[:, at])
    for c in range(2):
        for y0 in (0, 8):
            blocks = [vel[c, y0 : y0 + 8, 128 * b : 128 * b + 128] for b in range(8)]
            for y, value in enumerate(swap8(blocks)):
                flow[c * ROWS + y0 + y] = value


def sort_kernel(cur, both, one, two):
    for k in range(GROUP):
        for a in range(5):
            values = swap8([cur[(4 * j + k) * 5 + a] for j in range(8)])
            to = k
            if a < 3:
                to = (k + 1) % GROUP
                if to == 0:
                    values = [pltpu.roll(value, 1, 0) for value in values]
            half = one if to < 2 else two
            for y in range(8):
                half[(to % 2 * 5 + a) * 8 + y] = values[y]
                both[(to * 5 + a) * 8 + y] = values[y]


def masks(meta):
    low = lanes() < HALF
    sign = jnp.where(low, 1.0, -1.0)
    outside = jnp.where(low, meta[0], meta[1] - 1 - meta[0]) == 0
    return low, sign, outside


def putter(outside):
    def put(buf, at, r, value):
        if r == HALO - 1:
            value = jnp.where(outside, 0.0, value)
        buf[at, r] = value
        if r == BAND - 1:
            buf[at, BAND] = pltpu.roll(value, HALF, 1)

    return put


def stepper(meta, sign):
    kappa = time_step * kappa_coupling
    swing = kappa * sign

    def sweep(buf, base, flow, at, start, emit, scale):
        rows, climbs = {}, {}

        def row(r):
            if r not in rows:
                rows[r] = [buf[base + c, r] for c in range(3)]
            return rows[r]

        def climb(r):
            if r not in climbs:
                climbs[r] = [x - y for x, y in zip(row(r + 1), row(r))]
            return climbs[r]

        for r in range(start, BAND):
            u = row(r)
            west = [x - pltpu.roll(x, 1, 1) for x in u]
            east = [pltpu.roll(x, 127, 1) - x for x in u]
            across = flow[at, r] + (scale * kappa) * u[0]
            along = flow[at + 1, r] + (scale * swing) * u[1]
            emit(r, u, slope(west, east, climb(r - 1), climb(r), across, along, scale))

    def step(buf, base, flow, at, start, emit, scale=1.0):
        pl.when(meta[1] > 0)(lambda: sweep(buf, base, flow, at, start, emit, scale))

    return step


def fine_kernel(pair, meta, own, mate, other, vv, src, ua, *more):
    ub = more[-1]
    low, sign, outside = masks(meta)
    put, step = putter(outside), stepper(meta, sign)
    even = meta[0] % 2 == 0
    for k in range(2):
        for a in range(5):
            at = (k * 5 + a) * 8
            mine = [own[at + y] for y in range(8)]
            m = [mate[pair * 80 + at + y] for y in range(8)]
            o = [other[at + y] for y in range(8)]
            before = [jnp.where(even, x, y) for x, y in zip(o, m)]
            after = [jnp.where(even, y, x) for x, y in zip(o, m)]
            for y in range(8):
                rows = (
                    (y, jnp.where(low, before[y], after[7 - y])),
                    (y + 8, pltpu.roll(jnp.where(low, after[7 - y], before[y]), HALF, 1)),
                    (y + 16, jnp.where(low, mine[y], mine[7 - y])),
                )
                for r, value in rows:
                    if a < 3:
                        put(ua, 3 * k + a, r, value)
                        if pair == 0 and k == 0:
                            put(more[0], a, r, value)
                        continue
                    way = 1.0 if a == 3 else sign
                    vv[2 * k + a - 3, r] = (time_step * way) * value
                    if pair == 1 and k == 1:
                        vv[4 + a - 3, r] = (coarsest * way) * value

    def fine(k, carry):
        base = 3 * k

        def opening(r, u, s):
            for c in range(3):
                put(ub, base + c, r, u[c] + s[c])
                src[base + c, r] = u[c] + float(FINE) * s[c]

        def onward(buf):
            def emit(r, u, s):
                for c in range(3):
                    put(buf, base + c, r, u[c] + s[c])

            return emit

        def closing(r, u, s):
            for c in range(3):
                end = u[c] + s[c]
                put(ua, base + c, r, end)
                src[base + c, r] = end - src[base + c, r]

        step(ua, base, vv, 2 * k, 1, opening)
        step(ub, base, vv, 2 * k, 2, onward(ua))
        step(ua, base, vv, 2 * k, 3, onward(ub))
        step(ub, base, vv, 2 * k, 4, closing)
        return carry

    lax.fori_loop(0, 2, fine, 0)


def coarse_kernel(meta, ends, vv0, src0, begin, vv1, src1, out, ua, ub, gg, ff, xa, xb, yy, cc):
    lane, sub = lanes(), sublanes()
    low, sign, outside = masks(meta)
    put, step = putter(outside), stepper(meta, sign)
    flows = [(vv0, 0), (vv0, 2), (vv1, 0), (vv1, 2)]
    wide = (vv1, 4)
    srcs = [(src0, 0), (src0, 3), (src1, 0), (src1, 3)]

    def keep_g(r, u, s):
        for c in range(3):
            gg[c, r] = u[c] + s[c]

    step(begin, 0, *wide, 7, keep_g, float(FINE * GROUP))

    def plus(buf, k, base):
        src, at = srcs[k]

        def emit(r, u, s):
            for c in range(3):
                put(buf, base + c, r, u[c] + float(FINE) * s[c] + src[at + c, r])

        return emit

    step(ends, 0, *flows[1], 5, plus(ub, 1, 0))
    step(ub, 0, *flows[2], 6, plus(ua, 2, 0))

    def forcing(r, u, s):
        for c in range(3):
            ff[c, r] = u[c] + float(FINE) * s[c] + src1[3 + c, r] - gg[c, r]

    step(ua, 0, *flows[3], 7, forcing)

    for c in range(3):
        xb[c, 6] = begin[c, 6]
    for t in range(GROUPS):
        buf, to = (xa if t else begin, xb) if t % 2 == 0 else (xb, xa)

        def settle(r, u, s):
            for c in range(3):
                y = u[c] + s[c] + ff[c, r]
                if t == GROUPS - 1 and r >= HALO:
                    yy[c, r] = y
                put(to, c, r, jnp.where(sub == 0, begin[c, r], pltpu.roll(y, 1, 0)))

        step(buf, 0, *wide, max(7, 6 + t), settle, float(FINE * GROUP))

    step(xa, 0, *flows[0], 14, plus(cc, 0, 0))
    step(cc, 0, *flows[1], 15, plus(cc, 1, 3))
    step(cc, 3, *flows[2], 16, plus(cc, 2, 6))

    def compact(buf, base, c, y):
        m = jnp.where(low, buf[base + c, y + 16], buf[base + c, 23 - y])
        return jnp.where(lane < TILE, pltpu.roll(m, 128 - HALO, 1), pltpu.roll(m, 128 - HALO - TILE, 1))

    reads = [(xa, 0), (cc, 0), (cc, 3), (cc, 6), (yy, 0)]
    for c in range(3):
        before = [compact(*reads[0], c, y) for y in range(8)]
        for k in range(GROUP):
            own = [compact(*reads[k + 1], c, y) for y in range(8)]
            values = [jnp.where(low, x, pltpu.roll(y, HALF, 1)) for x, y in zip(own, before)]
            for j, value in enumerate(swap8(values)):
                out[(4 * j + k) * 3 + c] = value
            before = own


def gathered(tiles, c, b, part):
    group = lanes() // TILE
    value = None
    for q in range(4):
        shift = (TILE * (q - part)) % 128
        x = tiles[(4 * b + q) * 3 + c]
        x = pltpu.roll(x, shift, 1) if shift else x
        value = x if value is None else jnp.where(group == q, x, value)
    return value


def begin_kernel(meta, tiles, flow, begin, mate, other):
    even = meta[0] % 2 == 0
    for c in range(5):
        if c < 3:
            rows = []
            for part in (2, 3):
                rows += swap8([gathered(tiles, c, b, part) for b in range(8)])
            for y in range(ROWS):
                begin[c * ROWS + y] = rows[y]
        else:
            rows = [flow[(c - 3) * ROWS + y] for y in range(ROWS)]
        for y in range(FINE):
            down, up = rows[y], rows[ROWS - FINE + y]
            mate[c * FINE + y] = jnp.where(even, up, down)
            other[c * FINE + y] = jnp.where(even, down, up)


def own_kernel(tiles, own):
    for c in range(3):
        for b in range(8):
            at = slice(128 * b, 128 * b + 128)
            own[c, 0:8, at] = gathered(tiles, c, b, 0)
            own[c, 8:16, at] = gathered(tiles, c, b, 1)


def relax_kernel(meta, mid, flow, mate, other, out, wa, wb, vv):
    lane = lanes()
    tall = ROWS + 2 * FINE
    kappa = time_step * kappa_coupling
    even = meta[0] % 2 == 0
    for a in range(5):
        src, buf, at = (mid, wa, a) if a < 3 else (flow, vv, a - 3)
        scale = 1.0 if a < 3 else time_step
        for r in range(FINE):
            m, o = mate[a * FINE + r], other[a * FINE + r]
            buf[at * tall + r] = scale * jnp.where(even, o, m)
            buf[at * tall + FINE + ROWS + r] = scale * jnp.where(even, m, o)
        for r in range(ROWS):
            buf[at * tall + FINE + r] = scale * src[at * ROWS + r]

    bottom, top = meta[0] == 0, meta[0] == meta[1] - 1
    def sweep(section, buf, to):
        rows = {r: [buf[c * tall + r] for c in range(3)] for r in range(section, tall - section)}
        climbs = {r: [x - y for x, y in zip(rows[r + 1], rows[r])] for r in range(section, tall - section - 1)}
        ends = []
        for r in range(section + 1, tall - section - 1):
            u = rows[r]
            west, east = [], []
            for x in u:
                y = pltpu.roll(x, 1, 1)
                west.append(x - jnp.where(lane == 0, pltpu.roll(y, 1, 0), y))
                y = pltpu.roll(x, 127, 1)
                east.append(jnp.where(lane == 127, pltpu.roll(y, 7, 0), y) - x)
            across = vv[r] + kappa * u[0]
            along = vv[tall + r] + kappa * u[1]
            s = slope(west, east, climbs[r - 1], climbs[r], across, along)
            new = [x + y for x, y in zip(u, s)]
            ends.append(new)
            for c in range(3):
                if r == FINE - 1:
                    new[c] = jnp.where(bottom, 0.0, new[c])
                elif r == FINE + ROWS:
                    new[c] = jnp.where(top, 0.0, new[c])
                if section < FINE - 1:
                    to[c * tall + r] = new[c]
        if section == FINE - 1:
            for y0 in (0, 8):
                for c in range(3):
                    for b, value in enumerate(swap8([ends[y0 + y][c] for y in range(8)])):
                        out[c, y0 : y0 + 8, 128 * b : 128 * b + 128] = value

    for section in range(FINE):
        buf, to = (wa, wb) if section % 2 == 0 else (wb, wa)
        sweep(section, buf, to)


def f32(*shape):
    return jax.ShapeDtypeStruct(shape, jnp.float32)


def buffer(*shape):
    return pltpu.VMEM(shape, jnp.float32)


def call(kernel, n_scalars, n_arrays, outs, scratch=(), space=VMEM, mib=24):
    many = isinstance(outs, tuple)
    return pl.pallas_call(
        kernel,
        out_shape=outs,
        in_specs=[SMEM] * n_scalars + [space] * n_arrays,
        out_specs=(VMEM,) * len(outs) if many else VMEM,
        scratch_shapes=list(scratch),
        compiler_params=pltpu.CompilerParams(vmem_limit_bytes=mib * 1024 * 1024),
    )


def cut(meta, init, ends, vel):
    state, flow = buffer(3, ROWS, 1024), buffer(2, ROWS, 1024)
    scratch = [state, state, flow, pltpu.SemaphoreType.DMA((3,))]
    outs = (f32(160, 8, 128), f32(2 * ROWS, 8, 128))
    return call(cut_kernel, 1, 3, outs, scratch, HBM, 60)(meta, init, ends, vel)


def sort(cur):
    return call(sort_kernel, 0, 1, (f32(160, 8, 128), f32(80, 8, 128), f32(80, 8, 128)))(cur)


def fine(pair, meta, own, mate, other):
    tall = BAND + 1
    outs = [f32(4 + 2 * pair, BAND, 8, 128), f32(6, BAND, 8, 128)]
    scratch = [buffer(6, tall, 8, 128)]
    if pair == 0:
        outs += [f32(6, tall, 8, 128), f32(3, tall, 8, 128)]
    else:
        scratch *= 2
    kernel = functools.partial(fine_kernel, pair)
    return call(kernel, 1, 3, tuple(outs), scratch)(meta, own, mate, other)


def coarse(meta, *arrays):
    tall = BAND + 1
    scratch = [
        buffer(3, tall, 8, 128),
        buffer(3, tall, 8, 128),
        buffer(3, BAND, 8, 128),
        buffer(3, BAND, 8, 128),
        buffer(3, tall, 8, 128),
        buffer(3, tall, 8, 128),
        buffer(3, BAND, 8, 128),
        buffer(9, tall, 8, 128),
    ]
    return call(coarse_kernel, 1, 6, f32(96, 8, 128), scratch)(meta, *arrays)


def begins(meta, tiles, flow):
    halo = f32(5 * FINE, 8, 128)
    return call(begin_kernel, 1, 2, (f32(3 * ROWS, 8, 128), halo, halo))(meta, tiles, flow)


def owns(tiles):
    return call(own_kernel, 0, 1, f32(3, ROWS, 1024))(tiles)


def relax(meta, mid, flow, mate, other):
    tall = ROWS + 2 * FINE
    scratch = [buffer(3 * tall, 8, 128), buffer(3 * tall, 8, 128), buffer(2 * tall, 8, 128)]
    return call(relax_kernel, 1, 4, f32(3, ROWS, 1024), scratch)(meta, mid, flow, mate, other)


def per_device(initial_state, guessed_ends, velocity):
    slabs = lax.axis_size("gy")
    mates = [(i, i ^ 1) for i in range(slabs)]
    others = [(i, i + 1 if i % 2 else i - 1) for i in range(1, slabs - 1)]
    intervals = lax.axis_size("tm")
    here = lax.axis_index("tm").astype(jnp.int32).reshape(1)
    slab = jnp.stack([lax.axis_index("gy").astype(jnp.int32), jnp.int32(slabs)])

    windows, flow = cut(here, initial_state, guessed_ends[0], velocity[0])
    cur = lax.all_to_all(windows.reshape(intervals, 40, 128), "tm", 0, 0)
    cur = cur.reshape(intervals * 5, 8, 128)
    both, one, two = sort(cur)
    other_one = lax.ppermute(one, "gy", others)
    other_two = lax.ppermute(two, "gy", others)
    mate = lax.ppermute(both, "gy", mates)
    vv0, src0, ends, begin = fine(0, slab, one, mate, other_one)
    vv1, src1 = fine(1, slab, two, mate, other_two)
    tiles = coarse(slab, ends, vv0, src0, begin, vv1, src1)
    tiles = lax.all_to_all(tiles.reshape(intervals, 24, 128), "tm", 0, 0)
    tiles = tiles.reshape(intervals * 3, 8, 128)
    mid, mate, other = begins(slab, tiles, flow)
    mate = lax.ppermute(mate, "gy", mates)
    other = lax.ppermute(other, "gy", others)
    own = owns(tiles)
    relaxed = relax(slab, mid, flow, mate, other)
    return own[None], relaxed[None]


def solution(mesh):
    placed = (P(None, "gy", None), P("tm", None, "gy", None), P("tm", None, "gy", None))
    return jax.shard_map(
        per_device,
        mesh=mesh,
        in_specs=placed,
        out_specs=(P("tm", None, "gy", None), P("tm", None, "gy", None)),
        check_vma=False,
    )
```

```python
import jax
import jax.numpy as jnp
from jax import lax
from jax.experimental import pallas as pl
from jax.experimental.pallas import tpu as pltpu
from jax.sharding import PartitionSpec as P

FINE = 4
GROUP = 4
GROUPS = 8
HALO = 16
TILE = 32
ROWS = 16
HALF = 64
BAND = 24

diffusion = (0.05, 0.15, 0.4)
kappa_coupling = 0.1
time_step = 0.0125
coarsest = FINE * GROUP * time_step

VMEM = pl.BlockSpec(memory_space=pltpu.VMEM)
HBM = pl.BlockSpec(memory_space=pltpu.HBM)
SMEM = pl.BlockSpec(memory_space=pltpu.SMEM)


def lanes():
    return lax.broadcasted_iota(jnp.int32, (8, 128), 1)


def sublanes():
    return lax.broadcasted_iota(jnp.int32, (8, 128), 0)


def swap8(values):
    sub = sublanes()
    for s in (4, 2, 1):
        keep = sub % (2 * s) < s
        new = list(values)
        for p in range(8):
            if p % (2 * s) < s:
                a, b = values[p], values[p + s]
                new[p] = jnp.where(keep, a, pltpu.roll(b, s, 0))
                new[p + s] = jnp.where(keep, pltpu.roll(a, 8 - s, 0), b)
        values = new
    return values


def slope(west, east, below, above, across, along, scale=1.0):
    right, upward = across > 0.0, along > 0.0
    out = []
    for c in range(3):
        spread = (east[c] - west[c]) + (above[c] - below[c])
        transport = across * jnp.where(right, west[c], east[c]) + along * jnp.where(upward, below[c], above[c])
        out.append((scale * time_step * diffusion[c]) * spread - transport)
    return out


def cut_kernel(meta, init_hbm, ends_hbm, vel_hbm, out, flow, init, ends, vel, sems):
    copies = [
        pltpu.make_async_copy(far, near, sems.at[i])
        for i, (far, near) in enumerate(((init_hbm, init), (ends_hbm, ends), (vel_hbm, vel)))
    ]
    for copy in copies:
        copy.start()
    for copy in copies:
        copy.wait()
    last = meta[0] == GROUP * GROUPS - 1
    low = lanes() < HALF
    for a in range(5):
        if a < 3:
            top = jnp.where(last, init[a, 0:8, :], ends[a, 0:8, :])
            bottom = jnp.where(last, init[a, 8:16, :], ends[a, 8:16, :])
        else:
            top, bottom = vel[a - 3, 0:8, :], vel[a - 3, 8:16, :]
        for q in range(4):
            upper = pltpu.roll(top, (HALO - TILE * q) % 1024, 1)
            lower = pltpu.roll(bottom, (HALO + HALF - TILE * q) % 1024, 1)
            for b in range(8):
                at = slice(128 * b, 128 * b + 128)
                out[(4 * b + q) * 5 + a] = jnp.where(low, upper[:, at], lower[:, at])
    for c in range(2):
        for y0 in (0, 8):
            blocks = [vel[c, y0 : y0 + 8, 128 * b : 128 * b + 128] for b in range(8)]
            for y, value in enumerate(swap8(blocks)):
                flow[c * ROWS + y0 + y] = value


def cycle_kernel(meta, mate, cur, other, flow, xa, cc, yy, to_mate, to_other, ua, ub, vv, src, gg, ff, init, xb):
    lane, sub = lanes(), sublanes()
    low = lane < HALF
    sign = jnp.where(low, 1.0, -1.0)
    kappa = time_step * kappa_coupling
    swing = kappa * sign
    even = meta[0] % 2 == 0
    outside = jnp.where(low, meta[0], meta[1] - 1 - meta[0]) == 0

    def step(buf, base, k, start, emit, scale=1.0):
        pl.when(meta[1] > 0)(lambda: sweep(buf, base, k, start, emit, scale))

    def sweep(buf, base, k, start, emit, scale):
        rows, climbs = {}, {}

        def row(r):
            if r not in rows:
                rows[r] = [buf[base + c, r] for c in range(3)]
            return rows[r]

        def climb(r):
            if r not in climbs:
                climbs[r] = [x - y for x, y in zip(row(r + 1), row(r))]
            return climbs[r]

        for r in range(start, BAND):
            u = row(r)
            west = [x - pltpu.roll(x, 1, 1) for x in u]
            east = [pltpu.roll(x, 127, 1) - x for x in u]
            across = vv[2 * k, r] + (scale * kappa) * u[0]
            along = vv[2 * k + 1, r] + (scale * swing) * u[1]
            emit(r, u, slope(west, east, climb(r - 1), climb(r), across, along, scale))

    def put(buf, at, r, value):
        if r == HALO - 1:
            value = jnp.where(outside, 0.0, value)
        buf[at, r] = value
        if r == BAND - 1:
            buf[at, BAND] = pltpu.roll(value, HALF, 1)

    for k in range(GROUP):
        for a in range(5):
            at = [(4 * j + k) * 5 + a for j in range(8)]
            own = swap8([cur[i] for i in at])
            before = swap8([jnp.where(even, other[i], mate[i]) for i in at])
            after = swap8([jnp.where(even, mate[i], other[i]) for i in at])
            for y in range(8):
                rows = (
                    (y, jnp.where(low, before[y], after[7 - y])),
                    (y + 8, pltpu.roll(jnp.where(low, after[7 - y], before[y]), HALF, 1)),
                    (y + 16, jnp.where(low, own[y], own[7 - y])),
                )
                for r, value in rows:
                    if a == 3:
                        vv[2 * k, r] = time_step * value
                        if k == GROUP - 1:
                            vv[2 * GROUP, r] = coarsest * value
                    elif a == 4:
                        vv[2 * k + 1, r] = (time_step * sign) * value
                        if k == GROUP - 1:
                            vv[2 * GROUP + 1, r] = (coarsest * sign) * value
                    elif k == GROUP - 1:
                        value = pltpu.roll(value, 1, 0)
                        put(ua, a, r, value)
                        put(xa, a, r, value)
                        xb[a, r] = value
                        init[a, r] = value
                    else:
                        put(ua, 3 * (k + 1) + a, r, value)

    def keep_g(r, u, s):
        for c in range(3):
            gg[c, r] = u[c] + s[c]

    step(ua, 0, GROUP, 7, keep_g, float(FINE * GROUP))

    def fine(k, carry):
        base = 3 * k

        def opening(r, u, s):
            for c in range(3):
                put(ub, base + c, r, u[c] + s[c])
                src[base + c, r] = u[c] + float(FINE) * s[c]

        def onward(buf):
            def emit(r, u, s):
                for c in range(3):
                    put(buf, base + c, r, u[c] + s[c])

            return emit

        def closing(r, u, s):
            for c in range(3):
                end = u[c] + s[c]
                put(ua, base + c, r, end)
                src[base + c, r] = end - src[base + c, r]

        step(ua, base, k, 1, opening)
        step(ub, base, k, 2, onward(ua))
        step(ua, base, k, 3, onward(ub))
        step(ub, base, k, 4, closing)
        return carry

    lax.fori_loop(0, GROUP, fine, 0)

    def plus(buf, k, base):
        def emit(r, u, s):
            for c in range(3):
                put(buf, base + c, r, u[c] + float(FINE) * s[c] + src[3 * k + c, r])

        return emit

    step(ua, 0, 1, 5, plus(ub, 1, 0))
    step(ub, 0, 2, 6, plus(ua, 2, 0))

    def forcing(r, u, s):
        for c in range(3):
            ff[c, r] = u[c] + float(FINE) * s[c] + src[3 * (GROUP - 1) + c, r] - gg[c, r]

    step(ua, 0, GROUP - 1, 7, forcing)

    for t in range(GROUPS):
        buf, to = (xa, xb) if t % 2 == 0 else (xb, xa)

        def settle(r, u, s):
            for c in range(3):
                y = u[c] + s[c] + ff[c, r]
                if t == GROUPS - 1 and r >= HALO:
                    yy[c, r] = y
                put(to, c, r, jnp.where(sub == 0, init[c, r], pltpu.roll(y, 1, 0)))

        step(buf, 0, GROUP, max(7, 6 + t), settle, float(FINE * GROUP))

    step(xa, 0, 0, 14, plus(cc, 0, 0))
    step(cc, 0, 1, 15, plus(cc, 1, 3))
    step(cc, 3, 2, 16, plus(cc, 2, 6))

    group = lane // TILE
    for k, (buf, base) in enumerate([(xa, 0), (cc, 0), (cc, 3), (cc, 6)]):
        for q in range(FINE):
            sides = []
            for r, at in ((23 - FINE - q, HALF + HALO), (16 + q, HALO)):
                parts = [pltpu.roll(buf[base + c, r], (TILE * c - at) % 128, 1) for c in range(3)]
                sides.append(jnp.where(group == 0, parts[0], jnp.where(group == 1, parts[1], parts[2])))
            up, down = sides
            to_mate[k * FINE + q] = jnp.where(even, up, down)
            to_other[k * FINE + q] = jnp.where(even, down, up)
    for c in range(2):
        for q in range(FINE):
            down, up = flow[c * ROWS + q], flow[(c + 1) * ROWS - FINE + q]
            to_mate[(GROUP + c) * FINE + q] = jnp.where(even, up, down)
            to_other[(GROUP + c) * FINE + q] = jnp.where(even, down, up)


def pack_kernel(xa, cc, yy, out):
    lane = lanes()
    low = lane < HALF

    def compact(buf, base, c, y):
        m = jnp.where(low, buf[base + c, y + 16], buf[base + c, 23 - y])
        return jnp.where(lane < TILE, pltpu.roll(m, 128 - HALO, 1), pltpu.roll(m, 128 - HALO - TILE, 1))

    reads = [(xa, 0), (cc, 0), (cc, 3), (cc, 6), (yy, 0)]
    for c in range(3):
        before = [compact(*reads[0], c, y) for y in range(8)]
        for k in range(GROUP):
            own = [compact(*reads[k + 1], c, y) for y in range(8)]
            values = [jnp.where(low, x, pltpu.roll(y, HALF, 1)) for x, y in zip(own, before)]
            for j, value in enumerate(swap8(values)):
                out[(4 * j + k) * 3 + c] = value
            before = own


def edge_kernel(meta, tiles, mate, other, out):
    even = meta[0] % 2 == 0
    for i in range(GROUP * GROUPS):
        for c in range(3):
            out[4 * i + c] = tiles[3 * i + c]
    for k in range(GROUP):
        below, above = [], []
        for q in range(FINE):
            m, o = mate[k * FINE + q], other[k * FINE + q]
            below.append(jnp.where(even, o, m))
            above.append(jnp.where(even, m, o))
        for j, value in enumerate(swap8(below + above)):
            out[4 * (4 * j + k) + 3] = value


def gathered(tiles, block, b, part):
    group = lanes() // TILE
    value = None
    for q in range(4):
        shift = (TILE * (q - part)) % 128
        x = tiles[(4 * b + q) * 4 + block]
        x = pltpu.roll(x, shift, 1) if shift else x
        value = x if value is None else jnp.where(group == q, x, value)
    return value


def relax_kernel(meta, tiles, flow, mate, other, own_hbm, out_hbm, own, out, wa, wb, vv, sems):
    for c in range(3):
        for b in range(8):
            at = slice(128 * b, 128 * b + 128)
            own[c, 0:8, at] = gathered(tiles, c, b, 0)
            own[c, 8:16, at] = gathered(tiles, c, b, 1)
    first = pltpu.make_async_copy(own, own_hbm, sems.at[0])
    first.start()

    lane = lanes()
    tall = ROWS + 2 * FINE
    kappa = time_step * kappa_coupling
    even = meta[0] % 2 == 0
    for c in range(3):
        edges = swap8([gathered(tiles, 3, b, c) for b in range(8)])
        rows = edges[:FINE]
        for part in (2, 3):
            rows += swap8([gathered(tiles, c, b, part) for b in range(8)])
        for r, value in enumerate(rows + edges[FINE:]):
            wa[c * tall + r] = value
    for c in range(2):
        for r in range(FINE):
            m, o = mate[(GROUP + c) * FINE + r], other[(GROUP + c) * FINE + r]
            vv[c * tall + r] = time_step * jnp.where(even, o, m)
            vv[c * tall + FINE + ROWS + r] = time_step * jnp.where(even, m, o)
        for r in range(ROWS):
            vv[c * tall + FINE + r] = time_step * flow[c * ROWS + r]

    bottom, top = meta[0] == 0, meta[0] == meta[1] - 1
    def sweep(section, buf, to):
        rows = {r: [buf[c * tall + r] for c in range(3)] for r in range(section, tall - section)}
        climbs = {r: [x - y for x, y in zip(rows[r + 1], rows[r])] for r in range(section, tall - section - 1)}
        ends = []
        for r in range(section + 1, tall - section - 1):
            u = rows[r]
            west, east = [], []
            for x in u:
                y = pltpu.roll(x, 1, 1)
                west.append(x - jnp.where(lane == 0, pltpu.roll(y, 1, 0), y))
                y = pltpu.roll(x, 127, 1)
                east.append(jnp.where(lane == 127, pltpu.roll(y, 7, 0), y) - x)
            across = vv[r] + kappa * u[0]
            along = vv[tall + r] + kappa * u[1]
            s = slope(west, east, climbs[r - 1], climbs[r], across, along)
            new = [x + y for x, y in zip(u, s)]
            ends.append(new)
            for c in range(3):
                if r == FINE - 1:
                    new[c] = jnp.where(bottom, 0.0, new[c])
                elif r == FINE + ROWS:
                    new[c] = jnp.where(top, 0.0, new[c])
                if section < FINE - 1:
                    to[c * tall + r] = new[c]
        if section == FINE - 1:
            for y0 in (0, 8):
                for c in range(3):
                    for b, value in enumerate(swap8([ends[y0 + y][c] for y in range(8)])):
                        out[c, y0 : y0 + 8, 128 * b : 128 * b + 128] = value

    for section in range(FINE):
        buf, to = (wa, wb) if section % 2 == 0 else (wb, wa)
        sweep(section, buf, to)
    second = pltpu.make_async_copy(out, out_hbm, sems.at[1])
    second.start()
    first.wait()
    second.wait()


def f32(*shape):
    return jax.ShapeDtypeStruct(shape, jnp.float32)


def buffer(*shape):
    return pltpu.VMEM(shape, jnp.float32)


def call(kernel, n_scalars, n_arrays, outs, scratch=(), space=VMEM, to=VMEM, mib=24):
    many = isinstance(outs, tuple)
    return pl.pallas_call(
        kernel,
        out_shape=outs,
        in_specs=[SMEM] * n_scalars + [space] * n_arrays,
        out_specs=(to,) * len(outs) if many else to,
        scratch_shapes=list(scratch),
        compiler_params=pltpu.CompilerParams(vmem_limit_bytes=mib * 1024 * 1024),
    )


def cut(meta, init, ends, vel):
    state, flow = buffer(3, ROWS, 1024), buffer(2, ROWS, 1024)
    scratch = [state, state, flow, pltpu.SemaphoreType.DMA((3,))]
    outs = (f32(160, 8, 128), f32(2 * ROWS, 8, 128))
    return call(cut_kernel, 1, 3, outs, scratch, HBM, VMEM, 60)(meta, init, ends, vel)


def cycle(meta, mate, cur, other, flow):
    tall = BAND + 1
    edge = f32((GROUP + 2) * FINE, 8, 128)
    outs = (f32(3, tall, 8, 128), f32(9, tall, 8, 128), f32(3, BAND, 8, 128), edge, edge)
    scratch = [
        buffer(12, tall, 8, 128),
        buffer(12, tall, 8, 128),
        buffer(10, BAND, 8, 128),
        buffer(12, BAND, 8, 128),
        buffer(3, BAND, 8, 128),
        buffer(3, BAND, 8, 128),
        buffer(3, tall, 8, 128),
        buffer(3, tall, 8, 128),
    ]
    return call(cycle_kernel, 1, 4, outs, scratch)(meta, mate, cur, other, flow)


def pack(xa, cc, yy):
    return call(pack_kernel, 0, 3, f32(96, 8, 128))(xa, cc, yy)


def edge(meta, tiles, mate, other):
    return call(edge_kernel, 1, 3, f32(128, 8, 128))(meta, tiles, mate, other)


def relax(meta, tiles, flow, mate, other):
    tall = ROWS + 2 * FINE
    whole = f32(3, ROWS, 1024)
    scratch = [
        buffer(3, ROWS, 1024),
        buffer(3, ROWS, 1024),
        buffer(3 * tall, 8, 128),
        buffer(3 * tall, 8, 128),
        buffer(2 * tall, 8, 128),
        pltpu.SemaphoreType.DMA((2,)),
    ]
    return call(relax_kernel, 1, 4, (whole, whole), scratch, VMEM, HBM)(meta, tiles, flow, mate, other)


def per_device(initial_state, guessed_ends, velocity):
    slabs = lax.axis_size("gy")
    mates = [(i, i ^ 1) for i in range(slabs)]
    others = [(i, i + 1 if i % 2 else i - 1) for i in range(1, slabs - 1)]
    intervals = lax.axis_size("tm")
    here = lax.axis_index("tm").astype(jnp.int32).reshape(1)
    slab = jnp.stack([lax.axis_index("gy").astype(jnp.int32), jnp.int32(slabs)])

    windows, flow = cut(here, initial_state, guessed_ends[0], velocity[0])
    cur = lax.all_to_all(windows.reshape(intervals, 40, 128), "tm", 0, 0)
    cur = cur.reshape(intervals * 5, 8, 128)
    mate = lax.ppermute(cur, "gy", mates)
    other = lax.ppermute(cur, "gy", others)
    xa, cc, yy, to_mate, to_other = cycle(slab, mate, cur, other, flow)
    mate = lax.ppermute(to_mate, "gy", mates)
    other = lax.ppermute(to_other, "gy", others)
    tiles = pack(xa, cc, yy)
    tiles = edge(slab, tiles, mate, other)
    tiles = lax.all_to_all(tiles.reshape(intervals, 32, 128), "tm", 0, 0)
    own, relaxed = relax(slab, tiles.reshape(intervals * 4, 8, 128), flow, mate, other)
    return own[None], relaxed[None]


def solution(mesh):
    placed = (P(None, "gy", None), P("tm", None, "gy", None), P("tm", None, "gy", None))
    return jax.shard_map(
        per_device,
        mesh=mesh,
        in_specs=placed,
        out_specs=(P("tm", None, "gy", None), P("tm", None, "gy", None)),
        check_vma=False,
    )
```

```python
import functools

import jax
import jax.numpy as jnp
from jax import lax
from jax.experimental import pallas as pl
from jax.experimental.pallas import tpu as pltpu
from jax.sharding import PartitionSpec as P

FINE = 4
GROUP = 4
GROUPS = 8
HALO = 16
TILE = 32
ROWS = 16
HALF = 64
BAND = 24

diffusion = (0.05, 0.15, 0.4)
kappa_coupling = 0.1
time_step = 0.0125
coarsest = FINE * GROUP * time_step

VMEM = pl.BlockSpec(memory_space=pltpu.VMEM)
HBM = pl.BlockSpec(memory_space=pltpu.HBM)
SMEM = pl.BlockSpec(memory_space=pltpu.SMEM)


def lanes():
    return lax.broadcasted_iota(jnp.int32, (8, 128), 1)


def sublanes():
    return lax.broadcasted_iota(jnp.int32, (8, 128), 0)


def swap8(values):
    sub = sublanes()
    for s in (4, 2, 1):
        keep = sub % (2 * s) < s
        new = list(values)
        for p in range(8):
            if p % (2 * s) < s:
                a, b = values[p], values[p + s]
                new[p] = jnp.where(keep, a, pltpu.roll(b, s, 0))
                new[p + s] = jnp.where(keep, pltpu.roll(a, 8 - s, 0), b)
        values = new
    return values


def slope(west, east, below, above, across, along, scale=1.0):
    right, upward = across > 0.0, along > 0.0
    out = []
    for c in range(3):
        spread = (east[c] - west[c]) + (above[c] - below[c])
        transport = across * jnp.where(right, west[c], east[c]) + along * jnp.where(upward, below[c], above[c])
        out.append((scale * time_step * diffusion[c]) * spread - transport)
    return out


def cut_kernel(meta, init_hbm, ends_hbm, vel_hbm, out, flow, init, ends, vel, sems):
    copies = [
        pltpu.make_async_copy(far, near, sems.at[i])
        for i, (far, near) in enumerate(((init_hbm, init), (ends_hbm, ends), (vel_hbm, vel)))
    ]
    for copy in copies:
        copy.start()
    for copy in copies:
        copy.wait()
    last = meta[0] == GROUP * GROUPS - 1
    low = lanes() < HALF
    for a in range(5):
        if a < 3:
            top = jnp.where(last, init[a, 0:8, :], ends[a, 0:8, :])
            bottom = jnp.where(last, init[a, 8:16, :], ends[a, 8:16, :])
        else:
            top, bottom = vel[a - 3, 0:8, :], vel[a - 3, 8:16, :]
        for q in range(4):
            upper = pltpu.roll(top, (HALO - TILE * q) % 1024, 1)
            lower = pltpu.roll(bottom, (HALO + HALF - TILE * q) % 1024, 1)
            for b in range(8):
                at = slice(128 * b, 128 * b + 128)
                out[(4 * b + q) * 5 + a] = jnp.where(low, upper[:, at], lower[:, at])
    for c in range(2):
        for y0 in (0, 8):
            blocks = [vel[c, y0 : y0 + 8, 128 * b : 128 * b + 128] for b in range(8)]
            for y, value in enumerate(swap8(blocks)):
                flow[c * ROWS + y0 + y] = value


def sort_kernel(cur, one, two):
    for k in range(GROUP):
        for a in range(5):
            values = swap8([cur[(4 * j + k) * 5 + a] for j in range(8)])
            to = k
            if a < 3:
                to = (k + 1) % GROUP
                if to == 0:
                    values = [pltpu.roll(value, 1, 0) for value in values]
            half = one if to < 2 else two
            for y in range(8):
                half[(to % 2 * 5 + a) * 8 + y] = values[y]


def masks(meta):
    low = lanes() < HALF
    sign = jnp.where(low, 1.0, -1.0)
    outside = jnp.where(low, meta[0], meta[1] - 1 - meta[0]) == 0
    return low, sign, outside


def putter(outside):
    def put(buf, at, r, value):
        if r == HALO - 1:
            value = jnp.where(outside, 0.0, value)
        buf[at, r] = value
        if r == BAND - 1:
            buf[at, BAND] = pltpu.roll(value, HALF, 1)

    return put


def stepper(meta, sign):
    kappa = time_step * kappa_coupling
    swing = kappa * sign

    def sweep(buf, base, flow, at, start, emit, scale):
        rows, climbs = {}, {}

        def row(r):
            if r not in rows:
                rows[r] = [buf[base + c, r] for c in range(3)]
            return rows[r]

        def climb(r):
            if r not in climbs:
                climbs[r] = [x - y for x, y in zip(row(r + 1), row(r))]
            return climbs[r]

        for r in range(start, BAND):
            u = row(r)
            west = [x - pltpu.roll(x, 1, 1) for x in u]
            east = [pltpu.roll(x, 127, 1) - x for x in u]
            across = flow[at, r] + (scale * kappa) * u[0]
            along = flow[at + 1, r] + (scale * swing) * u[1]
            emit(r, u, slope(west, east, climb(r - 1), climb(r), across, along, scale))

    def step(buf, base, flow, at, start, emit, scale=1.0):
        pl.when(meta[1] > 0)(lambda: sweep(buf, base, flow, at, start, emit, scale))

    return step


def fine_kernel(pair, meta, own, mate, other, vv, src, ua, *more):
    ub = more[-1]
    low, sign, outside = masks(meta)
    put, step = putter(outside), stepper(meta, sign)
    even = meta[0] % 2 == 0
    for k in range(2):
        for a in range(5):
            at = (k * 5 + a) * 8
            mine = [own[at + y] for y in range(8)]
            m = [mate[at + y] for y in range(8)]
            o = [other[at + y] for y in range(8)]
            before = [jnp.where(even, x, y) for x, y in zip(o, m)]
            after = [jnp.where(even, y, x) for x, y in zip(o, m)]
            for y in range(8):
                rows = (
                    (y, jnp.where(low, before[y], after[7 - y])),
                    (y + 8, pltpu.roll(jnp.where(low, after[7 - y], before[y]), HALF, 1)),
                    (y + 16, jnp.where(low, mine[y], mine[7 - y])),
                )
                for r, value in rows:
                    if a < 3:
                        put(ua, 3 * k + a, r, value)
                        if pair == 0 and k == 0:
                            put(more[0], a, r, value)
                        continue
                    way = 1.0 if a == 3 else sign
                    vv[2 * k + a - 3, r] = (time_step * way) * value
                    if pair == 1 and k == 1:
                        vv[4 + a - 3, r] = (coarsest * way) * value

    def fine(k, carry):
        base = 3 * k

        def opening(r, u, s):
            for c in range(3):
                put(ub, base + c, r, u[c] + s[c])
                src[base + c, r] = u[c] + float(FINE) * s[c]

        def onward(buf):
            def emit(r, u, s):
                for c in range(3):
                    put(buf, base + c, r, u[c] + s[c])

            return emit

        def closing(r, u, s):
            for c in range(3):
                end = u[c] + s[c]
                put(ua, base + c, r, end)
                src[base + c, r] = end - src[base + c, r]

        step(ua, base, vv, 2 * k, 1, opening)
        step(ub, base, vv, 2 * k, 2, onward(ua))
        step(ua, base, vv, 2 * k, 3, onward(ub))
        step(ub, base, vv, 2 * k, 4, closing)
        return carry

    lax.fori_loop(0, 2, fine, 0)


def coarse_kernel(meta, ends, vv0, src0, begin, vv1, src1, out, ua, ub, gg, ff, xa, xb, yy, cc):
    lane, sub = lanes(), sublanes()
    low, sign, outside = masks(meta)
    put, step = putter(outside), stepper(meta, sign)
    flows = [(vv0, 0), (vv0, 2), (vv1, 0), (vv1, 2)]
    wide = (vv1, 4)
    srcs = [(src0, 0), (src0, 3), (src1, 0), (src1, 3)]

    def keep_g(r, u, s):
        for c in range(3):
            gg[c, r] = u[c] + s[c]

    step(begin, 0, *wide, 7, keep_g, float(FINE * GROUP))

    def plus(buf, k, base):
        src, at = srcs[k]

        def emit(r, u, s):
            for c in range(3):
                put(buf, base + c, r, u[c] + float(FINE) * s[c] + src[at + c, r])

        return emit

    step(ends, 0, *flows[1], 5, plus(ub, 1, 0))
    step(ub, 0, *flows[2], 6, plus(ua, 2, 0))

    def forcing(r, u, s):
        for c in range(3):
            ff[c, r] = u[c] + float(FINE) * s[c] + src1[3 + c, r] - gg[c, r]

    step(ua, 0, *flows[3], 7, forcing)

    for c in range(3):
        xb[c, 6] = begin[c, 6]
    for t in range(GROUPS):
        buf, to = (xa if t else begin, xb) if t % 2 == 0 else (xb, xa)

        def settle(r, u, s):
            for c in range(3):
                y = u[c] + s[c] + ff[c, r]
                if t == GROUPS - 1 and r >= HALO:
                    yy[c, r] = y
                put(to, c, r, jnp.where(sub == 0, begin[c, r], pltpu.roll(y, 1, 0)))

        step(buf, 0, *wide, max(7, 6 + t), settle, float(FINE * GROUP))

    step(xa, 0, *flows[0], 14, plus(cc, 0, 0))
    step(cc, 0, *flows[1], 15, plus(cc, 1, 3))
    step(cc, 3, *flows[2], 16, plus(cc, 2, 6))

    def compact(buf, base, c, y):
        m = jnp.where(low, buf[base + c, y + 16], buf[base + c, 23 - y])
        return jnp.where(lane < TILE, pltpu.roll(m, 128 - HALO, 1), pltpu.roll(m, 128 - HALO - TILE, 1))

    reads = [(xa, 0), (cc, 0), (cc, 3), (cc, 6), (yy, 0)]
    for c in range(3):
        before = [compact(*reads[0], c, y) for y in range(8)]
        for k in range(GROUP):
            own = [compact(*reads[k + 1], c, y) for y in range(8)]
            values = [jnp.where(low, x, pltpu.roll(y, HALF, 1)) for x, y in zip(own, before)]
            for j, value in enumerate(swap8(values)):
                out[(4 * j + k) * 3 + c] = value
            before = own


def gathered(tiles, c, b, part):
    group = lanes() // TILE
    value = None
    for q in range(4):
        shift = (TILE * (q - part)) % 128
        x = tiles[(4 * b + q) * 3 + c]
        x = pltpu.roll(x, shift, 1) if shift else x
        value = x if value is None else jnp.where(group == q, x, value)
    return value


def begin_kernel(meta, tiles, flow, begin, mate, other):
    even = meta[0] % 2 == 0
    for c in range(5):
        if c < 3:
            rows = []
            for part in (2, 3):
                rows += swap8([gathered(tiles, c, b, part) for b in range(8)])
            for y in range(ROWS):
                begin[c * ROWS + y] = rows[y]
        else:
            rows = [flow[(c - 3) * ROWS + y] for y in range(ROWS)]
        for y in range(FINE):
            down, up = rows[y], rows[ROWS - FINE + y]
            mate[c * FINE + y] = jnp.where(even, up, down)
            other[c * FINE + y] = jnp.where(even, down, up)


def own_kernel(tiles, own):
    for c in range(3):
        for b in range(8):
            at = slice(128 * b, 128 * b + 128)
            own[c, 0:8, at] = gathered(tiles, c, b, 0)
            own[c, 8:16, at] = gathered(tiles, c, b, 1)


def relax_kernel(meta, mid, flow, mate, other, out, wa, wb, vv):
    lane = lanes()
    tall = ROWS + 2 * FINE
    kappa = time_step * kappa_coupling
    even = meta[0] % 2 == 0
    for a in range(5):
        src, buf, at = (mid, wa, a) if a < 3 else (flow, vv, a - 3)
        scale = 1.0 if a < 3 else time_step
        for r in range(FINE):
            m, o = mate[a * FINE + r], other[a * FINE + r]
            buf[at * tall + r] = scale * jnp.where(even, o, m)
            buf[at * tall + FINE + ROWS + r] = scale * jnp.where(even, m, o)
        for r in range(ROWS):
            buf[at * tall + FINE + r] = scale * src[at * ROWS + r]

    bottom, top = meta[0] == 0, meta[0] == meta[1] - 1
    def sweep(section, buf, to):
        rows = {r: [buf[c * tall + r] for c in range(3)] for r in range(section, tall - section)}
        climbs = {r: [x - y for x, y in zip(rows[r + 1], rows[r])] for r in range(section, tall - section - 1)}
        ends = []
        for r in range(section + 1, tall - section - 1):
            u = rows[r]
            west, east = [], []
            for x in u:
                y = pltpu.roll(x, 1, 1)
                west.append(x - jnp.where(lane == 0, pltpu.roll(y, 1, 0), y))
                y = pltpu.roll(x, 127, 1)
                east.append(jnp.where(lane == 127, pltpu.roll(y, 7, 0), y) - x)
            across = vv[r] + kappa * u[0]
            along = vv[tall + r] + kappa * u[1]
            s = slope(west, east, climbs[r - 1], climbs[r], across, along)
            new = [x + y for x, y in zip(u, s)]
            ends.append(new)
            for c in range(3):
                if r == FINE - 1:
                    new[c] = jnp.where(bottom, 0.0, new[c])
                elif r == FINE + ROWS:
                    new[c] = jnp.where(top, 0.0, new[c])
                if section < FINE - 1:
                    to[c * tall + r] = new[c]
        if section == FINE - 1:
            for y0 in (0, 8):
                for c in range(3):
                    for b, value in enumerate(swap8([ends[y0 + y][c] for y in range(8)])):
                        out[c, y0 : y0 + 8, 128 * b : 128 * b + 128] = value

    for section in range(FINE):
        buf, to = (wa, wb) if section % 2 == 0 else (wb, wa)
        sweep(section, buf, to)


def f32(*shape):
    return jax.ShapeDtypeStruct(shape, jnp.float32)


def buffer(*shape):
    return pltpu.VMEM(shape, jnp.float32)


def call(kernel, n_scalars, n_arrays, outs, scratch=(), space=VMEM, mib=24):
    many = isinstance(outs, tuple)
    return pl.pallas_call(
        kernel,
        out_shape=outs,
        in_specs=[SMEM] * n_scalars + [space] * n_arrays,
        out_specs=(VMEM,) * len(outs) if many else VMEM,
        scratch_shapes=list(scratch),
        compiler_params=pltpu.CompilerParams(vmem_limit_bytes=mib * 1024 * 1024),
    )


def cut(meta, init, ends, vel):
    state, flow = buffer(3, ROWS, 1024), buffer(2, ROWS, 1024)
    scratch = [state, state, flow, pltpu.SemaphoreType.DMA((3,))]
    outs = (f32(160, 8, 128), f32(2 * ROWS, 8, 128))
    return call(cut_kernel, 1, 3, outs, scratch, HBM, 60)(meta, init, ends, vel)


def sort(cur):
    return call(sort_kernel, 0, 1, (f32(80, 8, 128), f32(80, 8, 128)))(cur)


def fine(pair, meta, own, mate, other):
    tall = BAND + 1
    outs = [f32(4 + 2 * pair, BAND, 8, 128), f32(6, BAND, 8, 128)]
    scratch = [buffer(6, tall, 8, 128)]
    if pair == 0:
        outs += [f32(6, tall, 8, 128), f32(3, tall, 8, 128)]
    else:
        scratch *= 2
    kernel = functools.partial(fine_kernel, pair)
    return call(kernel, 1, 3, tuple(outs), scratch)(meta, own, mate, other)


def coarse(meta, *arrays):
    tall = BAND + 1
    scratch = [
        buffer(3, tall, 8, 128),
        buffer(3, tall, 8, 128),
        buffer(3, BAND, 8, 128),
        buffer(3, BAND, 8, 128),
        buffer(3, tall, 8, 128),
        buffer(3, tall, 8, 128),
        buffer(3, BAND, 8, 128),
        buffer(9, tall, 8, 128),
    ]
    return call(coarse_kernel, 1, 6, f32(96, 8, 128), scratch)(meta, *arrays)


def begins(meta, tiles, flow):
    halo = f32(5 * FINE, 8, 128)
    return call(begin_kernel, 1, 2, (f32(3 * ROWS, 8, 128), halo, halo))(meta, tiles, flow)


def owns(tiles):
    return call(own_kernel, 0, 1, f32(3, ROWS, 1024))(tiles)


def relax(meta, mid, flow, mate, other):
    tall = ROWS + 2 * FINE
    scratch = [buffer(3 * tall, 8, 128), buffer(3 * tall, 8, 128), buffer(2 * tall, 8, 128)]
    return call(relax_kernel, 1, 4, f32(3, ROWS, 1024), scratch)(meta, mid, flow, mate, other)


def per_device(initial_state, guessed_ends, velocity):
    slabs = lax.axis_size("gy")
    mates = [(i, i ^ 1) for i in range(slabs)]
    others = [(i, i + 1 if i % 2 else i - 1) for i in range(1, slabs - 1)]
    intervals = lax.axis_size("tm")
    here = lax.axis_index("tm").astype(jnp.int32).reshape(1)
    slab = jnp.stack([lax.axis_index("gy").astype(jnp.int32), jnp.int32(slabs)])

    windows, flow = cut(here, initial_state, guessed_ends[0], velocity[0])
    cur = lax.all_to_all(windows.reshape(intervals, 40, 128), "tm", 0, 0)
    cur = cur.reshape(intervals * 5, 8, 128)
    one, two = sort(cur)
    mate_two = lax.ppermute(two, "gy", mates)
    mate_one = lax.ppermute(one, "gy", mates)
    other_two = lax.ppermute(two, "gy", others)
    other_one = lax.ppermute(one, "gy", others)
    vv0, src0, ends, begin = fine(0, slab, one, mate_one, other_one)
    vv1, src1 = fine(1, slab, two, mate_two, other_two)
    tiles = coarse(slab, ends, vv0, src0, begin, vv1, src1)
    tiles = lax.all_to_all(tiles.reshape(intervals, 24, 128), "tm", 0, 0)
    tiles = tiles.reshape(intervals * 3, 8, 128)
    mid, mate, other = begins(slab, tiles, flow)
    mate = lax.ppermute(mate, "gy", mates)
    other = lax.ppermute(other, "gy", others)
    own = owns(tiles)
    relaxed = relax(slab, mid, flow, mate, other)
    return own[None], relaxed[None]


def solution(mesh):
    placed = (P(None, "gy", None), P("tm", None, "gy", None), P("tm", None, "gy", None))
    return jax.shard_map(
        per_device,
        mesh=mesh,
        in_specs=placed,
        out_specs=(P("tm", None, "gy", None), P("tm", None, "gy", None)),
        check_vma=False,
    )
```

```python
import jax
import jax.numpy as jnp
from jax import lax
from jax.experimental import pallas as pl
from jax.experimental.pallas import tpu as pltpu
from jax.sharding import PartitionSpec as P

FINE = 4
GROUP = 4
GROUPS = 8
HALO = 16
TILE = 32
ROWS = 16
HALF = 64
BAND = 24

diffusion = (0.05, 0.15, 0.4)
kappa_coupling = 0.1
time_step = 0.0125
coarsest = FINE * GROUP * time_step

VMEM = pl.BlockSpec(memory_space=pltpu.VMEM)
HBM = pl.BlockSpec(memory_space=pltpu.HBM)
SMEM = pl.BlockSpec(memory_space=pltpu.SMEM)


def lanes():
    return lax.broadcasted_iota(jnp.int32, (8, 128), 1)


def sublanes():
    return lax.broadcasted_iota(jnp.int32, (8, 128), 0)


def swap8(values):
    sub = sublanes()
    for s in (4, 2, 1):
        keep = sub % (2 * s) < s
        new = list(values)
        for p in range(8):
            if p % (2 * s) < s:
                a, b = values[p], values[p + s]
                new[p] = jnp.where(keep, a, pltpu.roll(b, s, 0))
                new[p + s] = jnp.where(keep, pltpu.roll(a, 8 - s, 0), b)
        values = new
    return values


def slope(west, east, below, above, across, along, scale=1.0):
    right, upward = across > 0.0, along > 0.0
    out = []
    for c in range(3):
        spread = (east[c] - west[c]) + (above[c] - below[c])
        transport = across * jnp.where(right, west[c], east[c]) + along * jnp.where(upward, below[c], above[c])
        out.append((scale * time_step * diffusion[c]) * spread - transport)
    return out


def cut_kernel(meta, init_hbm, ends_hbm, vel_hbm, out, flow, init, ends, vel, sems):
    copies = [
        pltpu.make_async_copy(far, near, sems.at[i])
        for i, (far, near) in enumerate(((init_hbm, init), (ends_hbm, ends), (vel_hbm, vel)))
    ]
    for copy in copies:
        copy.start()
    for copy in copies:
        copy.wait()
    last = meta[0] == GROUP * GROUPS - 1
    low = lanes() < HALF
    for a in range(5):
        if a < 3:
            top = jnp.where(last, init[a, 0:8, :], ends[a, 0:8, :])
            bottom = jnp.where(last, init[a, 8:16, :], ends[a, 8:16, :])
        else:
            top, bottom = vel[a - 3, 0:8, :], vel[a - 3, 8:16, :]
        for q in range(4):
            upper = pltpu.roll(top, (HALO - TILE * q) % 1024, 1)
            lower = pltpu.roll(bottom, (HALO + HALF - TILE * q) % 1024, 1)
            for b in range(8):
                at = slice(128 * b, 128 * b + 128)
                out[(4 * b + q) * 5 + a] = jnp.where(low, upper[:, at], lower[:, at])
    for c in range(2):
        for y0 in (0, 8):
            blocks = [vel[c, y0 : y0 + 8, 128 * b : 128 * b + 128] for b in range(8)]
            for y, value in enumerate(swap8(blocks)):
                flow[c * ROWS + y0 + y] = value


def fold(own, out, parity):
    sub, near = sublanes(), lanes() // HALF == parity
    for m in range(10):
        tails = []
        for h in range(2):
            at = (2 * m + h) * 8
            x = [jnp.where(parity == 0, own[at + z], own[at + 7 - z]) for z in range(8)]
            for z in range(5):
                value = x[z]
                if 0 < z < 4:
                    both = jnp.where(sub <= 7 - z, value, pltpu.roll(x[8 - z], 8 - z, 0))
                    value = jnp.where(near, value, both)
                out[13 * m + 5 * h + z] = value
            tails.append(x[5:])
        for z in range(3):
            out[13 * m + 10 + z] = jnp.where(near, tails[0][z], pltpu.roll(tails[1][z], HALF, 1))


def unfold(folded, at):
    x = [folded[13 * (at // 2) + 5 * (at % 2) + z] for z in range(5)]
    tail = [folded[13 * (at // 2) + 10 + z] for z in range(3)]
    near = x + ([pltpu.roll(t, HALF, 1) for t in tail] if at % 2 else tail)
    far = x + [pltpu.roll(x[8 - z], 8 - z, 0) for z in range(5, 8)]
    return near, far


def sort_kernel(meta, cur, own, to_other, to_mate):
    for k in range(GROUP):
        for a in range(5):
            values = swap8([cur[(4 * j + k) * 5 + a] for j in range(8)])
            to = k
            if a < 3:
                to = (k + 1) % GROUP
                if to == 0:
                    values = [pltpu.roll(value, 1, 0) for value in values]
            for y in range(8):
                own[(to * 5 + a) * 8 + y] = values[y]
    parity = meta[0] % 2
    fold(own, to_other, parity)
    fold(own, to_mate, 1 - parity)


def cycle_kernel(meta, other, cur, mate, out, ua, ub, vv, src, gg, ff, init, xa, xb, yy, cc):
    lane, sub = lanes(), sublanes()
    low = lane < HALF
    sign = jnp.where(low, 1.0, -1.0)
    kappa = time_step * kappa_coupling
    swing = kappa * sign
    here = lane // HALF == meta[0] % 2
    outside = jnp.where(low, meta[0], meta[1] - 1 - meta[0]) == 0

    def step(buf, base, k, start, emit, scale=1.0):
        pl.when(meta[1] > 0)(lambda: sweep(buf, base, k, start, emit, scale))

    def sweep(buf, base, k, start, emit, scale):
        rows, climbs = {}, {}

        def row(r):
            if r not in rows:
                rows[r] = [buf[base + c, r] for c in range(3)]
            return rows[r]

        def climb(r):
            if r not in climbs:
                climbs[r] = [x - y for x, y in zip(row(r + 1), row(r))]
            return climbs[r]

        for r in range(start, BAND):
            u = row(r)
            west = [x - pltpu.roll(x, 1, 1) for x in u]
            east = [pltpu.roll(x, 127, 1) - x for x in u]
            across = vv[2 * k, r] + (scale * kappa) * u[0]
            along = vv[2 * k + 1, r] + (scale * swing) * u[1]
            emit(r, u, slope(west, east, climb(r - 1), climb(r), across, along, scale))

    def put(buf, at, r, value):
        if r == HALO - 1:
            value = jnp.where(outside, 0.0, value)
        buf[at, r] = value
        if r == BAND - 1:
            buf[at, BAND] = pltpu.roll(value, HALF, 1)

    for k in range(GROUP):
        for a in range(5):
            at = k * 5 + a
            mine = [cur[at * 8 + y] for y in range(8)]
            near, far = unfold(other, at)
            mate_near, mate_far = unfold(mate, at)
            for y in range(8):
                rows = (
                    (y, jnp.where(here, far[7 - y], mate_far[7 - y])),
                    (y + 8, pltpu.roll(jnp.where(here, mate_near[7 - y], near[7 - y]), HALF, 1)),
                    (y + 16, jnp.where(low, mine[y], mine[7 - y])),
                )
                for r, value in rows:
                    if a == 3:
                        vv[2 * k, r] = time_step * value
                        if k == GROUP - 1:
                            vv[2 * GROUP, r] = coarsest * value
                    elif a == 4:
                        vv[2 * k + 1, r] = (time_step * sign) * value
                        if k == GROUP - 1:
                            vv[2 * GROUP + 1, r] = (coarsest * sign) * value
                    else:
                        put(ua, 3 * k + a, r, value)
                        if k == 0:
                            put(xa, a, r, value)
                            xb[a, r] = value
                            init[a, r] = value

    def keep_g(r, u, s):
        for c in range(3):
            gg[c, r] = u[c] + s[c]

    step(ua, 0, GROUP, 7, keep_g, float(FINE * GROUP))

    def fine(k, carry):
        base = 3 * k

        def opening(r, u, s):
            for c in range(3):
                put(ub, base + c, r, u[c] + s[c])
                src[base + c, r] = u[c] + float(FINE) * s[c]

        def onward(buf):
            def emit(r, u, s):
                for c in range(3):
                    put(buf, base + c, r, u[c] + s[c])

            return emit

        def closing(r, u, s):
            for c in range(3):
                end = u[c] + s[c]
                put(ua, base + c, r, end)
                src[base + c, r] = end - src[base + c, r]

        step(ua, base, k, 1, opening)
        step(ub, base, k, 2, onward(ua))
        step(ua, base, k, 3, onward(ub))
        step(ub, base, k, 4, closing)
        return carry

    lax.fori_loop(0, GROUP, fine, 0)

    def plus(buf, k, base):
        def emit(r, u, s):
            for c in range(3):
                put(buf, base + c, r, u[c] + float(FINE) * s[c] + src[3 * k + c, r])

        return emit

    step(ua, 0, 1, 5, plus(ub, 1, 0))
    step(ub, 0, 2, 6, plus(ua, 2, 0))

    def forcing(r, u, s):
        for c in range(3):
            ff[c, r] = u[c] + float(FINE) * s[c] + src[3 * (GROUP - 1) + c, r] - gg[c, r]

    step(ua, 0, GROUP - 1, 7, forcing)

    for t in range(GROUPS):
        buf, to = (xa, xb) if t % 2 == 0 else (xb, xa)

        def settle(r, u, s):
            for c in range(3):
                y = u[c] + s[c] + ff[c, r]
                if t == GROUPS - 1 and r >= HALO:
                    yy[c, r] = y
                put(to, c, r, jnp.where(sub == 0, init[c, r], pltpu.roll(y, 1, 0)))

        step(buf, 0, GROUP, max(7, 6 + t), settle, float(FINE * GROUP))

    step(xa, 0, 0, 14, plus(cc, 0, 0))
    step(cc, 0, 1, 15, plus(cc, 1, 3))
    step(cc, 3, 2, 16, plus(cc, 2, 6))

    def compact(buf, base, c, y):
        m = jnp.where(low, buf[base + c, y + 16], buf[base + c, 23 - y])
        return jnp.where(lane < TILE, pltpu.roll(m, 128 - HALO, 1), pltpu.roll(m, 128 - HALO - TILE, 1))

    reads = [(xa, 0), (cc, 0), (cc, 3), (cc, 6), (yy, 0)]
    for c in range(3):
        before = [compact(*reads[0], c, y) for y in range(8)]
        for k in range(GROUP):
            own = [compact(*reads[k + 1], c, y) for y in range(8)]
            values = [jnp.where(low, x, pltpu.roll(y, HALF, 1)) for x, y in zip(own, before)]
            for j, value in enumerate(swap8(values)):
                out[(4 * j + k) * 3 + c] = value
            before = own


def gathered(tiles, c, b, part):
    group = lanes() // TILE
    value = None
    for q in range(4):
        shift = (TILE * (q - part)) % 128
        x = tiles[(4 * b + q) * 3 + c]
        x = pltpu.roll(x, shift, 1) if shift else x
        value = x if value is None else jnp.where(group == q, x, value)
    return value


def begin_kernel(meta, tiles, flow, begin, mate, other):
    even = meta[0] % 2 == 0
    for c in range(5):
        if c < 3:
            rows = []
            for part in (2, 3):
                rows += swap8([gathered(tiles, c, b, part) for b in range(8)])
            for y in range(ROWS):
                begin[c * ROWS + y] = rows[y]
        else:
            rows = [flow[(c - 3) * ROWS + y] for y in range(ROWS)]
        for y in range(FINE):
            down, up = rows[y], rows[ROWS - FINE + y]
            mate[c * FINE + y] = jnp.where(even, up, down)
            other[c * FINE + y] = jnp.where(even, down, up)


def own_kernel(tiles, own):
    for c in range(3):
        for b in range(8):
            at = slice(128 * b, 128 * b + 128)
            own[c, 0:8, at] = gathered(tiles, c, b, 0)
            own[c, 8:16, at] = gathered(tiles, c, b, 1)


def relax_kernel(meta, mid, flow, mate, other, out, wa, wb, vv):
    lane = lanes()
    tall = ROWS + 2 * FINE
    kappa = time_step * kappa_coupling
    even = meta[0] % 2 == 0
    for a in range(5):
        src, buf, at = (mid, wa, a) if a < 3 else (flow, vv, a - 3)
        scale = 1.0 if a < 3 else time_step
        for r in range(FINE):
            m, o = mate[a * FINE + r], other[a * FINE + r]
            buf[at * tall + r] = scale * jnp.where(even, o, m)
            buf[at * tall + FINE + ROWS + r] = scale * jnp.where(even, m, o)
        for r in range(ROWS):
            buf[at * tall + FINE + r] = scale * src[at * ROWS + r]

    bottom, top = meta[0] == 0, meta[0] == meta[1] - 1
    def sweep(section, buf, to):
        rows = {r: [buf[c * tall + r] for c in range(3)] for r in range(section, tall - section)}
        climbs = {r: [x - y for x, y in zip(rows[r + 1], rows[r])] for r in range(section, tall - section - 1)}
        ends = []
        for r in range(section + 1, tall - section - 1):
            u = rows[r]
            west, east = [], []
            for x in u:
                y = pltpu.roll(x, 1, 1)
                west.append(x - jnp.where(lane == 0, pltpu.roll(y, 1, 0), y))
                y = pltpu.roll(x, 127, 1)
                east.append(jnp.where(lane == 127, pltpu.roll(y, 7, 0), y) - x)
            across = vv[r] + kappa * u[0]
            along = vv[tall + r] + kappa * u[1]
            s = slope(west, east, climbs[r - 1], climbs[r], across, along)
            new = [x + y for x, y in zip(u, s)]
            ends.append(new)
            for c in range(3):
                if r == FINE - 1:
                    new[c] = jnp.where(bottom, 0.0, new[c])
                elif r == FINE + ROWS:
                    new[c] = jnp.where(top, 0.0, new[c])
                if section < FINE - 1:
                    to[c * tall + r] = new[c]
        if section == FINE - 1:
            for y0 in (0, 8):
                for c in range(3):
                    for b, value in enumerate(swap8([ends[y0 + y][c] for y in range(8)])):
                        out[c, y0 : y0 + 8, 128 * b : 128 * b + 128] = value

    for section in range(FINE):
        buf, to = (wa, wb) if section % 2 == 0 else (wb, wa)
        sweep(section, buf, to)


def f32(*shape):
    return jax.ShapeDtypeStruct(shape, jnp.float32)


def buffer(*shape):
    return pltpu.VMEM(shape, jnp.float32)


def call(kernel, n_scalars, n_arrays, outs, scratch=(), space=VMEM, mib=24):
    many = isinstance(outs, tuple)
    return pl.pallas_call(
        kernel,
        out_shape=outs,
        in_specs=[SMEM] * n_scalars + [space] * n_arrays,
        out_specs=(VMEM,) * len(outs) if many else VMEM,
        scratch_shapes=list(scratch),
        compiler_params=pltpu.CompilerParams(vmem_limit_bytes=mib * 1024 * 1024),
    )


def cut(meta, init, ends, vel):
    state, flow = buffer(3, ROWS, 1024), buffer(2, ROWS, 1024)
    scratch = [state, state, flow, pltpu.SemaphoreType.DMA((3,))]
    outs = (f32(160, 8, 128), f32(2 * ROWS, 8, 128))
    return call(cut_kernel, 1, 3, outs, scratch, HBM, 60)(meta, init, ends, vel)


def sort(meta, cur):
    return call(sort_kernel, 1, 1, (f32(160, 8, 128), f32(130, 8, 128), f32(130, 8, 128)))(meta, cur)


def cycle(meta, mate, cur, other):
    tall = BAND + 1
    scratch = [
        buffer(12, tall, 8, 128),
        buffer(12, tall, 8, 128),
        buffer(10, BAND, 8, 128),
        buffer(12, BAND, 8, 128),
        buffer(3, BAND, 8, 128),
        buffer(3, BAND, 8, 128),
        buffer(3, tall, 8, 128),
        buffer(3, tall, 8, 128),
        buffer(3, tall, 8, 128),
        buffer(3, BAND, 8, 128),
        buffer(9, tall, 8, 128),
    ]
    return call(cycle_kernel, 1, 3, f32(96, 8, 128), scratch)(meta, other, cur, mate)


def begins(meta, tiles, flow):
    halo = f32(5 * FINE, 8, 128)
    return call(begin_kernel, 1, 2, (f32(3 * ROWS, 8, 128), halo, halo))(meta, tiles, flow)


def owns(tiles):
    return call(own_kernel, 0, 1, f32(3, ROWS, 1024))(tiles)


def relax(meta, mid, flow, mate, other):
    tall = ROWS + 2 * FINE
    scratch = [buffer(3 * tall, 8, 128), buffer(3 * tall, 8, 128), buffer(2 * tall, 8, 128)]
    return call(relax_kernel, 1, 4, f32(3, ROWS, 1024), scratch)(meta, mid, flow, mate, other)


def per_device(initial_state, guessed_ends, velocity):
    slabs = lax.axis_size("gy")
    mates = [(i, i ^ 1) for i in range(slabs)]
    others = [(i, i + 1 if i % 2 else i - 1) for i in range(1, slabs - 1)]
    intervals = lax.axis_size("tm")
    here = lax.axis_index("tm").astype(jnp.int32).reshape(1)
    slab = jnp.stack([lax.axis_index("gy").astype(jnp.int32), jnp.int32(slabs)])

    windows, flow = cut(here, initial_state, guessed_ends[0], velocity[0])
    cur = lax.all_to_all(windows.reshape(intervals, 40, 128), "tm", 0, 0)
    cur = cur.reshape(intervals * 5, 8, 128)
    cur, to_other, to_mate = sort(slab, cur)
    other = lax.ppermute(to_other, "gy", others)
    mate = lax.ppermute(to_mate, "gy", mates)
    tiles = cycle(slab, mate, cur, other)
    tiles = lax.all_to_all(tiles.reshape(intervals, 24, 128), "tm", 0, 0)
    tiles = tiles.reshape(intervals * 3, 8, 128)
    mid, mate, other = begins(slab, tiles, flow)
    mate = lax.ppermute(mate, "gy", mates)
    other = lax.ppermute(other, "gy", others)
    own = owns(tiles)
    relaxed = relax(slab, mid, flow, mate, other)
    return own[None], relaxed[None]


def solution(mesh):
    placed = (P(None, "gy", None), P("tm", None, "gy", None), P("tm", None, "gy", None))
    return jax.shard_map(
        per_device,
        mesh=mesh,
        in_specs=placed,
        out_specs=(P("tm", None, "gy", None), P("tm", None, "gy", None)),
        check_vma=False,
    )
```

```python
import jax
import jax.numpy as jnp
from jax import lax
from jax.experimental import pallas as pl
from jax.experimental.pallas import tpu as pltpu
from jax.sharding import PartitionSpec as P

FINE = 4
GROUP = 4
GROUPS = 8
HALO = 16
TILE = 32
ROWS = 16
HALF = 64
BAND = 24

diffusion = (0.05, 0.15, 0.4)
kappa_coupling = 0.1
time_step = 0.0125
coarsest = FINE * GROUP * time_step

VMEM = pl.BlockSpec(memory_space=pltpu.VMEM)
HBM = pl.BlockSpec(memory_space=pltpu.HBM)


def slab():
    return lax.axis_index("gy")


def slabs():
    return lax.axis_size("gy")


def lanes():
    return lax.broadcasted_iota(jnp.int32, (8, 128), 1)


def sublanes():
    return lax.broadcasted_iota(jnp.int32, (8, 128), 0)


def swap8(values):
    sub = sublanes()
    for s in (4, 2, 1):
        keep = sub % (2 * s) < s
        new = list(values)
        for p in range(8):
            if p % (2 * s) < s:
                a, b = values[p], values[p + s]
                new[p] = jnp.where(keep, a, pltpu.roll(b, s, 0))
                new[p + s] = jnp.where(keep, pltpu.roll(a, 8 - s, 0), b)
        values = new
    return values


def slope(west, east, below, above, across, along, scale=1.0):
    right, upward = across > 0.0, along > 0.0
    out = []
    for c in range(3):
        spread = (east[c] - west[c]) + (above[c] - below[c])
        transport = across * jnp.where(right, west[c], east[c]) + along * jnp.where(upward, below[c], above[c])
        out.append((scale * time_step * diffusion[c]) * spread - transport)
    return out


def cut_kernel(init_hbm, ends_hbm, vel_hbm, out, flow, init, ends, vel, sems):
    copies = [
        pltpu.make_async_copy(far, near, sems.at[i])
        for i, (far, near) in enumerate(((init_hbm, init), (ends_hbm, ends), (vel_hbm, vel)))
    ]
    for copy in copies:
        copy.start()
    for copy in copies:
        copy.wait()
    last = lax.axis_index("tm") == GROUP * GROUPS - 1
    low = lanes() < HALF
    for a in range(5):
        if a < 3:
            top = jnp.where(last, init[a, 0:8, :], ends[a, 0:8, :])
            bottom = jnp.where(last, init[a, 8:16, :], ends[a, 8:16, :])
        else:
            top, bottom = vel[a - 3, 0:8, :], vel[a - 3, 8:16, :]
        for q in range(4):
            upper = pltpu.roll(top, (HALO - TILE * q) % 1024, 1)
            lower = pltpu.roll(bottom, (HALO + HALF - TILE * q) % 1024, 1)
            for b in range(8):
                at = slice(128 * b, 128 * b + 128)
                out[(4 * b + q) * 5 + a] = jnp.where(low, upper[:, at], lower[:, at])
    for c in range(2):
        for y0 in (0, 8):
            blocks = [vel[c, y0 : y0 + 8, 128 * b : 128 * b + 128] for b in range(8)]
            for y, value in enumerate(swap8(blocks)):
                flow[c * ROWS + y0 + y] = value


def fold(own, out, parity):
    sub, near = sublanes(), lanes() // HALF == parity
    for m in range(10):
        tails = []
        for h in range(2):
            at = (2 * m + h) * 8
            x = [jnp.where(parity == 0, own[at + z], own[at + 7 - z]) for z in range(8)]
            for z in range(5):
                value = x[z]
                if 0 < z < 4:
                    both = jnp.where(sub <= 7 - z, value, pltpu.roll(x[8 - z], 8 - z, 0))
                    value = jnp.where(near, value, both)
                out[13 * m + 5 * h + z] = value
            tails.append(x[5:])
        for z in range(3):
            out[13 * m + 10 + z] = jnp.where(near, tails[0][z], pltpu.roll(tails[1][z], HALF, 1))


def unfold(folded, at):
    x = [folded[13 * (at // 2) + 5 * (at % 2) + z] for z in range(5)]
    tail = [folded[13 * (at // 2) + 10 + z] for z in range(3)]
    near = x + ([pltpu.roll(t, HALF, 1) for t in tail] if at % 2 else tail)
    far = x + [pltpu.roll(x[8 - z], 8 - z, 0) for z in range(5, 8)]
    return near, far


def sort_kernel(cur, own, to_other, to_mate):
    for k in range(GROUP):
        for a in range(5):
            values = swap8([cur[(4 * j + k) * 5 + a] for j in range(8)])
            to = k
            if a < 3:
                to = (k + 1) % GROUP
                if to == 0:
                    values = [pltpu.roll(value, 1, 0) for value in values]
            for y in range(8):
                own[(to * 5 + a) * 8 + y] = values[y]
    parity = slab() % 2
    fold(own, to_other, parity)
    fold(own, to_mate, 1 - parity)


def cycle_kernel(other, cur, mate, out, ua, ub, vv, src, gg, ff, init, xa, xb, yy, cc):
    lane, sub = lanes(), sublanes()
    low = lane < HALF
    sign = jnp.where(low, 1.0, -1.0)
    kappa = time_step * kappa_coupling
    swing = kappa * sign
    here = lane // HALF == slab() % 2
    outside = jnp.where(low, slab(), slabs() - 1 - slab()) == 0

    def step(buf, base, k, start, emit, scale=1.0):
        pl.when(slab() >= 0)(lambda: sweep(buf, base, k, start, emit, scale))

    def sweep(buf, base, k, start, emit, scale):
        rows, climbs = {}, {}

        def row(r):
            if r not in rows:
                rows[r] = [buf[base + c, r] for c in range(3)]
            return rows[r]

        def climb(r):
            if r not in climbs:
                climbs[r] = [x - y for x, y in zip(row(r + 1), row(r))]
            return climbs[r]

        for r in range(start, BAND):
            u = row(r)
            west = [x - pltpu.roll(x, 1, 1) for x in u]
            east = [pltpu.roll(x, 127, 1) - x for x in u]
            across = vv[2 * k, r] + (scale * kappa) * u[0]
            along = vv[2 * k + 1, r] + (scale * swing) * u[1]
            emit(r, u, slope(west, east, climb(r - 1), climb(r), across, along, scale))

    def put(buf, at, r, value):
        if r == HALO - 1:
            value = jnp.where(outside, 0.0, value)
        buf[at, r] = value
        if r == BAND - 1:
            buf[at, BAND] = pltpu.roll(value, HALF, 1)

    for k in range(GROUP):
        for a in range(5):
            at = k * 5 + a
            mine = [cur[at * 8 + y] for y in range(8)]
            near, far = unfold(other, at)
            mate_near, mate_far = unfold(mate, at)
            for y in range(8):
                rows = (
                    (y, jnp.where(here, far[7 - y], mate_far[7 - y])),
                    (y + 8, pltpu.roll(jnp.where(here, mate_near[7 - y], near[7 - y]), HALF, 1)),
                    (y + 16, jnp.where(low, mine[y], mine[7 - y])),
                )
                for r, value in rows:
                    if a == 3:
                        vv[2 * k, r] = time_step * value
                        if k == GROUP - 1:
                            vv[2 * GROUP, r] = coarsest * value
                    elif a == 4:
                        vv[2 * k + 1, r] = (time_step * sign) * value
                        if k == GROUP - 1:
                            vv[2 * GROUP + 1, r] = (coarsest * sign) * value
                    else:
                        put(ua, 3 * k + a, r, value)
                        if k == 0:
                            put(xa, a, r, value)
                            xb[a, r] = value
                            init[a, r] = value

    def keep_g(r, u, s):
        for c in range(3):
            gg[c, r] = u[c] + s[c]

    step(ua, 0, GROUP, 7, keep_g, float(FINE * GROUP))

    def fine(k, carry):
        base = 3 * k

        def opening(r, u, s):
            for c in range(3):
                put(ub, base + c, r, u[c] + s[c])
                src[base + c, r] = u[c] + float(FINE) * s[c]

        def onward(buf):
            def emit(r, u, s):
                for c in range(3):
                    put(buf, base + c, r, u[c] + s[c])

            return emit

        def closing(r, u, s):
            for c in range(3):
                end = u[c] + s[c]
                put(ua, base + c, r, end)
                src[base + c, r] = end - src[base + c, r]

        step(ua, base, k, 1, opening)
        step(ub, base, k, 2, onward(ua))
        step(ua, base, k, 3, onward(ub))
        step(ub, base, k, 4, closing)
        return carry

    lax.fori_loop(0, GROUP, fine, 0)

    def plus(buf, k, base):
        def emit(r, u, s):
            for c in range(3):
                put(buf, base + c, r, u[c] + float(FINE) * s[c] + src[3 * k + c, r])

        return emit

    step(ua, 0, 1, 5, plus(ub, 1, 0))
    step(ub, 0, 2, 6, plus(ua, 2, 0))

    def forcing(r, u, s):
        for c in range(3):
            ff[c, r] = u[c] + float(FINE) * s[c] + src[3 * (GROUP - 1) + c, r] - gg[c, r]

    step(ua, 0, GROUP - 1, 7, forcing)

    for t in range(GROUPS):
        buf, to = (xa, xb) if t % 2 == 0 else (xb, xa)

        def settle(r, u, s):
            for c in range(3):
                y = u[c] + s[c] + ff[c, r]
                if t == GROUPS - 1 and r >= HALO:
                    yy[c, r] = y
                put(to, c, r, jnp.where(sub == 0, init[c, r], pltpu.roll(y, 1, 0)))

        step(buf, 0, GROUP, max(7, 6 + t), settle, float(FINE * GROUP))

    step(xa, 0, 0, 14, plus(cc, 0, 0))
    step(cc, 0, 1, 15, plus(cc, 1, 3))
    step(cc, 3, 2, 16, plus(cc, 2, 6))

    def compact(buf, base, c, y):
        m = jnp.where(low, buf[base + c, y + 16], buf[base + c, 23 - y])
        return jnp.where(lane < TILE, pltpu.roll(m, 128 - HALO, 1), pltpu.roll(m, 128 - HALO - TILE, 1))

    reads = [(xa, 0), (cc, 0), (cc, 3), (cc, 6), (yy, 0)]
    for c in range(3):
        before = [compact(*reads[0], c, y) for y in range(8)]
        for k in range(GROUP):
            own = [compact(*reads[k + 1], c, y) for y in range(8)]
            values = [jnp.where(low, x, pltpu.roll(y, HALF, 1)) for x, y in zip(own, before)]
            for j, value in enumerate(swap8(values)):
                out[(4 * j + k) * 3 + c] = value
            before = own


def gathered(tiles, c, b, part):
    group = lanes() // TILE
    value = None
    for q in range(4):
        shift = (TILE * (q - part)) % 128
        x = tiles[(4 * b + q) * 3 + c]
        x = pltpu.roll(x, shift, 1) if shift else x
        value = x if value is None else jnp.where(group == q, x, value)
    return value


def begin_kernel(tiles, flow, begin, mate, other):
    even = slab() % 2 == 0
    for c in range(5):
        if c < 3:
            rows = []
            for part in (2, 3):
                rows += swap8([gathered(tiles, c, b, part) for b in range(8)])
            for y in range(ROWS):
                begin[c * ROWS + y] = rows[y]
        else:
            rows = [flow[(c - 3) * ROWS + y] for y in range(ROWS)]
        for y in range(FINE):
            down, up = rows[y], rows[ROWS - FINE + y]
            mate[c * FINE + y] = jnp.where(even, up, down)
            other[c * FINE + y] = jnp.where(even, down, up)


def own_kernel(tiles, own):
    for c in range(3):
        for b in range(8):
            at = slice(128 * b, 128 * b + 128)
            own[c, 0:8, at] = gathered(tiles, c, b, 0)
            own[c, 8:16, at] = gathered(tiles, c, b, 1)


def relax_kernel(mid, flow, mate, other, out, wa, wb, vv):
    lane = lanes()
    tall = ROWS + 2 * FINE
    kappa = time_step * kappa_coupling
    even = slab() % 2 == 0
    for a in range(5):
        src, buf, at = (mid, wa, a) if a < 3 else (flow, vv, a - 3)
        scale = 1.0 if a < 3 else time_step
        for r in range(FINE):
            m, o = mate[a * FINE + r], other[a * FINE + r]
            buf[at * tall + r] = scale * jnp.where(even, o, m)
            buf[at * tall + FINE + ROWS + r] = scale * jnp.where(even, m, o)
        for r in range(ROWS):
            buf[at * tall + FINE + r] = scale * src[at * ROWS + r]

    bottom, top = slab() == 0, slab() == slabs() - 1
    def sweep(section, buf, to):
        rows = {r: [buf[c * tall + r] for c in range(3)] for r in range(section, tall - section)}
        climbs = {r: [x - y for x, y in zip(rows[r + 1], rows[r])] for r in range(section, tall - section - 1)}
        ends = []
        for r in range(section + 1, tall - section - 1):
            u = rows[r]
            west, east = [], []
            for x in u:
                y = pltpu.roll(x, 1, 1)
                west.append(x - jnp.where(lane == 0, pltpu.roll(y, 1, 0), y))
                y = pltpu.roll(x, 127, 1)
                east.append(jnp.where(lane == 127, pltpu.roll(y, 7, 0), y) - x)
            across = vv[r] + kappa * u[0]
            along = vv[tall + r] + kappa * u[1]
            s = slope(west, east, climbs[r - 1], climbs[r], across, along)
            new = [x + y for x, y in zip(u, s)]
            ends.append(new)
            for c in range(3):
                if r == FINE - 1:
                    new[c] = jnp.where(bottom, 0.0, new[c])
                elif r == FINE + ROWS:
                    new[c] = jnp.where(top, 0.0, new[c])
                if section < FINE - 1:
                    to[c * tall + r] = new[c]
        if section == FINE - 1:
            for y0 in (0, 8):
                for c in range(3):
                    for b, value in enumerate(swap8([ends[y0 + y][c] for y in range(8)])):
                        out[c, y0 : y0 + 8, 128 * b : 128 * b + 128] = value

    for section in range(FINE):
        buf, to = (wa, wb) if section % 2 == 0 else (wb, wa)
        sweep(section, buf, to)


def f32(*shape):
    return jax.ShapeDtypeStruct(shape, jnp.float32)


def buffer(*shape):
    return pltpu.VMEM(shape, jnp.float32)


def call(kernel, n_arrays, outs, scratch=(), space=VMEM, mib=24):
    many = isinstance(outs, tuple)
    return pl.pallas_call(
        kernel,
        out_shape=outs,
        in_specs=[space] * n_arrays,
        out_specs=(VMEM,) * len(outs) if many else VMEM,
        scratch_shapes=list(scratch),
        compiler_params=pltpu.CompilerParams(vmem_limit_bytes=mib * 1024 * 1024),
    )


def cut(init, ends, vel):
    state, flow = buffer(3, ROWS, 1024), buffer(2, ROWS, 1024)
    scratch = [state, state, flow, pltpu.SemaphoreType.DMA((3,))]
    outs = (f32(160, 8, 128), f32(2 * ROWS, 8, 128))
    return call(cut_kernel, 3, outs, scratch, HBM, 60)(init, ends, vel)


def sort(cur):
    return call(sort_kernel, 1, (f32(160, 8, 128), f32(130, 8, 128), f32(130, 8, 128)))(cur)


def cycle(mate, cur, other):
    tall = BAND + 1
    scratch = [
        buffer(12, tall, 8, 128),
        buffer(12, tall, 8, 128),
        buffer(10, BAND, 8, 128),
        buffer(12, BAND, 8, 128),
        buffer(3, BAND, 8, 128),
        buffer(3, BAND, 8, 128),
        buffer(3, tall, 8, 128),
        buffer(3, tall, 8, 128),
        buffer(3, tall, 8, 128),
        buffer(3, BAND, 8, 128),
        buffer(9, tall, 8, 128),
    ]
    return call(cycle_kernel, 3, f32(96, 8, 128), scratch)(other, cur, mate)


def begins(tiles, flow):
    halo = f32(5 * FINE, 8, 128)
    return call(begin_kernel, 2, (f32(3 * ROWS, 8, 128), halo, halo))(tiles, flow)


def owns(tiles):
    return call(own_kernel, 1, f32(3, ROWS, 1024))(tiles)


def relax(mid, flow, mate, other):
    tall = ROWS + 2 * FINE
    scratch = [buffer(3 * tall, 8, 128), buffer(3 * tall, 8, 128), buffer(2 * tall, 8, 128)]
    return call(relax_kernel, 4, f32(3, ROWS, 1024), scratch)(mid, flow, mate, other)


def per_device(initial_state, guessed_ends, velocity):
    slabs = lax.axis_size("gy")
    mates = [(i, i ^ 1) for i in range(slabs)]
    others = [(i, i + 1 if i % 2 else i - 1) for i in range(1, slabs - 1)]
    intervals = lax.axis_size("tm")

    windows, flow = cut(initial_state, guessed_ends[0], velocity[0])
    cur = lax.all_to_all(windows.reshape(intervals, 40, 128), "tm", 0, 0)
    cur = cur.reshape(intervals * 5, 8, 128)
    cur, to_other, to_mate = sort(cur)
    other = lax.ppermute(to_other, "gy", others)
    mate = lax.ppermute(to_mate, "gy", mates)
    tiles = cycle(mate, cur, other)
    tiles = lax.all_to_all(tiles.reshape(intervals, 24, 128), "tm", 0, 0)
    tiles = tiles.reshape(intervals * 3, 8, 128)
    mid, mate, other = begins(tiles, flow)
    mate = lax.ppermute(mate, "gy", mates)
    other = lax.ppermute(other, "gy", others)
    own = owns(tiles)
    relaxed = relax(mid, flow, mate, other)
    return own[None], relaxed[None]


def solution(mesh):
    placed = (P(None, "gy", None), P("tm", None, "gy", None), P("tm", None, "gy", None))
    return jax.shard_map(
        per_device,
        mesh=mesh,
        in_specs=placed,
        out_specs=(P("tm", None, "gy", None), P("tm", None, "gy", None)),
        check_vma=False,
    )
```

```python
import jax
import jax.numpy as jnp
from jax import lax
from jax.experimental import pallas as pl
from jax.experimental.pallas import tpu as pltpu
from jax.sharding import PartitionSpec as P

FINE = 4
GROUP = 4
GROUPS = 8
HALO = 16
TILE = 32
ROWS = 16
HALF = 64
BAND = 24

diffusion = (0.05, 0.15, 0.4)
kappa_coupling = 0.1
time_step = 0.0125
coarsest = FINE * GROUP * time_step

VMEM = pl.BlockSpec(memory_space=pltpu.VMEM)
HBM = pl.BlockSpec(memory_space=pltpu.HBM)


def slab():
    return lax.axis_index("gy")


def slabs():
    return lax.axis_size("gy")


def lanes():
    return lax.broadcasted_iota(jnp.int32, (8, 128), 1)


def sublanes():
    return lax.broadcasted_iota(jnp.int32, (8, 128), 0)


def swap8(values):
    sub = sublanes()
    for s in (4, 2, 1):
        keep = sub % (2 * s) < s
        new = list(values)
        for p in range(8):
            if p % (2 * s) < s:
                a, b = values[p], values[p + s]
                new[p] = jnp.where(keep, a, pltpu.roll(b, s, 0))
                new[p + s] = jnp.where(keep, pltpu.roll(a, 8 - s, 0), b)
        values = new
    return values


def slope(west, east, below, above, across, along, scale=1.0):
    right, upward = across > 0.0, along > 0.0
    out = []
    for c in range(3):
        spread = (east[c] - west[c]) + (above[c] - below[c])
        transport = across * jnp.where(right, west[c], east[c]) + along * jnp.where(upward, below[c], above[c])
        out.append((scale * time_step * diffusion[c]) * spread - transport)
    return out


def cut_kernel(init_hbm, ends_hbm, vel_hbm, out, flow, init, ends, vel, sems):
    copies = [
        pltpu.make_async_copy(far, near, sems.at[i])
        for i, (far, near) in enumerate(((init_hbm, init), (ends_hbm, ends), (vel_hbm, vel)))
    ]
    for copy in copies:
        copy.start()
    for copy in copies:
        copy.wait()
    last = lax.axis_index("tm") == GROUP * GROUPS - 1
    low = lanes() < HALF
    for a in range(5):
        if a < 3:
            top = jnp.where(last, init[a, 0:8, :], ends[a, 0:8, :])
            bottom = jnp.where(last, init[a, 8:16, :], ends[a, 8:16, :])
        else:
            top, bottom = vel[a - 3, 0:8, :], vel[a - 3, 8:16, :]
        for q in range(4):
            upper = pltpu.roll(top, (HALO - TILE * q) % 1024, 1)
            lower = pltpu.roll(bottom, (HALO + HALF - TILE * q) % 1024, 1)
            for b in range(8):
                at = slice(128 * b, 128 * b + 128)
                out[(4 * b + q) * 5 + a] = jnp.where(low, upper[:, at], lower[:, at])
    for c in range(2):
        for y0 in (0, 8):
            blocks = [vel[c, y0 : y0 + 8, 128 * b : 128 * b + 128] for b in range(8)]
            for y, value in enumerate(swap8(blocks)):
                flow[c * ROWS + y0 + y] = value


def fold(own, out, parity):
    sub, near = sublanes(), lanes() // HALF == parity
    for m in range(10):
        tails = []
        for h in range(2):
            at = (2 * m + h) * 8
            x = [jnp.where(parity == 0, own[at + z], own[at + 7 - z]) for z in range(8)]
            for z in range(5):
                value = x[z]
                if 0 < z < 4:
                    both = jnp.where(sub <= 7 - z, value, pltpu.roll(x[8 - z], 8 - z, 0))
                    value = jnp.where(near, value, both)
                out[13 * m + 5 * h + z] = value
            tails.append(x[5:])
        for z in range(3):
            out[13 * m + 10 + z] = jnp.where(near, tails[0][z], pltpu.roll(tails[1][z], HALF, 1))


def unfold(folded, at):
    x = [folded[13 * (at // 2) + 5 * (at % 2) + z] for z in range(5)]
    tail = [folded[13 * (at // 2) + 10 + z] for z in range(3)]
    near = x + ([pltpu.roll(t, HALF, 1) for t in tail] if at % 2 else tail)
    far = x + [pltpu.roll(x[8 - z], 8 - z, 0) for z in range(5, 8)]
    return near, far


def sort_kernel(cur, own, to_other, to_mate):
    for k in range(GROUP):
        for a in range(5):
            values = swap8([cur[(4 * j + k) * 5 + a] for j in range(8)])
            to = k
            if a < 3:
                to = (k + 1) % GROUP
                if to == 0:
                    values = [pltpu.roll(value, 1, 0) for value in values]
            for y in range(8):
                own[(to * 5 + a) * 8 + y] = values[y]
    parity = slab() % 2
    fold(own, to_other, parity)
    fold(own, to_mate, 1 - parity)


class Rows:
    def __init__(self, lower, upper, edge):
        self.lower, self.upper, self.edge = lower, upper, edge

    def __getitem__(self, at):
        i, r = at
        return self.upper[i, r - HALO] if r >= self.edge else self.lower[i, r]

    def __setitem__(self, at, value):
        i, r = at
        if r >= self.edge:
            self.upper[i, r - HALO] = value
        else:
            self.lower[i, r] = value


def tools():
    low = lanes() < HALF
    sign = jnp.where(low, 1.0, -1.0)
    kappa = time_step * kappa_coupling
    swing = kappa * sign
    outside = jnp.where(low, slab(), slabs() - 1 - slab()) == 0

    def step(*arguments):
        pl.when(slab() * slab() >= slab())(lambda: sweep(*arguments))

    def sweep(buf, base, flow, at, start, stop, emit, scale=1.0):
        rows, climbs = {}, {}

        def row(r):
            if r not in rows:
                rows[r] = [buf[base + c, r] for c in range(3)]
            return rows[r]

        def climb(r):
            if r not in climbs:
                climbs[r] = [x - y for x, y in zip(row(r + 1), row(r))]
            return climbs[r]

        for r in range(start, stop):
            u = row(r)
            west = [x - pltpu.roll(x, 1, 1) for x in u]
            east = [pltpu.roll(x, 127, 1) - x for x in u]
            across = flow[at, r] + (scale * kappa) * u[0]
            along = flow[at + 1, r] + (scale * swing) * u[1]
            emit(r, u, slope(west, east, climb(r - 1), climb(r), across, along, scale))

    def put(buf, at, r, value):
        if r == HALO - 1:
            value = jnp.where(outside, 0.0, value)
        buf[at, r] = value
        if r == BAND - 1:
            buf[at, BAND] = pltpu.roll(value, HALF, 1)

    return low, sign, step, put


def keep_flow(vv, k, a, r, value, sign):
    way = 1.0 if a == 3 else sign
    vv[2 * k + a - 3, r] = (time_step * way) * value
    if k == GROUP - 1:
        vv[2 * GROUP + a - 3, r] = (coarsest * way) * value


def fine_steps(states, vv, src_in, src, step, put, spans):
    def member(k, carry):
        base = 3 * k

        def opening(r, u, s):
            for c in range(3):
                put(states[1], base + c, r, u[c] + s[c])
                src_in[base + c, r] = u[c] + float(FINE) * s[c]

        def onward(buf):
            def emit(r, u, s):
                for c in range(3):
                    put(buf, base + c, r, u[c] + s[c])

            return emit

        def closing(r, u, s):
            for c in range(3):
                end = u[c] + s[c]
                put(states[4], base + c, r, end)
                src[base + c, r] = end - src_in[base + c, r]

        emits = (opening, onward(states[2]), onward(states[3]), closing)
        for i, (emit, span) in enumerate(zip(emits, spans)):
            step(states[i], base, vv, 2 * k, *span, emit)
        return carry

    lax.fori_loop(0, GROUP, member, 0)


def early_kernel(cur, e0, e1, e2, e3, e4, vv, src):
    low, sign, step, put = tools()
    states = [Rows(None, x, 0) for x in (e0, e1, e2, e3, e4)]
    vv, src = Rows(None, vv, 0), Rows(None, src, 0)
    for k in range(GROUP):
        for a in range(5):
            mine = [cur[(k * 5 + a) * 8 + y] for y in range(8)]
            for y in range(8):
                value = jnp.where(low, mine[y], mine[7 - y])
                if a < 3:
                    put(states[0], 3 * k + a, HALO + y, value)
                else:
                    keep_flow(vv, k, a, HALO + y, value, sign)
    fine_steps(states, vv, src, src, step, put, [(HALO + d, BAND) for d in range(1, 5)])


def cycle_kernel(other, mate, e0, e1, e2, e3, e4, ev, es, out, u0, u1, u2, u3, u4, lv, ls, gg, ff, ca, cb, xa, xb, yy, cc):
    low, sign, step, put = tools()
    lane, sub = lanes(), sublanes()
    here = lane // HALF == slab() % 2
    states = [Rows(u, e, HALO + d) for d, (u, e) in enumerate(zip((u0, u1, u2, u3, u4), (e0, e1, e2, e3, e4)))]
    vv = Rows(lv, ev, HALO)
    begin, ends, src = states[0], states[4], Rows(ls, es, HALO + 4)

    for k in range(GROUP):
        for a in range(5):
            near, far = unfold(other, k * 5 + a)
            mate_near, mate_far = unfold(mate, k * 5 + a)
            for y in range(8):
                rows = (
                    (y, jnp.where(here, far[7 - y], mate_far[7 - y])),
                    (y + 8, pltpu.roll(jnp.where(here, mate_near[7 - y], near[7 - y]), HALF, 1)),
                )
                for r, value in rows:
                    if a < 3:
                        put(begin, 3 * k + a, r, value)
                    else:
                        keep_flow(vv, k, a, r, value, sign)

    fine_steps(states, vv, Rows(ls, es, HALO + 1), src, step, put, [(d, HALO + d) for d in range(1, 5)])

    def keep_g(r, u, s):
        for c in range(3):
            gg[c, r] = u[c] + s[c]

    step(begin, 0, vv, 2 * GROUP, 7, BAND, keep_g, float(FINE * GROUP))

    def plus(buf, k, base):
        def emit(r, u, s):
            for c in range(3):
                put(buf, base + c, r, u[c] + float(FINE) * s[c] + src[3 * k + c, r])

        return emit

    step(ends, 0, vv, 2, 5, BAND, plus(cb, 1, 0))
    step(cb, 0, vv, 4, 6, BAND, plus(ca, 2, 0))

    def forcing(r, u, s):
        for c in range(3):
            ff[c, r] = u[c] + float(FINE) * s[c] + src[3 * (GROUP - 1) + c, r] - gg[c, r]

    step(ca, 0, vv, 2 * (GROUP - 1), 7, BAND, forcing)

    for c in range(3):
        xb[c, 6] = begin[c, 6]
    for t in range(GROUPS):
        buf, to = (xa if t else begin, xb) if t % 2 == 0 else (xb, xa)

        def settle(r, u, s):
            for c in range(3):
                y = u[c] + s[c] + ff[c, r]
                if t == GROUPS - 1 and r >= HALO:
                    yy[c, r] = y
                put(to, c, r, jnp.where(sub == 0, begin[c, r], pltpu.roll(y, 1, 0)))

        step(buf, 0, vv, 2 * GROUP, max(7, 6 + t), BAND, settle, float(FINE * GROUP))

    step(xa, 0, vv, 0, 14, BAND, plus(cc, 0, 0))
    step(cc, 0, vv, 2, 15, BAND, plus(cc, 1, 3))
    step(cc, 3, vv, 4, 16, BAND, plus(cc, 2, 6))

    def compact(buf, base, c, y):
        m = jnp.where(low, buf[base + c, y + 16], buf[base + c, 23 - y])
        return jnp.where(lane < TILE, pltpu.roll(m, 128 - HALO, 1), pltpu.roll(m, 128 - HALO - TILE, 1))

    reads = [(xa, 0), (cc, 0), (cc, 3), (cc, 6), (yy, 0)]
    for c in range(3):
        before = [compact(*reads[0], c, y) for y in range(8)]
        for k in range(GROUP):
            own = [compact(*reads[k + 1], c, y) for y in range(8)]
            values = [jnp.where(low, x, pltpu.roll(y, HALF, 1)) for x, y in zip(own, before)]
            for j, value in enumerate(swap8(values)):
                out[(4 * j + k) * 3 + c] = value
            before = own


def gathered(tiles, c, b, part):
    group = lanes() // TILE
    value = None
    for q in range(4):
        shift = (TILE * (q - part)) % 128
        x = tiles[(4 * b + q) * 3 + c]
        x = pltpu.roll(x, shift, 1) if shift else x
        value = x if value is None else jnp.where(group == q, x, value)
    return value


def begin_kernel(tiles, flow, begin, mate, other):
    even = slab() % 2 == 0
    for c in range(5):
        if c < 3:
            rows = []
            for part in (2, 3):
                rows += swap8([gathered(tiles, c, b, part) for b in range(8)])
            for y in range(ROWS):
                begin[c * ROWS + y] = rows[y]
        else:
            rows = [flow[(c - 3) * ROWS + y] for y in range(ROWS)]
        for y in range(FINE):
            down, up = rows[y], rows[ROWS - FINE + y]
            mate[c * FINE + y] = jnp.where(even, up, down)
            other[c * FINE + y] = jnp.where(even, down, up)


def own_kernel(tiles, own):
    for c in range(3):
        for b in range(8):
            at = slice(128 * b, 128 * b + 128)
            own[c, 0:8, at] = gathered(tiles, c, b, 0)
            own[c, 8:16, at] = gathered(tiles, c, b, 1)


def relax_kernel(mid, flow, mate, other, out, wa, wb, vv):
    lane = lanes()
    tall = ROWS + 2 * FINE
    kappa = time_step * kappa_coupling
    even = slab() % 2 == 0
    for a in range(5):
        src, buf, at = (mid, wa, a) if a < 3 else (flow, vv, a - 3)
        scale = 1.0 if a < 3 else time_step
        for r in range(FINE):
            m, o = mate[a * FINE + r], other[a * FINE + r]
            buf[at * tall + r] = scale * jnp.where(even, o, m)
            buf[at * tall + FINE + ROWS + r] = scale * jnp.where(even, m, o)
        for r in range(ROWS):
            buf[at * tall + FINE + r] = scale * src[at * ROWS + r]

    bottom, top = slab() == 0, slab() == slabs() - 1
    def sweep(section, buf, to):
        rows = {r: [buf[c * tall + r] for c in range(3)] for r in range(section, tall - section)}
        climbs = {r: [x - y for x, y in zip(rows[r + 1], rows[r])] for r in range(section, tall - section - 1)}
        ends = []
        for r in range(section + 1, tall - section - 1):
            u = rows[r]
            west, east = [], []
            for x in u:
                y = pltpu.roll(x, 1, 1)
                west.append(x - jnp.where(lane == 0, pltpu.roll(y, 1, 0), y))
                y = pltpu.roll(x, 127, 1)
                east.append(jnp.where(lane == 127, pltpu.roll(y, 7, 0), y) - x)
            across = vv[r] + kappa * u[0]
            along = vv[tall + r] + kappa * u[1]
            s = slope(west, east, climbs[r - 1], climbs[r], across, along)
            new = [x + y for x, y in zip(u, s)]
            ends.append(new)
            for c in range(3):
                if r == FINE - 1:
                    new[c] = jnp.where(bottom, 0.0, new[c])
                elif r == FINE + ROWS:
                    new[c] = jnp.where(top, 0.0, new[c])
                if section < FINE - 1:
                    to[c * tall + r] = new[c]
        if section == FINE - 1:
            for y0 in (0, 8):
                for c in range(3):
                    for b, value in enumerate(swap8([ends[y0 + y][c] for y in range(8)])):
                        out[c, y0 : y0 + 8, 128 * b : 128 * b + 128] = value

    for section in range(FINE):
        buf, to = (wa, wb) if section % 2 == 0 else (wb, wa)
        sweep(section, buf, to)


def f32(*shape):
    return jax.ShapeDtypeStruct(shape, jnp.float32)


def buffer(*shape):
    return pltpu.VMEM(shape, jnp.float32)


def call(kernel, n_arrays, outs, scratch=(), space=VMEM, mib=24):
    many = isinstance(outs, tuple)
    return pl.pallas_call(
        kernel,
        out_shape=outs,
        in_specs=[space] * n_arrays,
        out_specs=(VMEM,) * len(outs) if many else VMEM,
        scratch_shapes=list(scratch),
        compiler_params=pltpu.CompilerParams(vmem_limit_bytes=mib * 1024 * 1024),
    )


def cut(init, ends, vel):
    state, flow = buffer(3, ROWS, 1024), buffer(2, ROWS, 1024)
    scratch = [state, state, flow, pltpu.SemaphoreType.DMA((3,))]
    outs = (f32(160, 8, 128), f32(2 * ROWS, 8, 128))
    return call(cut_kernel, 3, outs, scratch, HBM, 60)(init, ends, vel)


def sort(cur):
    return call(sort_kernel, 1, (f32(160, 8, 128), f32(130, 8, 128), f32(130, 8, 128)))(cur)


def early(cur):
    top, flat = f32(12, 9, 8, 128), f32(12, 8, 8, 128)
    return call(early_kernel, 1, (top, top, top, top, top, f32(10, 8, 8, 128), flat))(cur)


def cycle(other, mate, *upper):
    tall = BAND + 1
    scratch = [buffer(12, HALO + d, 8, 128) for d in range(5)]
    scratch += [
        buffer(10, HALO, 8, 128),
        buffer(12, HALO + 4, 8, 128),
        buffer(3, BAND, 8, 128),
        buffer(3, BAND, 8, 128),
        buffer(3, tall, 8, 128),
        buffer(3, tall, 8, 128),
        buffer(3, tall, 8, 128),
        buffer(3, tall, 8, 128),
        buffer(3, BAND, 8, 128),
        buffer(9, tall, 8, 128),
    ]
    return call(cycle_kernel, 9, f32(96, 8, 128), scratch)(other, mate, *upper)


def begins(tiles, flow):
    halo = f32(5 * FINE, 8, 128)
    return call(begin_kernel, 2, (f32(3 * ROWS, 8, 128), halo, halo))(tiles, flow)


def owns(tiles):
    return call(own_kernel, 1, f32(3, ROWS, 1024))(tiles)


def relax(mid, flow, mate, other):
    tall = ROWS + 2 * FINE
    scratch = [buffer(3 * tall, 8, 128), buffer(3 * tall, 8, 128), buffer(2 * tall, 8, 128)]
    return call(relax_kernel, 4, f32(3, ROWS, 1024), scratch)(mid, flow, mate, other)


def per_device(initial_state, guessed_ends, velocity):
    slabs = lax.axis_size("gy")
    mates = [(i, i ^ 1) for i in range(slabs)]
    others = [(i, i + 1 if i % 2 else i - 1) for i in range(1, slabs - 1)]
    intervals = lax.axis_size("tm")

    windows, flow = cut(initial_state, guessed_ends[0], velocity[0])
    cur = lax.all_to_all(windows.reshape(intervals, 40, 128), "tm", 0, 0)
    cur = cur.reshape(intervals * 5, 8, 128)
    cur, to_other, to_mate = sort(cur)
    other = lax.ppermute(to_other, "gy", others)
    mate = lax.ppermute(to_mate, "gy", mates)
    tiles = cycle(other, mate, *early(cur))
    tiles = lax.all_to_all(tiles.reshape(intervals, 24, 128), "tm", 0, 0)
    tiles = tiles.reshape(intervals * 3, 8, 128)
    mid, mate, other = begins(tiles, flow)
    mate = lax.ppermute(mate, "gy", mates)
    other = lax.ppermute(other, "gy", others)
    own = owns(tiles)
    relaxed = relax(mid, flow, mate, other)
    return own[None], relaxed[None]


def solution(mesh):
    placed = (P(None, "gy", None), P("tm", None, "gy", None), P("tm", None, "gy", None))
    return jax.shard_map(
        per_device,
        mesh=mesh,
        in_specs=placed,
        out_specs=(P("tm", None, "gy", None), P("tm", None, "gy", None)),
        check_vma=False,
    )
```

```python
import jax
import jax.numpy as jnp
from jax import lax
from jax.experimental import pallas as pl
from jax.experimental.pallas import tpu as pltpu
from jax.sharding import PartitionSpec as P

FINE = 4
GROUP = 4
GROUPS = 8
HALO = 16
TILE = 32
ROWS = 16
HALF = 64
BAND = 24

diffusion = (0.05, 0.15, 0.4)
kappa_coupling = 0.1
time_step = 0.0125
coarsest = FINE * GROUP * time_step

VMEM = pl.BlockSpec(memory_space=pltpu.VMEM)
HBM = pl.BlockSpec(memory_space=pltpu.HBM)


def slab():
    return lax.axis_index("gy")


def slabs():
    return lax.axis_size("gy")


def lanes():
    return lax.broadcasted_iota(jnp.int32, (8, 128), 1)


def sublanes():
    return lax.broadcasted_iota(jnp.int32, (8, 128), 0)


def swap8(values):
    sub = sublanes()
    for s in (4, 2, 1):
        keep = sub % (2 * s) < s
        new = list(values)
        for p in range(8):
            if p % (2 * s) < s:
                a, b = values[p], values[p + s]
                new[p] = jnp.where(keep, a, pltpu.roll(b, s, 0))
                new[p + s] = jnp.where(keep, pltpu.roll(a, 8 - s, 0), b)
        values = new
    return values


def slope(west, east, below, above, across, along, scale=1.0):
    right, upward = across > 0.0, along > 0.0
    out = []
    for c in range(3):
        spread = (east[c] - west[c]) + (above[c] - below[c])
        transport = across * jnp.where(right, west[c], east[c]) + along * jnp.where(upward, below[c], above[c])
        out.append((scale * time_step * diffusion[c]) * spread - transport)
    return out


def cut_kernel(init_hbm, ends_hbm, vel_hbm, out_hbm, flow_hbm, init, ends, vel, out, flow, arrive, leave):
    def fetch(far, near, i, at):
        copy = pltpu.make_async_copy(far.at[i], near.at[i], arrive.at[at])
        copy.start()
        return copy

    coming = {3 + c: [fetch(vel_hbm, vel, c, c)] for c in range(2)}
    for c in range(3):
        coming[c] = [fetch(ends_hbm, ends, c, 2 + c), fetch(init_hbm, init, c, 5 + c)]
    going = []
    last = lax.axis_index("tm") == GROUP * GROUPS - 1
    low = lanes() < HALF
    for a in (3, 4, 0, 1, 2):
        for copy in coming[a]:
            copy.wait()
        if a < 3:
            top = jnp.where(last, init[a, 0:8, :], ends[a, 0:8, :])
            bottom = jnp.where(last, init[a, 8:16, :], ends[a, 8:16, :])
        else:
            top, bottom = vel[a - 3, 0:8, :], vel[a - 3, 8:16, :]
        for q in range(4):
            upper = pltpu.roll(top, (HALO - TILE * q) % 1024, 1)
            lower = pltpu.roll(bottom, (HALO + HALF - TILE * q) % 1024, 1)
            for b in range(8):
                at = slice(128 * b, 128 * b + 128)
                out[a, 4 * b + q] = jnp.where(low, upper[:, at], lower[:, at])
        copy = pltpu.make_async_copy(out.at[a], out_hbm.at[:, a], leave.at[a])
        copy.start()
        going.append(copy)
        if a < 3:
            continue
        for y0 in (0, 8):
            blocks = [vel[a - 3, y0 : y0 + 8, 128 * b : 128 * b + 128] for b in range(8)]
            for y, value in enumerate(swap8(blocks)):
                flow[(a - 3) * ROWS + y0 + y] = value
        if a == 4:
            copy = pltpu.make_async_copy(flow, flow_hbm, leave.at[5])
            copy.start()
            going.append(copy)
    for copy in going:
        copy.wait()


def fold(own, out, parity):
    sub, near = sublanes(), lanes() // HALF == parity
    for m in range(10):
        tails = []
        for h in range(2):
            at = (2 * m + h) * 8
            x = [jnp.where(parity == 0, own[at + z], own[at + 7 - z]) for z in range(8)]
            for z in range(5):
                value = x[z]
                if 0 < z < 4:
                    both = jnp.where(sub <= 7 - z, value, pltpu.roll(x[8 - z], 8 - z, 0))
                    value = jnp.where(near, value, both)
                out[13 * m + 5 * h + z] = value
            tails.append(x[5:])
        for z in range(3):
            out[13 * m + 10 + z] = jnp.where(near, tails[0][z], pltpu.roll(tails[1][z], HALF, 1))


def unfold(folded, at):
    x = [folded[13 * (at // 2) + 5 * (at % 2) + z] for z in range(5)]
    tail = [folded[13 * (at // 2) + 10 + z] for z in range(3)]
    near = x + ([pltpu.roll(t, HALF, 1) for t in tail] if at % 2 else tail)
    far = x + [pltpu.roll(x[8 - z], 8 - z, 0) for z in range(5, 8)]
    return near, far


def sort_kernel(cur, own, to_other, to_mate):
    for k in range(GROUP):
        for a in range(5):
            values = swap8([cur[(4 * j + k) * 5 + a] for j in range(8)])
            to = k
            if a < 3:
                to = (k + 1) % GROUP
                if to == 0:
                    values = [pltpu.roll(value, 1, 0) for value in values]
            for y in range(8):
                own[(to * 5 + a) * 8 + y] = values[y]
    parity = slab() % 2
    fold(own, to_other, parity)
    fold(own, to_mate, 1 - parity)


class Rows:
    def __init__(self, lower, upper, edge):
        self.lower, self.upper, self.edge = lower, upper, edge

    def __getitem__(self, at):
        i, r = at
        return self.upper[i, r - HALO] if r >= self.edge else self.lower[i, r]

    def __setitem__(self, at, value):
        i, r = at
        if r >= self.edge:
            self.upper[i, r - HALO] = value
        else:
            self.lower[i, r] = value


def tools():
    low = lanes() < HALF
    sign = jnp.where(low, 1.0, -1.0)
    kappa = time_step * kappa_coupling
    swing = kappa * sign
    outside = jnp.where(low, slab(), slabs() - 1 - slab()) == 0

    def step(*arguments):
        pl.when(slab() * slab() >= slab())(lambda: sweep(*arguments))

    def sweep(buf, base, flow, at, start, stop, emit, scale=1.0):
        rows, climbs = {}, {}

        def row(r):
            if r not in rows:
                rows[r] = [buf[base + c, r] for c in range(3)]
            return rows[r]

        def climb(r):
            if r not in climbs:
                climbs[r] = [x - y for x, y in zip(row(r + 1), row(r))]
            return climbs[r]

        for r in range(start, stop):
            u = row(r)
            west = [x - pltpu.roll(x, 1, 1) for x in u]
            east = [pltpu.roll(x, 127, 1) - x for x in u]
            across = flow[at, r] + (scale * kappa) * u[0]
            along = flow[at + 1, r] + (scale * swing) * u[1]
            emit(r, u, slope(west, east, climb(r - 1), climb(r), across, along, scale))

    def put(buf, at, r, value):
        if r == HALO - 1:
            value = jnp.where(outside, 0.0, value)
        buf[at, r] = value
        if r == BAND - 1:
            buf[at, BAND] = pltpu.roll(value, HALF, 1)

    return low, sign, step, put


def keep_flow(vv, k, a, r, value, sign):
    way = 1.0 if a == 3 else sign
    vv[2 * k + a - 3, r] = (time_step * way) * value
    if k == GROUP - 1:
        vv[2 * GROUP + a - 3, r] = (coarsest * way) * value


def fine_steps(states, vv, src_in, src, step, put, spans):
    def member(k, carry):
        base = 3 * k

        def opening(r, u, s):
            for c in range(3):
                put(states[1], base + c, r, u[c] + s[c])
                src_in[base + c, r] = u[c] + float(FINE) * s[c]

        def onward(buf):
            def emit(r, u, s):
                for c in range(3):
                    put(buf, base + c, r, u[c] + s[c])

            return emit

        def closing(r, u, s):
            for c in range(3):
                end = u[c] + s[c]
                put(states[4], base + c, r, end)
                src[base + c, r] = end - src_in[base + c, r]

        emits = (opening, onward(states[2]), onward(states[3]), closing)
        for i, (emit, span) in enumerate(zip(emits, spans)):
            step(states[i], base, vv, 2 * k, *span, emit)
        return carry

    lax.fori_loop(0, GROUP, member, 0)


def early_kernel(cur, e0, e1, e2, e3, e4, vv, src):
    low, sign, step, put = tools()
    states = [Rows(None, x, 0) for x in (e0, e1, e2, e3, e4)]
    vv, src = Rows(None, vv, 0), Rows(None, src, 0)
    for k in range(GROUP):
        for a in range(5):
            mine = [cur[(k * 5 + a) * 8 + y] for y in range(8)]
            for y in range(8):
                value = jnp.where(low, mine[y], mine[7 - y])
                if a < 3:
                    put(states[0], 3 * k + a, HALO + y, value)
                else:
                    keep_flow(vv, k, a, HALO + y, value, sign)
    fine_steps(states, vv, src, src, step, put, [(HALO + d, BAND) for d in range(1, 5)])


def cycle_kernel(other, mate, e0, e1, e2, e3, e4, ev, es, out, u0, u1, u2, u3, u4, lv, ls, gg, ff, ca, cb, xa, xb, yy, cc):
    low, sign, step, put = tools()
    lane, sub = lanes(), sublanes()
    here = lane // HALF == slab() % 2
    states = [Rows(u, e, HALO + d) for d, (u, e) in enumerate(zip((u0, u1, u2, u3, u4), (e0, e1, e2, e3, e4)))]
    vv = Rows(lv, ev, HALO)
    begin, ends, src = states[0], states[4], Rows(ls, es, HALO + 4)

    for k in range(GROUP):
        for a in range(5):
            near, far = unfold(other, k * 5 + a)
            mate_near, mate_far = unfold(mate, k * 5 + a)
            for y in range(8):
                rows = (
                    (y, jnp.where(here, far[7 - y], mate_far[7 - y])),
                    (y + 8, pltpu.roll(jnp.where(here, mate_near[7 - y], near[7 - y]), HALF, 1)),
                )
                for r, value in rows:
                    if a < 3:
                        put(begin, 3 * k + a, r, value)
                    else:
                        keep_flow(vv, k, a, r, value, sign)

    fine_steps(states, vv, Rows(ls, es, HALO + 1), src, step, put, [(d, HALO + d) for d in range(1, 5)])

    def keep_g(r, u, s):
        for c in range(3):
            gg[c, r] = u[c] + s[c]

    step(begin, 0, vv, 2 * GROUP, 7, BAND, keep_g, float(FINE * GROUP))

    def plus(buf, k, base):
        def emit(r, u, s):
            for c in range(3):
                put(buf, base + c, r, u[c] + float(FINE) * s[c] + src[3 * k + c, r])

        return emit

    step(ends, 0, vv, 2, 5, BAND, plus(cb, 1, 0))
    step(cb, 0, vv, 4, 6, BAND, plus(ca, 2, 0))

    def forcing(r, u, s):
        for c in range(3):
            ff[c, r] = u[c] + float(FINE) * s[c] + src[3 * (GROUP - 1) + c, r] - gg[c, r]

    step(ca, 0, vv, 2 * (GROUP - 1), 7, BAND, forcing)

    for c in range(3):
        xb[c, 6] = begin[c, 6]
    for t in range(GROUPS):
        buf, to = (xa if t else begin, xb) if t % 2 == 0 else (xb, xa)

        def settle(r, u, s):
            for c in range(3):
                y = u[c] + s[c] + ff[c, r]
                if t == GROUPS - 1 and r >= HALO:
                    yy[c, r] = y
                put(to, c, r, jnp.where(sub == 0, begin[c, r], pltpu.roll(y, 1, 0)))

        step(buf, 0, vv, 2 * GROUP, max(7, 6 + t), BAND, settle, float(FINE * GROUP))

    step(xa, 0, vv, 0, 14, BAND, plus(cc, 0, 0))
    step(cc, 0, vv, 2, 15, BAND, plus(cc, 1, 3))
    step(cc, 3, vv, 4, 16, BAND, plus(cc, 2, 6))

    def compact(buf, base, c, y):
        m = jnp.where(low, buf[base + c, y + 16], buf[base + c, 23 - y])
        return jnp.where(lane < TILE, pltpu.roll(m, 128 - HALO, 1), pltpu.roll(m, 128 - HALO - TILE, 1))

    reads = [(xa, 0), (cc, 0), (cc, 3), (cc, 6), (yy, 0)]
    for c in range(3):
        before = [compact(*reads[0], c, y) for y in range(8)]
        for k in range(GROUP):
            own = [compact(*reads[k + 1], c, y) for y in range(8)]
            values = [jnp.where(low, x, pltpu.roll(y, HALF, 1)) for x, y in zip(own, before)]
            for j, value in enumerate(swap8(values)):
                out[(4 * j + k) * 3 + c] = value
            before = own


def gathered(tiles, c, b, part):
    group = lanes() // TILE
    value = None
    for q in range(4):
        shift = (TILE * (q - part)) % 128
        x = tiles[(4 * b + q) * 3 + c]
        x = pltpu.roll(x, shift, 1) if shift else x
        value = x if value is None else jnp.where(group == q, x, value)
    return value


def begin_kernel(tiles, flow, begin, mate, other):
    even = slab() % 2 == 0
    for c in range(5):
        if c < 3:
            rows = []
            for part in (2, 3):
                rows += swap8([gathered(tiles, c, b, part) for b in range(8)])
            for y in range(ROWS):
                begin[c * ROWS + y] = rows[y]
        else:
            rows = [flow[(c - 3) * ROWS + y] for y in range(ROWS)]
        for y in range(FINE):
            down, up = rows[y], rows[ROWS - FINE + y]
            mate[c * FINE + y] = jnp.where(even, up, down)
            other[c * FINE + y] = jnp.where(even, down, up)


def own_kernel(tiles, own):
    for c in range(3):
        for b in range(8):
            at = slice(128 * b, 128 * b + 128)
            own[c, 0:8, at] = gathered(tiles, c, b, 0)
            own[c, 8:16, at] = gathered(tiles, c, b, 1)


def relax_kernel(mid, flow, mate, other, out, wa, wb, vv):
    lane = lanes()
    tall = ROWS + 2 * FINE
    kappa = time_step * kappa_coupling
    even = slab() % 2 == 0
    for a in range(5):
        src, buf, at = (mid, wa, a) if a < 3 else (flow, vv, a - 3)
        scale = 1.0 if a < 3 else time_step
        for r in range(FINE):
            m, o = mate[a * FINE + r], other[a * FINE + r]
            buf[at * tall + r] = scale * jnp.where(even, o, m)
            buf[at * tall + FINE + ROWS + r] = scale * jnp.where(even, m, o)
        for r in range(ROWS):
            buf[at * tall + FINE + r] = scale * src[at * ROWS + r]

    bottom, top = slab() == 0, slab() == slabs() - 1
    def sweep(section, buf, to):
        rows = {r: [buf[c * tall + r] for c in range(3)] for r in range(section, tall - section)}
        climbs = {r: [x - y for x, y in zip(rows[r + 1], rows[r])] for r in range(section, tall - section - 1)}
        ends = []
        for r in range(section + 1, tall - section - 1):
            u = rows[r]
            west, east = [], []
            for x in u:
                y = pltpu.roll(x, 1, 1)
                west.append(x - jnp.where(lane == 0, pltpu.roll(y, 1, 0), y))
                y = pltpu.roll(x, 127, 1)
                east.append(jnp.where(lane == 127, pltpu.roll(y, 7, 0), y) - x)
            across = vv[r] + kappa * u[0]
            along = vv[tall + r] + kappa * u[1]
            s = slope(west, east, climbs[r - 1], climbs[r], across, along)
            new = [x + y for x, y in zip(u, s)]
            ends.append(new)
            for c in range(3):
                if r == FINE - 1:
                    new[c] = jnp.where(bottom, 0.0, new[c])
                elif r == FINE + ROWS:
                    new[c] = jnp.where(top, 0.0, new[c])
                if section < FINE - 1:
                    to[c * tall + r] = new[c]
        if section == FINE - 1:
            for y0 in (0, 8):
                for c in range(3):
                    for b, value in enumerate(swap8([ends[y0 + y][c] for y in range(8)])):
                        out[c, y0 : y0 + 8, 128 * b : 128 * b + 128] = value

    for section in range(FINE):
        buf, to = (wa, wb) if section % 2 == 0 else (wb, wa)
        sweep(section, buf, to)


def f32(*shape):
    return jax.ShapeDtypeStruct(shape, jnp.float32)


def buffer(*shape):
    return pltpu.VMEM(shape, jnp.float32)


def call(kernel, n_arrays, outs, scratch=(), space=VMEM, to=VMEM, mib=24):
    many = isinstance(outs, tuple)
    return pl.pallas_call(
        kernel,
        out_shape=outs,
        in_specs=[space] * n_arrays,
        out_specs=(to,) * len(outs) if many else to,
        scratch_shapes=list(scratch),
        compiler_params=pltpu.CompilerParams(vmem_limit_bytes=mib * 1024 * 1024),
    )


def cut(init, ends, vel):
    state, flow = buffer(3, ROWS, 1024), buffer(2, ROWS, 1024)
    scratch = [state, state, flow, buffer(5, 32, 8, 128), buffer(2 * ROWS, 8, 128)]
    scratch += [pltpu.SemaphoreType.DMA((8,)), pltpu.SemaphoreType.DMA((6,))]
    outs = (f32(32, 5, 8, 128), f32(2 * ROWS, 8, 128))
    return call(cut_kernel, 3, outs, scratch, HBM, HBM, 60)(init, ends, vel)


def sort(cur):
    return call(sort_kernel, 1, (f32(160, 8, 128), f32(130, 8, 128), f32(130, 8, 128)))(cur)


def early(cur):
    top, flat = f32(12, 9, 8, 128), f32(12, 8, 8, 128)
    return call(early_kernel, 1, (top, top, top, top, top, f32(10, 8, 8, 128), flat))(cur)


def cycle(other, mate, *upper):
    tall = BAND + 1
    scratch = [buffer(12, HALO + d, 8, 128) for d in range(5)]
    scratch += [
        buffer(10, HALO, 8, 128),
        buffer(12, HALO + 4, 8, 128),
        buffer(3, BAND, 8, 128),
        buffer(3, BAND, 8, 128),
        buffer(3, tall, 8, 128),
        buffer(3, tall, 8, 128),
        buffer(3, tall, 8, 128),
        buffer(3, tall, 8, 128),
        buffer(3, BAND, 8, 128),
        buffer(9, tall, 8, 128),
    ]
    return call(cycle_kernel, 9, f32(96, 8, 128), scratch)(other, mate, *upper)


def begins(tiles, flow):
    halo = f32(5 * FINE, 8, 128)
    return call(begin_kernel, 2, (f32(3 * ROWS, 8, 128), halo, halo))(tiles, flow)


def owns(tiles):
    return call(own_kernel, 1, f32(3, ROWS, 1024))(tiles)


def relax(mid, flow, mate, other):
    tall = ROWS + 2 * FINE
    scratch = [buffer(3 * tall, 8, 128), buffer(3 * tall, 8, 128), buffer(2 * tall, 8, 128)]
    return call(relax_kernel, 4, f32(3, ROWS, 1024), scratch)(mid, flow, mate, other)


def per_device(initial_state, guessed_ends, velocity):
    slabs = lax.axis_size("gy")
    mates = [(i, i ^ 1) for i in range(slabs)]
    others = [(i, i + 1 if i % 2 else i - 1) for i in range(1, slabs - 1)]
    intervals = lax.axis_size("tm")

    windows, flow = cut(initial_state, guessed_ends[0], velocity[0])
    cur = lax.all_to_all(windows.reshape(intervals, 40, 128), "tm", 0, 0)
    cur = cur.reshape(intervals * 5, 8, 128)
    cur, to_other, to_mate = sort(cur)
    other = lax.ppermute(to_other, "gy", others)
    mate = lax.ppermute(to_mate, "gy", mates)
    tiles = cycle(other, mate, *early(cur))
    tiles = lax.all_to_all(tiles.reshape(intervals, 24, 128), "tm", 0, 0)
    tiles = tiles.reshape(intervals * 3, 8, 128)
    mid, mate, other = begins(tiles, flow)
    mate = lax.ppermute(mate, "gy", mates)
    other = lax.ppermute(other, "gy", others)
    own = owns(tiles)
    relaxed = relax(mid, flow, mate, other)
    return own[None], relaxed[None]


def solution(mesh):
    placed = (P(None, "gy", None), P("tm", None, "gy", None), P("tm", None, "gy", None))
    return jax.shard_map(
        per_device,
        mesh=mesh,
        in_specs=placed,
        out_specs=(P("tm", None, "gy", None), P("tm", None, "gy", None)),
        check_vma=False,
    )
```

```python
import jax
import jax.numpy as jnp
from jax import lax
from jax.experimental import pallas as pl
from jax.experimental.pallas import tpu as pltpu
from jax.sharding import PartitionSpec as P

FINE = 4
GROUP = 4
GROUPS = 8
HALO = 16
TILE = 32
ROWS = 16
HALF = 64
BAND = 24

diffusion = (0.05, 0.15, 0.4)
kappa_coupling = 0.1
time_step = 0.0125
coarsest = FINE * GROUP * time_step

VMEM = pl.BlockSpec(memory_space=pltpu.VMEM)
HBM = pl.BlockSpec(memory_space=pltpu.HBM)


def slab():
    return lax.axis_index("gy")


def slabs():
    return lax.axis_size("gy")


def lanes():
    return lax.broadcasted_iota(jnp.int32, (8, 128), 1)


def sublanes():
    return lax.broadcasted_iota(jnp.int32, (8, 128), 0)


def swap8(values):
    sub = sublanes()
    for s in (4, 2, 1):
        keep = sub % (2 * s) < s
        new = list(values)
        for p in range(8):
            if p % (2 * s) < s:
                a, b = values[p], values[p + s]
                new[p] = jnp.where(keep, a, pltpu.roll(b, s, 0))
                new[p + s] = jnp.where(keep, pltpu.roll(a, 8 - s, 0), b)
        values = new
    return values


def slope(west, east, below, above, across, along, scale=1.0):
    right, upward = across > 0.0, along > 0.0
    out = []
    for c in range(3):
        spread = (east[c] - west[c]) + (above[c] - below[c])
        transport = across * jnp.where(right, west[c], east[c]) + along * jnp.where(upward, below[c], above[c])
        out.append((scale * time_step * diffusion[c]) * spread - transport)
    return out


def cut_kernel(init_hbm, ends_hbm, vel_hbm, out_hbm, flow_hbm, init, ends, vel, out, flow, arrive, leave):
    def fetch(far, near, i, at):
        copy = pltpu.make_async_copy(far.at[i], near.at[i], arrive.at[at])
        copy.start()
        return copy

    coming = {3 + c: [fetch(vel_hbm, vel, c, c)] for c in range(2)}
    for c in range(3):
        coming[c] = [fetch(ends_hbm, ends, c, 2 + c), fetch(init_hbm, init, c, 5 + c)]
    going = []
    last = lax.axis_index("tm") == GROUP * GROUPS - 1
    low = lanes() < HALF
    for a in (3, 4, 0, 1, 2):
        for copy in coming[a]:
            copy.wait()
        if a < 3:
            top = jnp.where(last, init[a, 0:8, :], ends[a, 0:8, :])
            bottom = jnp.where(last, init[a, 8:16, :], ends[a, 8:16, :])
        else:
            top, bottom = vel[a - 3, 0:8, :], vel[a - 3, 8:16, :]
        for q in range(4):
            upper = pltpu.roll(top, (HALO - TILE * q) % 1024, 1)
            lower = pltpu.roll(bottom, (HALO + HALF - TILE * q) % 1024, 1)
            for b in range(8):
                at = slice(128 * b, 128 * b + 128)
                out[a, 4 * b + q] = jnp.where(low, upper[:, at], lower[:, at])
        copy = pltpu.make_async_copy(out.at[a], out_hbm.at[:, a], leave.at[a])
        copy.start()
        going.append(copy)
        if a < 3:
            continue
        for y0 in (0, 8):
            blocks = [vel[a - 3, y0 : y0 + 8, 128 * b : 128 * b + 128] for b in range(8)]
            for y, value in enumerate(swap8(blocks)):
                flow[(a - 3) * ROWS + y0 + y] = value
        if a == 4:
            copy = pltpu.make_async_copy(flow, flow_hbm, leave.at[5])
            copy.start()
            going.append(copy)
    for copy in going:
        copy.wait()


def fold(own, out, parity):
    sub, near = sublanes(), lanes() // HALF == parity
    for m in range(10):
        tails = []
        for h in range(2):
            at = (2 * m + h) * 8
            x = [jnp.where(parity == 0, own[at + z], own[at + 7 - z]) for z in range(8)]
            for z in range(5):
                value = x[z]
                if 0 < z < 4:
                    both = jnp.where(sub <= 7 - z, value, pltpu.roll(x[8 - z], 8 - z, 0))
                    value = jnp.where(near, value, both)
                out[13 * m + 5 * h + z] = value
            tails.append(x[5:])
        for z in range(3):
            out[13 * m + 10 + z] = jnp.where(near, tails[0][z], pltpu.roll(tails[1][z], HALF, 1))


def unfold(folded, at):
    x = [folded[13 * (at // 2) + 5 * (at % 2) + z] for z in range(5)]
    tail = [folded[13 * (at // 2) + 10 + z] for z in range(3)]
    near = x + ([pltpu.roll(t, HALF, 1) for t in tail] if at % 2 else tail)
    far = x + [pltpu.roll(x[8 - z], 8 - z, 0) for z in range(5, 8)]
    return near, far


def sort_kernel(cur, own, to_other, to_mate):
    for k in range(GROUP):
        for a in range(5):
            values = swap8([cur[(4 * j + k) * 5 + a] for j in range(8)])
            to = k
            if a < 3:
                to = (k + 1) % GROUP
                if to == 0:
                    values = [pltpu.roll(value, 1, 0) for value in values]
            for y in range(8):
                own[(to * 5 + a) * 8 + y] = values[y]
    parity = slab() % 2
    fold(own, to_other, parity)
    fold(own, to_mate, 1 - parity)


class Rows:
    def __init__(self, lower, upper, edge):
        self.lower, self.upper, self.edge = lower, upper, edge

    def __getitem__(self, at):
        i, r = at
        return self.upper[i, r - HALO] if r >= self.edge else self.lower[i, r]

    def __setitem__(self, at, value):
        i, r = at
        if r >= self.edge:
            self.upper[i, r - HALO] = value
        else:
            self.lower[i, r] = value


def tools():
    low = lanes() < HALF
    sign = jnp.where(low, 1.0, -1.0)
    kappa = time_step * kappa_coupling
    swing = kappa * sign
    outside = jnp.where(low, slab(), slabs() - 1 - slab()) == 0

    def step(*arguments):
        pl.when(slab() * slab() >= slab())(lambda: sweep(*arguments))

    def sweep(buf, base, flow, at, start, stop, emit, scale=1.0):
        rows, climbs = {}, {}

        def row(r):
            if r not in rows:
                rows[r] = [buf[base + c, r] for c in range(3)]
            return rows[r]

        def climb(r):
            if r not in climbs:
                climbs[r] = [x - y for x, y in zip(row(r + 1), row(r))]
            return climbs[r]

        for r in range(start, stop):
            u = row(r)
            west = [x - pltpu.roll(x, 1, 1) for x in u]
            east = [pltpu.roll(x, 127, 1) - x for x in u]
            across = flow[at, r] + (scale * kappa) * u[0]
            along = flow[at + 1, r] + (scale * swing) * u[1]
            emit(r, u, slope(west, east, climb(r - 1), climb(r), across, along, scale))

    def put(buf, at, r, value):
        if r == HALO - 1:
            value = jnp.where(outside, 0.0, value)
        buf[at, r] = value
        if r == BAND - 1:
            buf[at, BAND] = pltpu.roll(value, HALF, 1)

    return low, sign, step, put


def keep_flow(vv, k, a, r, value, sign):
    way = 1.0 if a == 3 else sign
    vv[2 * k + a - 3, r] = (time_step * way) * value
    if k == GROUP - 1:
        vv[2 * GROUP + a - 3, r] = (coarsest * way) * value


def fine_steps(states, vv, src_in, src, step, put, spans):
    def member(k, carry):
        base = 3 * k

        def opening(r, u, s):
            for c in range(3):
                put(states[1], base + c, r, u[c] + s[c])
                src_in[base + c, r] = u[c] + float(FINE) * s[c]

        def onward(buf):
            def emit(r, u, s):
                for c in range(3):
                    put(buf, base + c, r, u[c] + s[c])

            return emit

        def closing(r, u, s):
            for c in range(3):
                end = u[c] + s[c]
                put(states[4], base + c, r, end)
                src[base + c, r] = end - src_in[base + c, r]

        emits = (opening, onward(states[2]), onward(states[3]), closing)
        for i, (emit, span) in enumerate(zip(emits, spans)):
            step(states[i], base, vv, 2 * k, *span, emit)
        return carry

    lax.fori_loop(0, GROUP, member, 0)


def early_kernel(cur, e0, e1, e2, e3, e4, vv, src):
    low, sign, step, put = tools()
    states = [Rows(None, x, 0) for x in (e0, e1, e2, e3, e4)]
    vv, src = Rows(None, vv, 0), Rows(None, src, 0)
    for k in range(GROUP):
        for a in range(5):
            mine = [cur[(k * 5 + a) * 8 + y] for y in range(8)]
            for y in range(8):
                value = jnp.where(low, mine[y], mine[7 - y])
                if a < 3:
                    put(states[0], 3 * k + a, HALO + y, value)
                else:
                    keep_flow(vv, k, a, HALO + y, value, sign)
    fine_steps(states, vv, src, src, step, put, [(HALO + d, BAND) for d in range(1, 5)])


def cycle_kernel(other, mate, e0, e1, e2, e3, e4, ev, es, out, u0, u1, u2, u3, u4, lv, ls, gg, ff, ca, cb, xa, xb, yy, cc):
    low, sign, step, put = tools()
    lane, sub = lanes(), sublanes()
    here = lane // HALF == slab() % 2
    states = [Rows(u, e, HALO + d) for d, (u, e) in enumerate(zip((u0, u1, u2, u3, u4), (e0, e1, e2, e3, e4)))]
    vv = Rows(lv, ev, HALO)
    begin, ends, src = states[0], states[4], Rows(ls, es, HALO + 4)

    for k in range(GROUP):
        for a in range(5):
            near, far = unfold(other, k * 5 + a)
            mate_near, mate_far = unfold(mate, k * 5 + a)
            for y in range(8):
                rows = (
                    (y, jnp.where(here, far[7 - y], mate_far[7 - y])),
                    (y + 8, pltpu.roll(jnp.where(here, mate_near[7 - y], near[7 - y]), HALF, 1)),
                )
                for r, value in rows:
                    if a < 3:
                        put(begin, 3 * k + a, r, value)
                    else:
                        keep_flow(vv, k, a, r, value, sign)

    fine_steps(states, vv, Rows(ls, es, HALO + 1), src, step, put, [(d, HALO + d) for d in range(1, 5)])

    def keep_g(r, u, s):
        for c in range(3):
            gg[c, r] = u[c] + s[c]

    step(begin, 0, vv, 2 * GROUP, 7, BAND, keep_g, float(FINE * GROUP))

    def plus(buf, k, base):
        def emit(r, u, s):
            for c in range(3):
                put(buf, base + c, r, u[c] + float(FINE) * s[c] + src[3 * k + c, r])

        return emit

    step(ends, 0, vv, 2, 5, BAND, plus(cb, 1, 0))
    step(cb, 0, vv, 4, 6, BAND, plus(ca, 2, 0))

    def forcing(r, u, s):
        for c in range(3):
            ff[c, r] = u[c] + float(FINE) * s[c] + src[3 * (GROUP - 1) + c, r] - gg[c, r]

    step(ca, 0, vv, 2 * (GROUP - 1), 7, BAND, forcing)

    for c in range(3):
        xb[c, 6] = begin[c, 6]
    for t in range(GROUPS):
        buf, to = (xa if t else begin, xb) if t % 2 == 0 else (xb, xa)

        def settle(r, u, s):
            for c in range(3):
                y = u[c] + s[c] + ff[c, r]
                if t == GROUPS - 1 and r >= HALO:
                    yy[c, r] = y
                put(to, c, r, jnp.where(sub == 0, begin[c, r], pltpu.roll(y, 1, 0)))

        step(buf, 0, vv, 2 * GROUP, max(7, 6 + t), BAND, settle, float(FINE * GROUP))

    step(xa, 0, vv, 0, 14, BAND, plus(cc, 0, 0))
    step(cc, 0, vv, 2, 15, BAND, plus(cc, 1, 3))
    step(cc, 3, vv, 4, 16, BAND, plus(cc, 2, 6))

    def compact(buf, base, c, y):
        m = jnp.where(low, buf[base + c, y + 16], buf[base + c, 23 - y])
        return jnp.where(lane < TILE, pltpu.roll(m, 128 - HALO, 1), pltpu.roll(m, 128 - HALO - TILE, 1))

    reads = [(xa, 0), (cc, 0), (cc, 3), (cc, 6), (yy, 0)]
    for c in range(3):
        before = [compact(*reads[0], c, y) for y in range(8)]
        for k in range(GROUP):
            own = [compact(*reads[k + 1], c, y) for y in range(8)]
            values = [jnp.where(low, x, pltpu.roll(y, HALF, 1)) for x, y in zip(own, before)]
            for j, value in enumerate(swap8(values)):
                out[(4 * j + k) * 3 + c] = value
            before = own


def gathered(tiles, c, b, part):
    group = lanes() // TILE
    value = None
    for q in range(4):
        shift = (TILE * (q - part)) % 128
        x = tiles[(4 * b + q) * 3 + c]
        x = pltpu.roll(x, shift, 1) if shift else x
        value = x if value is None else jnp.where(group == q, x, value)
    return value


def begin_kernel(tiles, flow, begin, mate, other):
    even = slab() % 2 == 0
    for c in range(5):
        if c < 3:
            rows = []
            for part in (2, 3):
                rows += swap8([gathered(tiles, c, b, part) for b in range(8)])
            for y in range(ROWS):
                begin[c * ROWS + y] = rows[y]
        else:
            rows = [flow[(c - 3) * ROWS + y] for y in range(ROWS)]
        for y in range(FINE):
            down, up = rows[y], rows[ROWS - FINE + y]
            mate[c * FINE + y] = jnp.where(even, up, down)
            other[c * FINE + y] = jnp.where(even, down, up)


def own_kernel(tiles, own):
    for c in range(3):
        for b in range(8):
            at = slice(128 * b, 128 * b + 128)
            own[c, 0:8, at] = gathered(tiles, c, b, 0)
            own[c, 8:16, at] = gathered(tiles, c, b, 1)


def relax_kernel(mid, flow, other, mate, out, wa, wb, vv):
    lane = lanes()
    tall = ROWS + 2 * FINE
    kappa = time_step * kappa_coupling
    even = slab() % 2 == 0
    for a in range(5):
        src, buf, at = (mid, wa, a) if a < 3 else (flow, vv, a - 3)
        scale = 1.0 if a < 3 else time_step
        for r in range(FINE):
            m, o = mate[a * FINE + r], other[a * FINE + r]
            buf[at * tall + r] = scale * jnp.where(even, o, m)
            buf[at * tall + FINE + ROWS + r] = scale * jnp.where(even, m, o)
        for r in range(ROWS):
            buf[at * tall + FINE + r] = scale * src[at * ROWS + r]

    bottom, top = slab() == 0, slab() == slabs() - 1
    def sweep(section, buf, to):
        rows = {r: [buf[c * tall + r] for c in range(3)] for r in range(section, tall - section)}
        climbs = {r: [x - y for x, y in zip(rows[r + 1], rows[r])] for r in range(section, tall - section - 1)}
        ends = []
        for r in range(section + 1, tall - section - 1):
            u = rows[r]
            west, east = [], []
            for x in u:
                y = pltpu.roll(x, 1, 1)
                west.append(x - jnp.where(lane == 0, pltpu.roll(y, 1, 0), y))
                y = pltpu.roll(x, 127, 1)
                east.append(jnp.where(lane == 127, pltpu.roll(y, 7, 0), y) - x)
            across = vv[r] + kappa * u[0]
            along = vv[tall + r] + kappa * u[1]
            s = slope(west, east, climbs[r - 1], climbs[r], across, along)
            new = [x + y for x, y in zip(u, s)]
            ends.append(new)
            for c in range(3):
                if r == FINE - 1:
                    new[c] = jnp.where(bottom, 0.0, new[c])
                elif r == FINE + ROWS:
                    new[c] = jnp.where(top, 0.0, new[c])
                if section < FINE - 1:
                    to[c * tall + r] = new[c]
        if section == FINE - 1:
            for y0 in (0, 8):
                for c in range(3):
                    for b, value in enumerate(swap8([ends[y0 + y][c] for y in range(8)])):
                        out[c, y0 : y0 + 8, 128 * b : 128 * b + 128] = value

    for section in range(FINE):
        buf, to = (wa, wb) if section % 2 == 0 else (wb, wa)
        sweep(section, buf, to)


def f32(*shape):
    return jax.ShapeDtypeStruct(shape, jnp.float32)


def buffer(*shape):
    return pltpu.VMEM(shape, jnp.float32)


def call(kernel, n_arrays, outs, scratch=(), space=VMEM, to=VMEM, mib=24):
    many = isinstance(outs, tuple)
    return pl.pallas_call(
        kernel,
        out_shape=outs,
        in_specs=[space] * n_arrays,
        out_specs=(to,) * len(outs) if many else to,
        scratch_shapes=list(scratch),
        compiler_params=pltpu.CompilerParams(vmem_limit_bytes=mib * 1024 * 1024),
    )


def cut(init, ends, vel):
    state, flow = buffer(3, ROWS, 1024), buffer(2, ROWS, 1024)
    scratch = [state, state, flow, buffer(5, 32, 8, 128), buffer(2 * ROWS, 8, 128)]
    scratch += [pltpu.SemaphoreType.DMA((8,)), pltpu.SemaphoreType.DMA((6,))]
    outs = (f32(32, 5, 8, 128), f32(2 * ROWS, 8, 128))
    return call(cut_kernel, 3, outs, scratch, HBM, HBM, 60)(init, ends, vel)


def sort(cur):
    return call(sort_kernel, 1, (f32(160, 8, 128), f32(130, 8, 128), f32(130, 8, 128)))(cur)


def early(cur):
    top, flat = f32(12, 9, 8, 128), f32(12, 8, 8, 128)
    return call(early_kernel, 1, (top, top, top, top, top, f32(10, 8, 8, 128), flat))(cur)


def cycle(other, mate, *upper):
    tall = BAND + 1
    scratch = [buffer(12, HALO + d, 8, 128) for d in range(5)]
    scratch += [
        buffer(10, HALO, 8, 128),
        buffer(12, HALO + 4, 8, 128),
        buffer(3, BAND, 8, 128),
        buffer(3, BAND, 8, 128),
        buffer(3, tall, 8, 128),
        buffer(3, tall, 8, 128),
        buffer(3, tall, 8, 128),
        buffer(3, tall, 8, 128),
        buffer(3, BAND, 8, 128),
        buffer(9, tall, 8, 128),
    ]
    return call(cycle_kernel, 9, f32(96, 8, 128), scratch)(other, mate, *upper)


def begins(tiles, flow):
    halo = f32(5 * FINE, 8, 128)
    return call(begin_kernel, 2, (f32(3 * ROWS, 8, 128), halo, halo))(tiles, flow)


def owns(tiles):
    return call(own_kernel, 1, f32(3, ROWS, 1024))(tiles)


def relax(mid, flow, other, mate):
    tall = ROWS + 2 * FINE
    scratch = [buffer(3 * tall, 8, 128), buffer(3 * tall, 8, 128), buffer(2 * tall, 8, 128)]
    return call(relax_kernel, 4, f32(3, ROWS, 1024), scratch)(mid, flow, other, mate)


def per_device(initial_state, guessed_ends, velocity):
    slabs = lax.axis_size("gy")
    mates = [(i, i ^ 1) for i in range(slabs)]
    others = [(i, i + 1 if i % 2 else i - 1) for i in range(1, slabs - 1)]
    intervals = lax.axis_size("tm")

    windows, flow = cut(initial_state, guessed_ends[0], velocity[0])
    cur = lax.all_to_all(windows.reshape(intervals, 40, 128), "tm", 0, 0)
    cur = cur.reshape(intervals * 5, 8, 128)
    cur, to_other, to_mate = sort(cur)
    other = lax.ppermute(to_other, "gy", others)
    mate = lax.ppermute(to_mate, "gy", mates)
    tiles = cycle(other, mate, *early(cur))
    tiles = lax.all_to_all(tiles.reshape(intervals, 24, 128), "tm", 0, 0)
    tiles = tiles.reshape(intervals * 3, 8, 128)
    mid, mate, other = begins(tiles, flow)
    mate = lax.ppermute(mate, "gy", mates)
    other = lax.ppermute(other, "gy", others)
    own = owns(tiles)
    relaxed = relax(mid, flow, other, mate)
    return own[None], relaxed[None]


def solution(mesh):
    placed = (P(None, "gy", None), P("tm", None, "gy", None), P("tm", None, "gy", None))
    return jax.shard_map(
        per_device,
        mesh=mesh,
        in_specs=placed,
        out_specs=(P("tm", None, "gy", None), P("tm", None, "gy", None)),
        check_vma=False,
    )
```

```python
import jax
import jax.numpy as jnp
from jax import lax
from jax.experimental import pallas as pl
from jax.experimental.pallas import tpu as pltpu
from jax.sharding import PartitionSpec as P

FINE = 4
GROUP = 4
GROUPS = 8
HALO = 16
TILE = 32
ROWS = 16
HALF = 64
BAND = 24

diffusion = (0.05, 0.15, 0.4)
kappa_coupling = 0.1
time_step = 0.0125
coarsest = FINE * GROUP * time_step

VMEM = pl.BlockSpec(memory_space=pltpu.VMEM)
HBM = pl.BlockSpec(memory_space=pltpu.HBM)


def slab():
    return lax.axis_index("gy")


def slabs():
    return lax.axis_size("gy")


def lanes():
    return lax.broadcasted_iota(jnp.int32, (8, 128), 1)


def sublanes():
    return lax.broadcasted_iota(jnp.int32, (8, 128), 0)


def swap8(values):
    sub = sublanes()
    for s in (4, 2, 1):
        keep = sub % (2 * s) < s
        new = list(values)
        for p in range(8):
            if p % (2 * s) < s:
                a, b = values[p], values[p + s]
                new[p] = jnp.where(keep, a, pltpu.roll(b, s, 0))
                new[p + s] = jnp.where(keep, pltpu.roll(a, 8 - s, 0), b)
        values = new
    return values


def slope(west, east, below, above, across, along, scale=1.0):
    right, upward = across > 0.0, along > 0.0
    out = []
    for c in range(3):
        spread = (east[c] - west[c]) + (above[c] - below[c])
        transport = across * jnp.where(right, west[c], east[c]) + along * jnp.where(upward, below[c], above[c])
        out.append((scale * time_step * diffusion[c]) * spread - transport)
    return out


def cut_kernel(init_hbm, ends_hbm, vel_hbm, out_hbm, flow_hbm, init, ends, vel, out, flow, arrive, leave):
    def fetch(far, near, i, at):
        copy = pltpu.make_async_copy(far.at[i], near.at[i], arrive.at[at])
        copy.start()
        return copy

    coming = {3 + c: [fetch(vel_hbm, vel, c, c)] for c in range(2)}
    for c in range(3):
        coming[c] = [fetch(ends_hbm, ends, c, 2 + c), fetch(init_hbm, init, c, 5 + c)]
    going = []
    last = lax.axis_index("tm") == GROUP * GROUPS - 1
    low = lanes() < HALF
    for a in (3, 4, 0, 1, 2):
        for copy in coming[a]:
            copy.wait()
        if a < 3:
            top = jnp.where(last, init[a, 0:8, :], ends[a, 0:8, :])
            bottom = jnp.where(last, init[a, 8:16, :], ends[a, 8:16, :])
        else:
            top, bottom = vel[a - 3, 0:8, :], vel[a - 3, 8:16, :]
        for q in range(4):
            upper = pltpu.roll(top, (HALO - TILE * q) % 1024, 1)
            lower = pltpu.roll(bottom, (HALO + HALF - TILE * q) % 1024, 1)
            for b in range(8):
                at = slice(128 * b, 128 * b + 128)
                out[a, 4 * b + q] = jnp.where(low, upper[:, at], lower[:, at])
        copy = pltpu.make_async_copy(out.at[a], out_hbm.at[:, a], leave.at[a])
        copy.start()
        going.append(copy)
        if a < 3:
            continue
        for y0 in (0, 8):
            blocks = [vel[a - 3, y0 : y0 + 8, 128 * b : 128 * b + 128] for b in range(8)]
            for y, value in enumerate(swap8(blocks)):
                flow[(a - 3) * ROWS + y0 + y] = value
        if a == 4:
            copy = pltpu.make_async_copy(flow, flow_hbm, leave.at[5])
            copy.start()
            going.append(copy)
    for copy in going:
        copy.wait()


def fold(own, out, parity):
    sub, near = sublanes(), lanes() // HALF == parity
    for m in range(10):
        tails = []
        for h in range(2):
            at = (2 * m + h) * 8
            x = [jnp.where(parity == 0, own[at + z], own[at + 7 - z]) for z in range(8)]
            for z in range(5):
                value = x[z]
                if 0 < z < 4:
                    both = jnp.where(sub <= 7 - z, value, pltpu.roll(x[8 - z], 8 - z, 0))
                    value = jnp.where(near, value, both)
                out[13 * m + 5 * h + z] = value
            tails.append(x[5:])
        for z in range(3):
            out[13 * m + 10 + z] = jnp.where(near, tails[0][z], pltpu.roll(tails[1][z], HALF, 1))


def unfold(folded, at):
    x = [folded[13 * (at // 2) + 5 * (at % 2) + z] for z in range(5)]
    tail = [folded[13 * (at // 2) + 10 + z] for z in range(3)]
    near = x + ([pltpu.roll(t, HALF, 1) for t in tail] if at % 2 else tail)
    far = x + [pltpu.roll(x[8 - z], 8 - z, 0) for z in range(5, 8)]
    return near, far


def sort_kernel(cur, own, to_other, to_mate):
    for k in range(GROUP):
        for a in range(5):
            values = swap8([cur[(4 * j + k) * 5 + a] for j in range(8)])
            to = k
            if a < 3:
                to = (k + 1) % GROUP
                if to == 0:
                    values = [pltpu.roll(value, 1, 0) for value in values]
            for y in range(8):
                own[(to * 5 + a) * 8 + y] = values[y]
    parity = slab() % 2
    fold(own, to_other, parity)
    fold(own, to_mate, 1 - parity)


class Rows:
    def __init__(self, lower, upper, edge):
        self.lower, self.upper, self.edge = lower, upper, edge

    def __getitem__(self, at):
        i, r = at
        return self.upper[i, r - HALO] if r >= self.edge else self.lower[i, r]

    def __setitem__(self, at, value):
        i, r = at
        if r >= self.edge:
            self.upper[i, r - HALO] = value
        else:
            self.lower[i, r] = value


def tools():
    low = lanes() < HALF
    sign = jnp.where(low, 1.0, -1.0)
    kappa = time_step * kappa_coupling
    swing = kappa * sign
    outside = jnp.where(low, slab(), slabs() - 1 - slab()) == 0

    def step(*arguments):
        pl.when(slab() * slab() >= slab())(lambda: sweep(*arguments))

    def sweep(buf, base, flow, at, start, stop, emit, scale=1.0):
        rows, climbs = {}, {}

        def row(r):
            if r not in rows:
                rows[r] = [buf[base + c, r] for c in range(3)]
            return rows[r]

        def climb(r):
            if r not in climbs:
                climbs[r] = [x - y for x, y in zip(row(r + 1), row(r))]
            return climbs[r]

        for r in range(start, stop):
            u = row(r)
            west = [x - pltpu.roll(x, 1, 1) for x in u]
            east = [pltpu.roll(x, 127, 1) - x for x in u]
            across = flow[at, r] + (scale * kappa) * u[0]
            along = flow[at + 1, r] + (scale * swing) * u[1]
            emit(r, u, slope(west, east, climb(r - 1), climb(r), across, along, scale))

    def put(buf, at, r, value):
        if r == HALO - 1:
            value = jnp.where(outside, 0.0, value)
        buf[at, r] = value
        if r == BAND - 1:
            buf[at, BAND] = pltpu.roll(value, HALF, 1)

    return low, sign, step, put


def keep_flow(vv, k, a, r, value, sign):
    way = 1.0 if a == 3 else sign
    vv[2 * k + a - 3, r] = (time_step * way) * value
    if k == GROUP - 1:
        vv[2 * GROUP + a - 3, r] = (coarsest * way) * value


def fine_steps(states, vv, src_in, src, step, put, spans):
    def member(k, carry):
        base = 3 * k

        def opening(r, u, s):
            for c in range(3):
                put(states[1], base + c, r, u[c] + s[c])
                src_in[base + c, r] = u[c] + float(FINE) * s[c]

        def onward(buf):
            def emit(r, u, s):
                for c in range(3):
                    put(buf, base + c, r, u[c] + s[c])

            return emit

        def closing(r, u, s):
            for c in range(3):
                end = u[c] + s[c]
                put(states[4], base + c, r, end)
                src[base + c, r] = end - src_in[base + c, r]

        emits = (opening, onward(states[2]), onward(states[3]), closing)
        for i, (emit, span) in enumerate(zip(emits, spans)):
            step(states[i], base, vv, 2 * k, *span, emit)
        return carry

    lax.fori_loop(0, GROUP, member, 0)


def early_kernel(cur, e0, e1, e2, e3, e4, vv, src):
    low, sign, step, put = tools()
    states = [Rows(None, x, 0) for x in (e0, e1, e2, e3, e4)]
    vv, src = Rows(None, vv, 0), Rows(None, src, 0)
    for k in range(GROUP):
        for a in range(5):
            mine = [cur[(k * 5 + a) * 8 + y] for y in range(8)]
            for y in range(8):
                value = jnp.where(low, mine[y], mine[7 - y])
                if a < 3:
                    put(states[0], 3 * k + a, HALO + y, value)
                else:
                    keep_flow(vv, k, a, HALO + y, value, sign)
    fine_steps(states, vv, src, src, step, put, [(HALO + d, BAND) for d in range(1, 5)])


def cycle_kernel(other, mate, e0, e1, e2, e3, e4, ev, es, out, u0, u1, u2, u3, u4, lv, ls, gg, ff, ca, cb, xa, xb, yy, cc):
    low, sign, step, put = tools()
    lane, sub = lanes(), sublanes()
    here = lane // HALF == slab() % 2
    states = [Rows(u, e, HALO + d) for d, (u, e) in enumerate(zip((u0, u1, u2, u3, u4), (e0, e1, e2, e3, e4)))]
    vv = Rows(lv, ev, HALO)
    begin, ends, src = states[0], states[4], Rows(ls, es, HALO + 4)

    for k in range(GROUP):
        for a in range(5):
            near, far = unfold(other, k * 5 + a)
            mate_near, mate_far = unfold(mate, k * 5 + a)
            for y in range(8):
                rows = (
                    (y, jnp.where(here, far[7 - y], mate_far[7 - y])),
                    (y + 8, pltpu.roll(jnp.where(here, mate_near[7 - y], near[7 - y]), HALF, 1)),
                )
                for r, value in rows:
                    if a < 3:
                        put(begin, 3 * k + a, r, value)
                    else:
                        keep_flow(vv, k, a, r, value, sign)

    fine_steps(states, vv, Rows(ls, es, HALO + 1), src, step, put, [(d, HALO + d) for d in range(1, 5)])

    def keep_g(r, u, s):
        for c in range(3):
            gg[c, r] = u[c] + s[c]

    step(begin, 0, vv, 2 * GROUP, 7, BAND, keep_g, float(FINE * GROUP))

    def plus(buf, k, base):
        def emit(r, u, s):
            for c in range(3):
                put(buf, base + c, r, u[c] + float(FINE) * s[c] + src[3 * k + c, r])

        return emit

    step(ends, 0, vv, 2, 5, BAND, plus(cb, 1, 0))
    step(cb, 0, vv, 4, 6, BAND, plus(ca, 2, 0))

    def forcing(r, u, s):
        for c in range(3):
            ff[c, r] = u[c] + float(FINE) * s[c] + src[3 * (GROUP - 1) + c, r] - gg[c, r]

    step(ca, 0, vv, 2 * (GROUP - 1), 7, BAND, forcing)

    for c in range(3):
        xb[c, 6] = begin[c, 6]
    for t in range(GROUPS):
        buf, to = (xa if t else begin, xb) if t % 2 == 0 else (xb, xa)

        def settle(r, u, s):
            for c in range(3):
                y = u[c] + s[c] + ff[c, r]
                if t == GROUPS - 1 and r >= HALO:
                    yy[c, r] = y
                put(to, c, r, jnp.where(sub == 0, begin[c, r], pltpu.roll(y, 1, 0)))

        step(buf, 0, vv, 2 * GROUP, max(7, 6 + t), BAND, settle, float(FINE * GROUP))

    step(xa, 0, vv, 0, 14, BAND, plus(cc, 0, 0))
    step(cc, 0, vv, 2, 15, BAND, plus(cc, 1, 3))
    step(cc, 3, vv, 4, 16, BAND, plus(cc, 2, 6))

    def compact(buf, base, c, y):
        m = jnp.where(low, buf[base + c, y + 16], buf[base + c, 23 - y])
        return jnp.where(lane < TILE, pltpu.roll(m, 128 - HALO, 1), pltpu.roll(m, 128 - HALO - TILE, 1))

    reads = [(xa, 0), (cc, 0), (cc, 3), (cc, 6), (yy, 0)]
    for c in range(3):
        before = [compact(*reads[0], c, y) for y in range(8)]
        for k in range(GROUP):
            own = [compact(*reads[k + 1], c, y) for y in range(8)]
            values = [jnp.where(low, x, pltpu.roll(y, HALF, 1)) for x, y in zip(own, before)]
            for j, value in enumerate(swap8(values)):
                out[(4 * j + k) * 3 + c] = value
            before = own


def gathered(tiles, c, b, part):
    group = lanes() // TILE
    value = None
    for q in range(4):
        shift = (TILE * (q - part)) % 128
        x = tiles[(4 * b + q) * 3 + c]
        x = pltpu.roll(x, shift, 1) if shift else x
        value = x if value is None else jnp.where(group == q, x, value)
    return value


def begin_kernel(tiles, flow, begin, mate, other):
    even = slab() % 2 == 0
    for c in range(5):
        if c < 3:
            rows = []
            for part in (2, 3):
                rows += swap8([gathered(tiles, c, b, part) for b in range(8)])
            for y in range(ROWS):
                begin[c * ROWS + y] = rows[y]
        else:
            rows = [flow[(c - 3) * ROWS + y] for y in range(ROWS)]
        for y in range(FINE):
            down, up = rows[y], rows[ROWS - FINE + y]
            mate[c * FINE + y] = jnp.where(even, up, down)
            other[c * FINE + y] = jnp.where(even, down, up)


def own_kernel(tiles, own):
    for c in range(3):
        for b in range(8):
            at = slice(128 * b, 128 * b + 128)
            own[c, 0:8, at] = gathered(tiles, c, b, 0)
            own[c, 8:16, at] = gathered(tiles, c, b, 1)


def relax_kernel(mid, flow, other, mate, out, wa, wb, vv, near, leave):
    lane = lanes()
    tall = ROWS + 2 * FINE
    kappa = time_step * kappa_coupling
    even = slab() % 2 == 0
    for a in range(5):
        src, buf, at = (mid, wa, a) if a < 3 else (flow, vv, a - 3)
        scale = 1.0 if a < 3 else time_step
        for r in range(FINE):
            m, o = mate[a * FINE + r], other[a * FINE + r]
            buf[at * tall + r] = scale * jnp.where(even, o, m)
            buf[at * tall + FINE + ROWS + r] = scale * jnp.where(even, m, o)
        for r in range(ROWS):
            buf[at * tall + FINE + r] = scale * src[at * ROWS + r]

    bottom, top = slab() == 0, slab() == slabs() - 1
    def sweep(section, buf, to):
        rows = {r: [buf[c * tall + r] for c in range(3)] for r in range(section, tall - section)}
        climbs = {r: [x - y for x, y in zip(rows[r + 1], rows[r])] for r in range(section, tall - section - 1)}
        ends = []
        for r in range(section + 1, tall - section - 1):
            u = rows[r]
            west, east = [], []
            for x in u:
                y = pltpu.roll(x, 1, 1)
                west.append(x - jnp.where(lane == 0, pltpu.roll(y, 1, 0), y))
                y = pltpu.roll(x, 127, 1)
                east.append(jnp.where(lane == 127, pltpu.roll(y, 7, 0), y) - x)
            across = vv[r] + kappa * u[0]
            along = vv[tall + r] + kappa * u[1]
            s = slope(west, east, climbs[r - 1], climbs[r], across, along)
            new = [x + y for x, y in zip(u, s)]
            ends.append(new)
            for c in range(3):
                if r == FINE - 1:
                    new[c] = jnp.where(bottom, 0.0, new[c])
                elif r == FINE + ROWS:
                    new[c] = jnp.where(top, 0.0, new[c])
                if section < FINE - 1:
                    to[c * tall + r] = new[c]
        if section == FINE - 1:
            going = []
            for y0 in (0, 8):
                at = pl.ds(y0, 8)
                for c in range(3):
                    for b, value in enumerate(swap8([ends[y0 + y][c] for y in range(8)])):
                        near[c, at, 128 * b : 128 * b + 128] = value
                going.append(pltpu.make_async_copy(near.at[:, at], out.at[:, at], leave.at[y0 // 8]))
                going[-1].start()
            for copy in going:
                copy.wait()

    for section in range(FINE):
        buf, to = (wa, wb) if section % 2 == 0 else (wb, wa)
        sweep(section, buf, to)


def f32(*shape):
    return jax.ShapeDtypeStruct(shape, jnp.float32)


def buffer(*shape):
    return pltpu.VMEM(shape, jnp.float32)


def call(kernel, n_arrays, outs, scratch=(), space=VMEM, to=VMEM, mib=24):
    many = isinstance(outs, tuple)
    return pl.pallas_call(
        kernel,
        out_shape=outs,
        in_specs=[space] * n_arrays,
        out_specs=(to,) * len(outs) if many else to,
        scratch_shapes=list(scratch),
        compiler_params=pltpu.CompilerParams(vmem_limit_bytes=mib * 1024 * 1024),
    )


def cut(init, ends, vel):
    state, flow = buffer(3, ROWS, 1024), buffer(2, ROWS, 1024)
    scratch = [state, state, flow, buffer(5, 32, 8, 128), buffer(2 * ROWS, 8, 128)]
    scratch += [pltpu.SemaphoreType.DMA((8,)), pltpu.SemaphoreType.DMA((6,))]
    outs = (f32(32, 5, 8, 128), f32(2 * ROWS, 8, 128))
    return call(cut_kernel, 3, outs, scratch, HBM, HBM, 60)(init, ends, vel)


def sort(cur):
    return call(sort_kernel, 1, (f32(160, 8, 128), f32(130, 8, 128), f32(130, 8, 128)))(cur)


def early(cur):
    top, flat = f32(12, 9, 8, 128), f32(12, 8, 8, 128)
    return call(early_kernel, 1, (top, top, top, top, top, f32(10, 8, 8, 128), flat))(cur)


def cycle(other, mate, *upper):
    tall = BAND + 1
    scratch = [buffer(12, HALO + d, 8, 128) for d in range(5)]
    scratch += [
        buffer(10, HALO, 8, 128),
        buffer(12, HALO + 4, 8, 128),
        buffer(3, BAND, 8, 128),
        buffer(3, BAND, 8, 128),
        buffer(3, tall, 8, 128),
        buffer(3, tall, 8, 128),
        buffer(3, tall, 8, 128),
        buffer(3, tall, 8, 128),
        buffer(3, BAND, 8, 128),
        buffer(9, tall, 8, 128),
    ]
    return call(cycle_kernel, 9, f32(96, 8, 128), scratch)(other, mate, *upper)


def begins(tiles, flow):
    halo = f32(5 * FINE, 8, 128)
    return call(begin_kernel, 2, (f32(3 * ROWS, 8, 128), halo, halo))(tiles, flow)


def owns(tiles):
    return call(own_kernel, 1, f32(3, ROWS, 1024))(tiles)


def relax(mid, flow, other, mate):
    tall = ROWS + 2 * FINE
    scratch = [buffer(3 * tall, 8, 128), buffer(3 * tall, 8, 128), buffer(2 * tall, 8, 128)]
    scratch += [buffer(3, ROWS, 1024), pltpu.SemaphoreType.DMA((2,))]
    return call(relax_kernel, 4, f32(3, ROWS, 1024), scratch, to=HBM)(mid, flow, other, mate)


def per_device(initial_state, guessed_ends, velocity):
    slabs = lax.axis_size("gy")
    mates = [(i, i ^ 1) for i in range(slabs)]
    others = [(i, i + 1 if i % 2 else i - 1) for i in range(1, slabs - 1)]
    intervals = lax.axis_size("tm")

    windows, flow = cut(initial_state, guessed_ends[0], velocity[0])
    cur = lax.all_to_all(windows.reshape(intervals, 40, 128), "tm", 0, 0)
    cur = cur.reshape(intervals * 5, 8, 128)
    cur, to_other, to_mate = sort(cur)
    other = lax.ppermute(to_other, "gy", others)
    mate = lax.ppermute(to_mate, "gy", mates)
    tiles = cycle(other, mate, *early(cur))
    tiles = lax.all_to_all(tiles.reshape(intervals, 24, 128), "tm", 0, 0)
    tiles = tiles.reshape(intervals * 3, 8, 128)
    mid, mate, other = begins(tiles, flow)
    mate = lax.ppermute(mate, "gy", mates)
    other = lax.ppermute(other, "gy", others)
    own = owns(tiles)
    relaxed = relax(mid, flow, other, mate)
    return own[None], relaxed[None]


def solution(mesh):
    placed = (P(None, "gy", None), P("tm", None, "gy", None), P("tm", None, "gy", None))
    return jax.shard_map(
        per_device,
        mesh=mesh,
        in_specs=placed,
        out_specs=(P("tm", None, "gy", None), P("tm", None, "gy", None)),
        check_vma=False,
    )
```
